128 devices in a mesh: dp: 32 (over z, y, core), bank: 4 (over x).
Axes of the slice: x: 4, y: 4, z: 4, core: 2. Of those that a mesh axis runs over, the one named last changes fastest.
Arguments:
- chars: int32 [4096, 50], P('dp'), may hold values from 0 to 261
- counts: int32 [32], P('dp'), may hold values from 1 to 128, as said below
- char_table: float32 [262, 16], replicated, may hold values from -6 to 6
- conv_weight: float32 [112, 2048], P(None, 'bank'), may hold values from -0.875 to 0.875
- conv_bias: float32 [2048], P('bank'), may hold values from -3 to 3
- transform_weight: float32 [2, 2048, 2048], P(None, None, 'bank'), may hold values from -0.125 to 0.125
- transform_bias: float32 [2, 2048], P(None, 'bank'), may hold values from -3 to 3
- gate_weight: float32 [2, 2048, 2048], P(None, None, 'bank'), may hold values from -0.125 to 0.125
- gate_bias: float32 [2, 2048], P(None, 'bank'), may hold values from -3 to 3
- proj_weight: float32 [2048, 512], P(None, 'bank'), may hold values from -0.125 to 0.125
- proj_bias: float32 [512], P('bank'), may hold values from -3 to 3
- cotangent: float32 [4096, 512], P('dp', 'bank'), may hold values from -6 to 6
Outputs:
- encoded: float32 [4096, 512], P('dp', 'bank')
- grad_char_table: float32 [262, 16], replicated
- grad_conv_weight: float32 [112, 2048], P(None, 'bank')
- grad_conv_bias: float32 [2048], P('bank')
- grad_transform_weight: float32 [2, 2048, 2048], P(None, None, 'bank')
- grad_transform_bias: float32 [2, 2048], P(None, 'bank')
- grad_gate_weight: float32 [2, 2048, 2048], P(None, None, 'bank')
- grad_gate_bias: float32 [2, 2048], P(None, 'bank')
- grad_proj_weight: float32 [2048, 512], P(None, 'bank')
- grad_proj_bias: float32 [512], P('bank')
The draws below stay inside these ranges and needn't reach their ends.
Inputs may be any that keep to these rules, and one draw needn't show every extreme that they name: `counts`: the live tokens of a block of 128 slots are its first ones; the rest are padding.
All inputs are finite; a program needn't handle non-finite values.
Results may differ from the reference program's by a relative error of at most 0.0003.
Values sent between devices are 32-bit elements; how exact they have to be, the bound alone decides.
No kernel may reach another device: no remote copies, remote signals or barrier semaphores. Data moves between devices by JAX's collectives and lax.ppermute only.
A program may use at most 256 MiB of HBM per device.

```python
import jax
import jax.numpy as jnp
from jax import lax

VOCAB = 262
EMB = 16
FILTERS = 2048
PROJ = 512
CHARS = 50
KTAPS = 7
LAYERS = 2
GROUP = 128
KW = 112
TOKENS = 4096
GROUPS = 32


def draw_counts(key, part):
    key = jax.random.fold_in(key, 11)
    rising = GROUP * 5 // 8
    index = jnp.arange(GROUPS, dtype=jnp.int32)
    base = 1 + index * rising // max(GROUPS - 1, 1)
    spread = jax.random.randint(key, (GROUPS,), 0, GROUP - rising, dtype=jnp.int32)
    values = base + spread
    values = values.at[0].set(1)
    values = values.at[GROUPS - 1].set(GROUP)
    return values.astype(jnp.int32)


def set_ends(entries, own_key, smallest, largest):
    longest = entries.shape.index(max(entries.shape))
    spots = []
    for shift in (0, 1):
        where = [jax.random.randint(jax.random.fold_in(own_key, axis), (), 0, length) for axis, length in enumerate(entries.shape)]
        where[longest] = (where[longest] + shift) % entries.shape[longest]
        spots.append(tuple(where))
    return entries.at[spots[0]].set(smallest).at[spots[1]].set(largest)


def level_of(key, dims, shards, least, top_value):
    def one(dim, parts):
        draws = jax.random.uniform(jax.random.fold_in(jax.random.fold_in(key, 6), dim), (parts,), jnp.float32, least / len(shards), top_value / len(shards))
        return jnp.repeat(jnp.exp(draws), dims[dim] // parts).reshape((-1,) + (1,) * (len(dims) - dim - 1))

    gain = one(*shards[0])
    for cut in shards[1:]:
        gain = gain * one(*cut)
    return gain


def centred(own_key, dims, deviation, bound, pieces=(), held_as=jnp.bfloat16):
    result = deviation * jax.random.normal(own_key, dims, jnp.float32)
    if pieces:
        result = result * level_of(own_key, dims, pieces, -0.22, 0.18)
    return jnp.clip(result, -bound, bound).astype(held_as)


def setup_inputs(seed: int = 0) -> dict:
    splits = jax.random.split(jax.random.key(seed), 13)
    return {
        "chars": set_ends(jax.random.randint(splits[0], (TOKENS, CHARS), 0, VOCAB), jax.random.fold_in(splits[0], 1), 0, VOCAB - 1).astype(jnp.int32),
        "counts": draw_counts(jax.random.fold_in(splits[12], 71), 0),
        "char_table": centred(splits[2], (VOCAB, EMB), 1.0, 6.0, (), jnp.float32),
        "conv_weight": centred(splits[3], (KW, FILTERS), (3 * EMB) ** -0.5, 0.875, ((1, 4),), jnp.float32),
        "conv_bias": centred(splits[4], (FILTERS,), 0.5, 3.0, ((0, 4),), jnp.float32),
        "transform_weight": centred(splits[5], (LAYERS, FILTERS, FILTERS), FILTERS ** -0.5, 0.125, ((2, 4),), jnp.float32),
        "transform_bias": centred(splits[6], (LAYERS, FILTERS), 0.5, 3.0, ((1, 4),), jnp.float32),
        "gate_weight": centred(splits[7], (LAYERS, FILTERS, FILTERS), FILTERS ** -0.5, 0.125, ((2, 4),), jnp.float32),
        "gate_bias": centred(splits[8], (LAYERS, FILTERS), 0.5, 3.0, ((1, 4),), jnp.float32),
        "proj_weight": centred(splits[9], (FILTERS, PROJ), FILTERS ** -0.5, 0.125, ((1, 4),), jnp.float32),
        "proj_bias": centred(splits[10], (PROJ,), 0.5, 3.0, ((0, 4),), jnp.float32),
        "cotangent": centred(splits[11], (TOKENS, PROJ), 1.0, 6.0, ((0, 32), (1, 4)), jnp.float32),
    }


HIGHEST_PRECISION = lax.Precision.HIGHEST

@jax.custom_vjp
def low(v):
    return lax.optimization_barrier(v.astype(jnp.bfloat16)).astype(jnp.float32)

@jax.custom_vjp
def low_back(v):
    return v

def low_keep(v):
    return (low(v), None)

def low_pass(kept, grad):
    return (grad,)

def back_keep(v):
    return (v, None)

def back_low(kept, grad):
    return (low(grad),)
low.defvjp(low_keep, low_pass)
low_back.defvjp(back_keep, back_low)

def filter_widths(columns, filters):
    unit = filters // 64
    widths = jnp.ones_like(columns)
    for power in range(6):
        widths = widths + (columns >= unit * 2 ** power).astype(jnp.int32)
    return widths

def forward(weights, block_chars, live_mask):
    char_table, conv_weight, conv_bias, transform_weight, transform_bias, gate_weight, gate_bias, proj_weight, proj_bias = weights
    widths = filter_widths(jnp.arange(FILTERS, dtype=jnp.int32), FILTERS)
    tap_index = jnp.arange(KW, dtype=jnp.int32) // EMB
    tap_mask = (tap_index[:, None] < widths[None, :]).astype(jnp.float32)
    position = jnp.arange(CHARS, dtype=jnp.int32)
    position_mask = (position[:, None] <= CHARS - widths[None, :]).astype(jnp.float32)
    valid_count = (CHARS + 1 - widths).astype(jnp.float32)
    onehot = (block_chars[:, :, None] == jnp.arange(VOCAB, dtype=jnp.int32)).astype(jnp.float32)
    embedded = jnp.einsum('tcv,ve->tce', onehot, char_table, precision=HIGHEST_PRECISION)
    padded = jnp.pad(embedded, ((0, 0), (0, KTAPS - 1), (0, 0)))
    windows = jnp.concatenate([padded[:, tap:tap + CHARS] for tap in range(KTAPS)], axis=2)
    pre_conv = jnp.einsum('tck,kf->tcf', windows, conv_weight * tap_mask, precision=HIGHEST_PRECISION) + conv_bias
    lifted = jnp.exp(jax.nn.softplus(pre_conv)) * position_mask
    hidden = jnp.log(lax.optimization_barrier(jnp.sum(lifted, axis=1)) / valid_count)
    for layer in range(LAYERS):
        pre_t = jnp.dot(hidden, transform_weight[layer], precision=HIGHEST_PRECISION) + transform_bias[layer]
        pre_g = jnp.dot(hidden, gate_weight[layer], precision=HIGHEST_PRECISION) + gate_bias[layer]
        gate = jax.nn.sigmoid(pre_g)
        hidden = gate * jax.nn.silu(pre_t) + (1.0 - gate) * hidden
    return live_mask[:, None] * (jnp.dot(hidden, proj_weight, precision=HIGHEST_PRECISION) + proj_bias)

def reference(chars, counts, char_table, conv_weight, conv_bias, transform_weight, transform_bias, gate_weight, gate_bias, proj_weight, proj_bias, cotangent):
    weights = (char_table, conv_weight, conv_bias, transform_weight, transform_bias, gate_weight, gate_bias, proj_weight, proj_bias)
    total = jnp.sum(counts).astype(jnp.float32)
    scale = lax.rsqrt(total)
    char_blocks = chars.reshape(GROUPS, GROUP, CHARS)
    cot_blocks = cotangent.reshape(GROUPS, GROUP, PROJ)

    def block_step(accumulated, item):
        block_chars, block_count, block_cot = item
        live_mask = (jnp.arange(GROUP, dtype=jnp.int32) < block_count).astype(jnp.float32)
        output, pullback = jax.vjp(lambda *values: forward(values, block_chars, live_mask), *weights)
        gradients = pullback(block_cot * scale)
        return (tuple((left + right for left, right in zip(accumulated, gradients))), output)
    zeros = tuple((jnp.zeros_like(weight) for weight in weights))
    gradients, outputs = lax.scan(block_step, zeros, (char_blocks, counts, cot_blocks))
    grad_table, grad_kernel, grad_cbias, grad_wt, grad_bt, grad_wg, grad_bg, grad_pw, grad_pb = gradients
    return (outputs.reshape(TOKENS, PROJ), grad_table, grad_kernel, grad_cbias, grad_wt, grad_bt, grad_wg, grad_bg, grad_pw, grad_pb)
```

```python
import functools

import jax
import jax.numpy as jnp
from jax import lax
from jax.experimental import pallas as pl
from jax.experimental.pallas import tpu as pltpu
from jax.sharding import PartitionSpec as P

F32 = jnp.float32
BF16 = jnp.bfloat16
LOG2E = 1.4426950408889634
MIB = 2**20

TOK = 128
CH = 50
CHP = 56
FB = 512
TAPS = 7
EMB = 16
ROWS = TAPS * EMB
BANKS = 4
RING = 4
STEP = 10

VMEM_LIMIT = 62 * MIB

VMEM = functools.partial(pl.BlockSpec, memory_space=pltpu.VMEM)
ANY = functools.partial(pl.BlockSpec, memory_space=pl.ANY)
SMEM = functools.partial(pl.BlockSpec, memory_space=pltpu.SMEM)


PARAMS = pltpu.CompilerParams(vmem_limit_bytes=VMEM_LIMIT)


def shape(*dims, dtype=F32):
    return jax.ShapeDtypeStruct(dims, dtype)


def run(kernel, name, outs, meta, inputs, scratch=(), after=(), specs=None, out_specs=None, aliases=None):
    inputs, after = list(inputs), list(after)
    count = 1 + len(inputs)

    def body(*refs):
        kernel(*refs[:count], *refs[count + len(after) :])

    return pl.pallas_call(
        body,
        out_shape=outs,
        in_specs=[SMEM()] + list(specs or [VMEM()] * len(inputs)) + [ANY()] * len(after),
        out_specs=list(out_specs or [VMEM()] * len(outs)),
        scratch_shapes=list(scratch),
        input_output_aliases=aliases or {},
        compiler_params=PARAMS,
        name=name,
    )(meta, *inputs, *after)


def gate_kernel(meta, *refs):
    pass


def gate(meta, values, after):
    values = list(values)
    return run(
        gate_kernel,
        "gate",
        [jax.ShapeDtypeStruct(v.shape, v.dtype) for v in values],
        meta,
        values,
        after=after,
        specs=[ANY()] * len(values),
        out_specs=[ANY()] * len(values),
        aliases={1 + i: i for i in range(len(values))},
    )


def along_bank(value, shift):
    return lax.ppermute(value, "bank", [(i, (i + shift) % BANKS) for i in range(BANKS)])


def place_of(z, y, core):
    return (z * RING + y) * 2 + core


def to_partner(value):
    return lax.ppermute(value, "dp", [(i, i ^ 1) for i in range(2 * RING * RING)])


def ring_perm(shift, z_core):
    perm = []
    for z in range(RING):
        for y in range(RING):
            for core in range(2):
                if core == z_core:
                    to = place_of((z + shift) % RING, y, core)
                else:
                    to = place_of(z, (y + shift) % RING, core)
                perm.append((place_of(z, y, core), to))
    return perm


FIRST_RINGS = [[place_of(z, y, 0) for z in range(RING)] for y in range(RING)] + [
    [place_of(z, y, 1) for y in range(RING)] for z in range(RING)
]
SECOND_RINGS = [[place_of(z, y, 0) for y in range(RING)] for z in range(RING)] + [
    [place_of(z, y, 1) for z in range(RING)] for y in range(RING)
]


def along_first(value, shift):
    return lax.ppermute(value, "dp", ring_perm(shift, 0))


def along_second(value, shift):
    return lax.ppermute(value, "dp", ring_perm(shift, 1))


def split(value):
    high = value.astype(BF16)
    low = (value - high.astype(F32)).astype(BF16)
    return high, low


def dot(left, right, dims=((1,), (0,))):
    return lax.dot_general(left, right, (dims, ((), ())), preferred_element_type=F32)


def dot3(left, right, dims=((1,), (0,))):
    lh, ll = split(left)
    rh, rl = split(right)
    return dot(lh, rh, dims) + dot(ll, rh, dims) + dot(lh, rl, dims)


def widths_of(column):
    width = jnp.ones_like(column)
    for power in range(6):
        width = width + (column >= 32 * 2**power).astype(jnp.int32)
    return width


def conv_forward_kernel(
    meta, chars, table, weight, bias, pooled, summed, lifted_out, emb_high, emb_low, wide, wide_table, lifted, sems
):
    start = meta[0] * FB
    column = start + lax.broadcasted_iota(jnp.int32, (ROWS, FB), 1)
    tap = lax.broadcasted_iota(jnp.int32, (ROWS, FB), 0) // EMB
    kernel = jnp.where(tap < widths_of(column), weight[...], 0.0) * LOG2E
    high = kernel.astype(BF16).astype(F32)
    shift = bias[...] * LOG2E
    shift_high = shift.astype(BF16).astype(F32)
    row = lax.broadcasted_iota(jnp.int32, (EMB, FB), 0)
    shifts = jnp.where(row == 0, shift_high, jnp.where(row == 1, shift - shift_high, 0.0))
    rows = [high, kernel - high, shifts, jnp.zeros((EMB, FB), F32)]
    wide[...] = jnp.concatenate(rows, axis=0).T.astype(BF16)
    wide_table[:, 0 : table.shape[1]] = table[...]
    parts = [wide_table[:, 128 * i : 128 * (i + 1)] for i in range(3)]
    for p in range(CH):
        ids = jnp.broadcast_to(chars[p : p + 1, :], (EMB, TOK))
        lane = ids & 127
        part = ids >> 7
        found = [
            jnp.take_along_axis(t, lane, axis=1, mode="promise_in_bounds") for t in parts
        ]
        value = jnp.where(part == 0, found[0], jnp.where(part == 1, found[1], found[2]))
        high, low = split(value)
        emb_high[p * EMB : (p + 1) * EMB, :] = high
        emb_low[p * EMB : (p + 1) * EMB, :] = low
    zeros = jnp.zeros(((CHP - CH) * EMB, TOK), BF16)
    emb_high[CH * EMB :, :] = zeros
    emb_low[CH * EMB :, :] = zeros
    one_row = lax.broadcasted_iota(jnp.int32, (EMB, 2 * TOK), 0)
    ones = jnp.where(one_row < 2, 1.0, 0.0).astype(BF16)
    width = widths_of(start + lax.broadcasted_iota(jnp.int32, (FB, TOK), 0))

    def window(ref, pair):
        base = pair * 2 * EMB
        return jnp.concatenate(
            [ref[base : base + ROWS, :], ref[base + EMB : base + EMB + ROWS, :]], axis=1
        )

    for pair in range(CH // 2):
        high = window(emb_high, pair)
        low = window(emb_low, pair)
        pre = dot(wide[:, : 2 * ROWS + EMB], jnp.concatenate([high, high, ones], axis=0))
        pre += dot(wide[:, :ROWS], low)
        both = jnp.exp2(pre)
        first, second = both[:, :TOK], both[:, TOK:]
        if 2 * pair + 1 > CH - TAPS:
            first = jnp.where(width <= CH - 2 * pair, first, 0.0)
            second = jnp.where(width <= CH - 2 * pair - 1, second, 0.0)
        lifted[2 * pair] = first
        lifted[2 * pair + 1] = second
        pltpu.make_async_copy(
            lifted.at[pl.ds(2 * pair, 2)], lifted_out.at[pl.ds(2 * pair, 2)], sems.at[pair]
        ).start()
        if pair:
            summed[...] += first + second
        else:
            summed[...] = first + second
    valid = (CH + 1 - width).astype(F32)
    total = summed[...] + valid
    summed[...] = total
    pooled[...] = jnp.log(total / valid).T
    for pair in range(CH // 2):
        pltpu.make_async_copy(
            lifted.at[pl.ds(2 * pair, 2)], lifted_out.at[pl.ds(2 * pair, 2)], sems.at[pair]
        ).wait()


def conv_forward(meta, chars_t, table_t, weight, bias, after):
    return run(
        conv_forward_kernel,
        "conv_forward",
        (
            shape(TOK, FB),
            shape(FB, TOK),
            shape(CH, FB, TOK),
            shape(CHP * EMB, TOK, dtype=BF16),
            shape(CHP * EMB, TOK, dtype=BF16),
        ),
        meta,
        (chars_t, table_t, weight, bias),
        (
            pltpu.VMEM((FB, 2 * ROWS + 2 * EMB), BF16),
            pltpu.VMEM((EMB, 384), F32),
            pltpu.VMEM((CH, FB, TOK), F32),
            pltpu.SemaphoreType.DMA((CH // 2,)),
        ),
        after,
        out_specs=[VMEM(), VMEM(), ANY(), VMEM(), VMEM()],
    )


def bank_sum_kernel(meta, count, r0, r1, r2, r3, residual, summed, proj_bias, coef, encoded):
    total = r0[...] + r1[...] + r2[...] + r3[...]
    coef[...] = (total[0:TOK] + residual[...]).T / summed[...]
    value = jnp.concatenate([total[TOK:, q * 128 : (q + 1) * 128] for q in range(4)], axis=0)
    live = live_rows(count[0], 128)
    encoded[...] = jnp.where(live, value + proj_bias[...], 0.0)


def conv_backward_kernel(
    meta, coef, lifted, emb_high, emb_low, weight, chars, bias0, bias1, bias_p, keep, send, table,
    kernel, grads, windows, acc, grad_emb, buffer, sems,
):
    start = meta[0] * FB
    copies = [
        pltpu.make_async_copy(
            lifted.at[pl.ds(i * 2, 2)], buffer.at[pl.ds(i * 2, 2)], sems.at[i]
        )
        for i in range(CH // 2)
    ]
    for copy in copies:
        copy.start()
    column = start + lax.broadcasted_iota(jnp.int32, (ROWS, FB), 1)
    tap = lax.broadcasted_iota(jnp.int32, (ROWS, FB), 0) // EMB
    high, low = split(jnp.where(tap < widths_of(column), weight[...], 0.0))
    kernel[0:ROWS] = high
    kernel[ROWS:] = low
    grad_emb[...] = jnp.zeros_like(grad_emb)
    row = lax.broadcasted_iota(jnp.int32, (EMB, STEP * TOK), 0)
    ones = jnp.where(row < 1, 1.0, 0.0).astype(BF16)
    for slot in range(2):
        windows[slot, 2 * ROWS :, :] = ones

    for step in range(CH // STEP):
        slot = step % 2
        for j in range(STEP):
            p = step * STEP + j
            if p % 2 == 0:
                copies[p // 2].wait()
            high, low = split(coef[...] * buffer[p])
            lanes = slice(j * TOK, (j + 1) * TOK)
            grads[slot, 0:FB, lanes] = high
            grads[slot, FB:, lanes] = low
            windows[slot, 0:ROWS, lanes] = emb_high[p * EMB : p * EMB + ROWS, :]
            windows[slot, ROWS : 2 * ROWS, lanes] = emb_low[p * EMB : p * EMB + ROWS, :]
        part = dot(grads[slot], windows[slot], ((1,), (1,)))
        if step:
            acc[...] += part
        else:
            acc[...] = part
        from_high = dot(kernel[...], grads[slot, 0:FB, :])
        from_low = dot(kernel[0:ROWS, :], grads[slot, FB:, :])
        grad_windows = from_high[0:ROWS] + from_high[ROWS:] + from_low
        for j in range(STEP):
            base = (step * STEP + j) * EMB
            grad_emb[base : base + ROWS, :] += grad_windows[:, j * TOK : (j + 1) * TOK]

    total = acc[...]
    grad_kernel = total[0:FB, 0:ROWS] + total[0:FB, ROWS : 2 * ROWS] + total[FB:, 0:ROWS]
    grad_bias = total[0:FB, 2 * ROWS :] + total[FB:, 2 * ROWS :]
    full = jnp.concatenate([grad_kernel, grad_bias], axis=1).T
    column = start + lax.broadcasted_iota(jnp.int32, (ROWS + EMB, FB), 1)
    row = lax.broadcasted_iota(jnp.int32, (ROWS + EMB, FB), 0)
    full = jnp.where((row > ROWS) | (row // EMB >= widths_of(column)) & (row < ROWS), 0.0, full)
    more = jnp.concatenate(
        [
            bias0[0:2],
            bias1[0:2],
            jnp.concatenate([bias_p[0:1], jnp.zeros((1, FB - 128), F32)], axis=1),
            jnp.zeros((10, FB), F32),
        ],
        axis=0,
    )
    full = jnp.concatenate([full[: ROWS + 1], more], axis=0)
    first_core = meta[1] == 0
    keep[...] = jnp.where(first_core, full[:64], full[64:])
    send[...] = jnp.where(first_core, full[64:], full[:64])
    found = jnp.zeros((2 * EMB, 384), F32)
    vocab = lax.broadcasted_iota(jnp.int32, (TOK, 384), 1)
    for begin in range(0, CH, STEP):
        left, right = [], []
        for q in range(begin, begin + STEP):
            high, low = split(grad_emb[q * EMB : (q + 1) * EMB, :])
            left.append(jnp.concatenate([high, low], axis=0))
            right.append(jnp.where(chars[:, q : q + 1] == vocab, 1.0, 0.0).astype(BF16))
        found += dot(jnp.concatenate(left, axis=1), jnp.concatenate(right, axis=0))
    found = found[0:EMB] + found[EMB:]
    for i in range(3):
        table[i * EMB : (i + 1) * EMB] = found[:, i * 128 : (i + 1) * 128]


def conv_backward(meta, inputs, weight, chars, biases, after):
    return run(
        conv_backward_kernel,
        "conv_backward",
        [shape(64, FB), shape(64, FB), shape(48, 128)],
        meta,
        (*inputs, weight, chars, *biases),
        (
            pltpu.VMEM((2 * ROWS, FB), BF16),
            pltpu.VMEM((2, 2 * FB, STEP * TOK), BF16),
            pltpu.VMEM((2, 2 * ROWS + EMB, STEP * TOK), BF16),
            pltpu.VMEM((2 * FB, 2 * ROWS + EMB), F32),
            pltpu.VMEM((CHP * EMB, TOK), F32),
            pltpu.VMEM((CH, FB, TOK), F32),
            pltpu.SemaphoreType.DMA((CH // 2,)),
        ),
        after,
        [VMEM(), ANY()] + [VMEM()] * 7,
    )


def live_rows(count, columns):
    return lax.broadcasted_iota(jnp.int32, (TOK, columns), 0) < count


def early_rows_kernel(meta, received, out, grads):
    for j in range(1, BANKS):
        source = (meta[0] + BANKS - j) % BANKS
        out[j - 1] = received[source, TOK:]
        grads[j - 1] = received[source, 0:TOK]


def bank_rows(meta, mine, others):
    found = []
    first = meta[1] == 0
    for i in range(BANKS - 1):
        low = jnp.where(first, mine[i], others[i])
        high = jnp.where(first, others[i], mine[i])
        found.append(jnp.concatenate([low, high], axis=0))
    return found


def grad_hidden_kernel(meta, count, cot, grads, mine, others, proj, token, out):
    live = live_rows(count[0], 128)
    total = dot3(jnp.where(live, cot[...], 0.0), proj[...], ((1,), (1,)))
    for i, rows in enumerate(bank_rows(meta, mine, others)):
        total += dot3(jnp.where(live, grads[i], 0.0), rows, ((1,), (1,)))
    out[...] = total


def with_bank_rows(kernel, name, outs, meta, count, inputs, proj, after):
    return pl.pallas_call(
        kernel,
        out_shape=outs,
        grid_spec=pltpu.PrefetchScalarGridSpec(
            num_scalar_prefetch=2,
            grid=(1,),
            in_specs=[VMEM()] * len(inputs)
            + [pl.BlockSpec((FB, 128), lambda i, meta, count: (meta[0], 0)), ANY()],
            out_specs=[VMEM()] * len(outs),
        ),
        compiler_params=PARAMS,
        name=name,
    )(meta, count, *inputs, proj, after)


def projection_kernel(meta, count, hidden, cot, cots, mine, others, proj, token, keep, send, encoded, bias):
    live = live_rows(count[0], 128)
    grads = [jnp.where(live, value, 0.0) for value in (cot[...], cots[0], cots[1], cots[2])]
    rows = [proj[...]] + bank_rows(meta, mine, others)
    value = hidden[...]
    both = jnp.concatenate(split(value), axis=0)
    turned = jnp.concatenate(split(value.T), axis=0)
    first = meta[1] == 0
    for j in range(BANKS):
        high, low = split(rows[j])
        part = dot(both, high)
        part = part[0:TOK] + part[TOK:] + dot(both[0:TOK], low)
        for q in range(4):
            encoded[j * 32 : (j + 1) * 32, q * 128 : (q + 1) * 128] = part[q * 32 : (q + 1) * 32]
        high, low = split(grads[j])
        part = dot(turned, high)
        part = part[0:FB] + part[FB:] + dot(turned[0:FB], low)
        lanes = slice(j * 128, (j + 1) * 128)
        keep[:, lanes] = jnp.where(first, part[0:256], part[256:])
        send[:, lanes] = jnp.where(first, part[256:], part[0:256])
    bias[...] = jnp.broadcast_to(jnp.sum(grads[0], axis=0, keepdims=True), (8, 128))


def early_pack_kernel(meta, cot, p1, p2, p3, out):
    for j, ref in enumerate((p1, p2, p3)):
        to = (meta[0] + 1 + j) % BANKS
        out[to, 0:TOK] = cot[...]
        out[to, TOK:] = ref[...]


def early_pack(meta, cot, proj):
    def rows(j):
        return pl.BlockSpec((256, 128), lambda i, meta: ((meta[0] + j) % BANKS * 2 + meta[1], 0))

    return pl.pallas_call(
        early_pack_kernel,
        out_shape=shape(BANKS, TOK + 256, 128),
        grid_spec=pltpu.PrefetchScalarGridSpec(
            num_scalar_prefetch=1,
            grid=(1,),
            in_specs=[VMEM()] + [rows(j) for j in range(1, BANKS)],
            out_specs=VMEM(),
        ),
        compiler_params=PARAMS,
        name="early_pack",
    )(meta, cot, proj, proj, proj)


def sigmoid(value):
    return 1.0 / (1.0 + jnp.exp(-value))


def weight_copies(layer, shift, meta, weights, buffer, sems):
    found = []
    for i in range(BANKS):
        for m, ref in enumerate(weights):
            base = pl.multiple_of((meta[0] + shift + i) % BANKS * FB, FB)
            for half in range(2):
                rows = pl.ds(base + half * 256, 256)
                found.append(
                    pltpu.make_async_copy(
                        ref.at[layer, rows],
                        buffer.at[m, i, pl.ds(half * 256, 256)],
                        sems.at[m, i, half],
                    )
                )
    return found


WEIGHT_SCRATCH = (
    pltpu.VMEM((2, BANKS, FB, FB), F32),
    pltpu.SemaphoreType.DMA((2, BANKS, 2)),
)


def forward_kernel(layer, meta, x0, x1, x2, x3, weight_t, weight_g, bias_t, bias_g, *rest):
    last = layer == 1
    *rest, buffer, sems = rest
    if last:
        grad, hidden, out_t, out_g, out_r, keep, stack = rest
    else:
        hidden, out_t, out_g, out_r, stack = rest
    copies = weight_copies(layer, 0, meta, (weight_t, weight_g), buffer, sems)
    for copy in copies:
        copy.start()
    acc = [jnp.zeros((TOK, FB), F32), jnp.zeros((TOK, FB), F32)]
    for i, ref in enumerate((x0, x1, x2, x3)):
        value = ref[...]
        stack[i * TOK : (i + 1) * TOK] = value
        both = jnp.concatenate(split(value), axis=0)
        for m in range(2):
            for copy in copies[i * 4 + m * 2 : i * 4 + m * 2 + 2]:
                copy.wait()
            high, low = split(buffer[m, i])
            found = dot(both, high)
            acc[m] += found[0:TOK] + found[TOK:] + dot(both[0:TOK], low)
    pre_t = acc[0] + bias_t[layer : layer + 1]
    gate = sigmoid(acc[1] + bias_g[layer : layer + 1])
    sigma = sigmoid(pre_t)
    own = x0[...]
    silu = pre_t * sigma
    hidden[...] = gate * silu + (1.0 - gate) * own
    slope_t = gate * sigma * (1.0 + pre_t * (1.0 - sigma))
    slope_g = (silu - own) * gate * (1.0 - gate)
    if last:
        grad_t = grad[...] * slope_t
        grad_g = grad[...] * slope_g
        out_t[...] = grad_t
        out_g[...] = grad_g
        out_r[...] = grad[...] * (1.0 - gate)
        first = meta[1] == 0
        keep[...] = jnp.where(first, grad_t, grad_g)
        stack[BANKS * TOK :] = jnp.where(first, grad_g, grad_t)
    else:
        out_t[...] = slope_t
        out_g[...] = slope_g
        out_r[...] = 1.0 - gate


def highway_forward(layer, meta, blocks, weight_t, weight_g, bias_t, bias_g, after, grad=()):
    last = layer == 1
    outs = [shape(TOK, FB)] * (4 + last) + [shape((BANKS + last) * TOK, FB)]
    return run(
        functools.partial(forward_kernel, layer),
        "highway_forward",
        outs,
        meta,
        (*blocks, weight_t, weight_g, bias_t, bias_g, *grad),
        WEIGHT_SCRATCH,
        after,
        [VMEM()] * 4 + [ANY()] * 2 + [VMEM()] * (2 + last),
    )


def slopes_kernel(
    meta, count, received, residual, slope_t, slope_g, slope_r, out_t, out_g, out_r, keep, send
):
    grad = received[0] + received[1] + received[2] + received[3] + residual[...]
    grad_t = grad * slope_t[...]
    grad_g = grad * slope_g[...]
    first = meta[1] == 0
    out_t[...] = grad_t
    out_g[...] = grad_g
    out_r[...] = grad * slope_r[...]
    keep[...] = jnp.where(first, grad_t, grad_g)
    send[0:TOK] = jnp.where(first, grad_g, grad_t)
    send[TOK:] = jnp.full((8, FB), count[0].astype(F32))


def backward_kernel(layer, meta, grad_t, grad_g, *rest):
    *rest, bias, buffer, sems = rest
    encoded = rest.pop(0) if layer == 0 else None
    weight_t, weight_g, *outs = rest
    if layer == 1:
        outs = [outs[0].at[(meta[0] + 1 + i) % BANKS] for i in range(BANKS)]
    copies = weight_copies(layer, 1, meta, (weight_t, weight_g), buffer, sems)
    for copy in copies:
        copy.start()
    left = [jnp.concatenate(split(ref[...]), axis=0) for ref in (grad_t, grad_g)]
    sums = [jnp.sum(ref[...], axis=0, keepdims=True) for ref in (grad_t, grad_g)]
    row = lax.broadcasted_iota(jnp.int32, (8, FB), 0)
    bias[...] = jnp.where(row == 0, sums[0], jnp.where(row == 1, sums[1], 0.0))
    for i in range(BANKS):
        total = jnp.zeros((TOK, FB), F32)
        for m in range(2):
            for copy in copies[i * 4 + m * 2 : i * 4 + m * 2 + 2]:
                copy.wait()
            high, low = split(buffer[m, i])
            both = dot(left[m], high, ((1,), (1,)))
            total += both[0:TOK] + both[TOK:] + dot(left[m][0:TOK], low, ((1,), (1,)))
        outs[i][0:TOK] = total
        if layer == 0:
            j = BANKS - 1 - i
            outs[i][TOK:] = encoded[j * 32 : (j + 1) * 32]


def highway_backward(layer, meta, grad_t, grad_g, weight_t, weight_g, after, encoded=()):
    parts = [shape(TOK + 32, FB)] * BANKS if layer == 0 else [shape(BANKS, TOK, FB)]
    return run(
        functools.partial(backward_kernel, layer),
        "highway_backward",
        parts + [shape(8, FB)],
        meta,
        (grad_t, grad_g, *encoded, weight_t, weight_g),
        WEIGHT_SCRATCH,
        after,
        [VMEM()] * (2 + len(encoded)) + [ANY()] * 2,
    )


PART = FB + 64 + 8


def local_grad_kernel(layer, meta, mine, theirs, *refs):
    *refs, out, stage, sems = refs
    if layer == 1:
        grads = [refs[0][...], theirs[BANKS * TOK :]]
    else:
        count, keep, other, keep_p, other_p = refs
        grads = [keep[...], other[0:TOK]]
        chip = other[TOK:] + count[0].astype(F32)
    high, low = split(jnp.concatenate(grads, axis=0))
    copies = []
    for i in range(BANKS):
        rows = slice(i * TOK, (i + 1) * TOK)
        hidden = jnp.concatenate([mine[rows], theirs[rows]], axis=0).T
        left_high, left_low = split(hidden)
        stage[i, 0:FB] = dot(left_high, high) + dot(left_low, high) + dot(left_high, low)
        position = (meta[0] + i) % BANKS
        if layer == 0:
            rows = pl.ds(pl.multiple_of(position * 64, 64), 64)
            stage[i, FB : FB + 64] = keep_p[rows, :] + other_p[rows, :]
            stage[i, FB + 64 :] = chip
        copies.append(pltpu.make_async_copy(stage.at[i], out.at[position], sems.at[i]))
        copies[-1].start()
    for copy in copies:
        copy.wait()


def local_grad(layer, meta, inputs, after):
    rows = FB if layer == 1 else PART
    specs = [VMEM()] * len(inputs)
    if layer == 0:
        specs[2] = SMEM()
    (out,) = run(
        functools.partial(local_grad_kernel, layer),
        "local_grad",
        [shape(RING, rows, FB)],
        meta,
        inputs,
        (pltpu.VMEM((BANKS, rows, FB), F32), pltpu.SemaphoreType.DMA((BANKS,))),
        after,
        specs,
        [ANY()],
    )
    return out


def middle_kernel(meta, received, *rest):
    outs, total = rest[:-1], rest[-1]
    total[...] = received[0] + received[1] + received[2] + received[3]
    for k, out in enumerate(outs):
        spot = (meta[3] + k) % RING
        rows = pl.ds(pl.multiple_of(spot * 128, 128), 128)
        out[0:128] = total[rows, :]
        out[128:144] = total[pl.ds(pl.multiple_of(FB + spot * 16, 16), 16), :]
        out[144:] = total[FB + 64 :]


def collect_ring_kernel(meta, r0, r1, r2, r3, table, out, factor, *crossing):
    total = r0[...] + r1[...] + r2[...] + r3[...]
    scale = lax.rsqrt(total[144:145, :])
    out[...] = total[0:128] * scale
    for k, ref in enumerate(crossing):
        j = (BANKS - k) % BANKS
        ref[0:EMB] = total[128:144, j * 128 : (j + 1) * 128] * scale[:, 0:128]
        ref[EMB:] = table[...] * scale[:, 0:128]
    factor[...] = jnp.broadcast_to(scale, (8, FB))


def collect_kernel(meta, own, keep, theirs, x0, x1, x2, x3, factor, out):
    scale = factor[0:1, :]
    out[0:128] = own[...]
    for j, ref in enumerate((x0, x1, x2, x3)):
        out[128:144, j * 128 : (j + 1) * 128] = ref[0:EMB]
    out[144:208] = (keep[...] + theirs[...]) * scale
    table = x0[EMB:] + x1[EMB:] + x2[EMB:] + x3[EMB:]
    blocks = [table[i * EMB : (i + 1) * EMB] for i in range(3)] + [jnp.zeros((EMB, 128), F32)]
    out[208:] = jnp.concatenate(blocks, axis=1)


def merge_kernel(meta, *refs):
    *parts, low, high = refs
    for i, ref in enumerate(parts):
        out, spot = (low, i) if i < 2 else (high, i - 2)
        out[spot * 144 : (spot + 1) * 144] = ref[0:144]
    high[288:] = sum(ref[144:] for ref in parts)


def place_last_kernel(given, meta, gathered, factor, *refs):
    out_t, out_g, stage, loads, puts = refs[given:]
    copies = [
        pltpu.make_async_copy(
            gathered.at[pl.ds(i * 2, 2)], stage.at[pl.ds(i * 2, 2)], loads.at[i]
        )
        for i in range(RING * RING)
    ]
    for copy in copies:
        copy.start()
    scale = factor[0:1, :]
    done = []
    for i, copy in enumerate(copies):
        copy.wait()
        for core, out in enumerate((out_t, out_g)):
            stage[i * 2 + core] = stage[i * 2 + core] * scale
            row = i if core == 0 else i % RING * RING + i // RING
            done.append(
                pltpu.make_async_copy(
                    stage.at[i * 2 + core], out.at[1, pl.ds(row * 128, 128)], puts.at[i * 2 + core]
                )
            )
            done[-1].start()
    for copy in done:
        copy.wait()


def place_last(meta, gathered, factor, outs, after):
    return run(
        functools.partial(place_last_kernel, len(outs)),
        "place",
        [shape(2, 2048, FB)] * 2,
        meta,
        (gathered, factor, *outs),
        (
            pltpu.VMEM((32, 128, FB), F32),
            pltpu.SemaphoreType.DMA((16,)),
            pltpu.SemaphoreType.DMA((32,)),
        ),
        after,
        [ANY(), VMEM()] + [ANY()] * len(outs),
        [ANY()] * 2,
        {3 + i: i for i in range(len(outs))},
    )


ROWS0 = 144


def place_kernel(sources, meta, *refs):
    count = len(sources)
    mine, theirs = refs[:count], refs[count : 2 * count]
    outs = refs[-5 - count : -2 - count]
    stages, loads, sems = refs[-2 - count : -2], refs[-2], refs[-1]

    def load(i, core):
        ref = (mine, theirs)[core][i]
        many = len(sources[i][1]) * ROWS0
        return pltpu.make_async_copy(ref.at[pl.ds(0, many)], stages[i].at[core], loads.at[i, core])

    for i in range(count):
        for core in range(2):
            load(i, core).start()
    puts = []
    for i, (j, blocks) in enumerate(sources):
        for core in range(2):
            load(i, core).wait()
        for stream in range(2):
            holder = jnp.where(meta[1] == stream, 0, 1)
            major, minor = (meta[4], meta[5]) if stream == 0 else (meta[5], meta[4])
            first = (major + RING - j) % RING
            for spot, k in enumerate(blocks):
                second = (minor + RING - k) % RING
                base = pl.multiple_of((first * RING + second) * 128, 128)
                found = [
                    (
                        stages[i].at[holder, pl.ds(spot * ROWS0, 128)],
                        outs[stream].at[0, pl.ds(base, 128)],
                    )
                ]
                for q in range(BANKS):
                    bank = (meta[0] + BANKS - q) % BANKS
                    base = pl.multiple_of(bank * FB + stream * 256 + first * 64 + second * 16, 16)
                    found.append(
                        (
                            stages[i].at[holder, pl.ds(spot * ROWS0 + 128, 16), pl.ds(q * 128, 128)],
                            outs[2].at[pl.ds(base, 16)],
                        )
                    )
                for a, b in found:
                    puts.append(pltpu.make_async_copy(a, b, sems.at[len(puts)]))
                    puts[-1].start()
    for copy in puts:
        copy.wait()


def place(sources, meta, mine, theirs, outs, after):
    total = sum(len(blocks) for _, blocks in sources) * 2 * 5
    inputs = [*mine, *theirs, *outs]
    return run(
        functools.partial(place_kernel, sources),
        "place",
        [shape(2, 2048, FB)] * 2 + [shape(2048, 128)],
        meta,
        inputs,
        [pltpu.VMEM((2, len(blocks) * ROWS0, FB), F32) for _, blocks in sources]
        + [
            pltpu.SemaphoreType.DMA((len(sources), 2)),
            pltpu.SemaphoreType.DMA((total,)),
        ],
        after,
        specs=[ANY()] * len(inputs),
        out_specs=[ANY()] * 3,
        aliases={1 + 2 * len(sources) + i: i for i in range(len(outs))},
    )


def finish_kernel(meta, *refs):
    *refs, stage, sems = refs
    kernel, cbias, bt, bg, pb, table = refs[-6:]
    copies = [
        pltpu.make_async_copy(ref.at[pl.ds(ref.shape[0] - 80, 80)], stage.at[i], sems.at[i])
        for i, ref in enumerate(refs[: 2 * RING])
    ]
    for copy in copies:
        copy.start()
    for copy in copies:
        copy.wait()
    own = sum(stage[i] for i in range(RING))
    other = sum(stage[i] for i in range(RING, 2 * RING))
    first = meta[1] == 0
    low = jnp.where(first, own, other)
    high = jnp.where(first, other, own)
    flat = jnp.concatenate([low[0:64], high[0:64]], axis=0)
    kernel[...] = flat[:ROWS]
    cbias[...] = flat[ROWS : ROWS + 1]
    row = ROWS + 1
    bt[...] = jnp.concatenate([flat[row : row + 1], flat[row + 2 : row + 3]], axis=0)
    bg[...] = jnp.concatenate([flat[row + 1 : row + 2], flat[row + 3 : row + 4]], axis=0)
    pb[...] = flat[row + 4 : row + 5, 0:128]
    table[...] = (own[64:] + other[64:])[:, 0:262]


def finish(meta, mine, theirs):
    outs = [
        shape(ROWS, FB), shape(1, FB), shape(2, FB), shape(2, FB), shape(1, 128), shape(EMB, 262),
    ]
    return run(
        finish_kernel,
        "finish",
        outs,
        meta,
        (*mine, *theirs),
        (pltpu.VMEM((2 * RING, 80, FB), F32), pltpu.SemaphoreType.DMA((2 * RING,))),
        specs=[ANY()] * (2 * RING),
    )


def on_device(
    chars,
    counts,
    char_table,
    conv_weight,
    conv_bias,
    transform_weight,
    transform_bias,
    gate_weight,
    gate_bias,
    proj_weight,
    proj_bias,
    cotangent,
):
    here = lax.axis_index("dp")
    bank = lax.axis_index("bank")
    z, y, core = here // (2 * RING), here // 2 % RING, here % 2
    first = jnp.where(core == 0, z, y)
    second = jnp.where(core == 0, y, z)
    meta = jnp.stack([bank, core, first, second, z, y]).astype(jnp.int32)

    early = early_pack(meta, cotangent, proj_weight)
    early_received = lax.all_to_all(early, "bank", 0, 0, tiled=True)
    pooled, summed, lifted, emb_high, emb_low = conv_forward(
        meta, chars.T, char_table.T, conv_weight, conv_bias[None], [early]
    )

    def gather(block):
        others = {i: along_bank(block, -i) for i in (2, 1, 3)}
        return [block, others[1], others[2], others[3]]

    def bank_pieces(parts):
        return [parts[3]] + [along_bank(parts[i - 1], i) for i in (2, 1, 3)]

    def ring_gather(value, mover):
        moved = {k: mover(value, k) for k in (2, 1, 3)}
        return [value, moved[1], moved[2], moved[3]]

    def ring_pieces(pieces, mover):
        moved = {k: mover(pieces[k], k) for k in (2, 1, 3)}
        return [pieces[0], moved[1], moved[2], moved[3]]

    weights = (transform_weight, gate_weight, transform_bias, gate_bias)
    blocks0 = gather(pooled)
    rows, cots = run(
        early_rows_kernel,
        "early_rows",
        [shape(3, 256, 128), shape(3, TOK, 128)],
        meta,
        (early_received,),
        after=[pooled],
    )
    banks = (cotangent, cots, rows, to_partner(rows))
    hidden1, slope_t, slope_g, slope_r, stack0 = highway_forward(
        0, meta, blocks0, *weights, [rows]
    )
    blocks1 = gather(hidden1)
    (grad_last,) = with_bank_rows(
        grad_hidden_kernel, "grad_hidden", [shape(TOK, FB)], meta, counts, banks, proj_weight, hidden1
    )
    stack0_there = to_partner(stack0)
    hidden2, grad_t1, grad_g1, res1, keep1, stack1 = highway_forward(
        1, meta, blocks1, *weights, [], [grad_last]
    )

    parts1, bias1 = highway_backward(
        1, meta, grad_t1, grad_g1, transform_weight, gate_weight, []
    )
    received1 = lax.all_to_all(parts1, "bank", 0, 0, tiled=True)
    local1 = local_grad(1, meta, (stack1, to_partner(stack1), keep1), [bias1])
    ring1 = lax.psum_scatter(local1, "dp", axis_index_groups=FIRST_RINGS)
    keep_p, send_p, encoded_parts, bias_p = with_bank_rows(
        projection_kernel,
        "projection",
        [shape(256, FB), shape(256, FB), shape(128, FB), shape(8, 128)],
        meta,
        counts,
        (hidden2, *banks),
        proj_weight,
        local1,
    )
    theirs_p = to_partner(send_p)
    grad_t0, grad_g0, res0, keep0, send0 = run(
        slopes_kernel,
        "slopes",
        [shape(TOK, FB)] * 4 + [shape(TOK + 8, FB)],
        meta,
        (counts, received1, res1, slope_t, slope_g, slope_r),
        after=[keep_p],
        specs=[SMEM()] + [VMEM()] * 5,
    )
    local0 = local_grad(
        0, meta, (stack0, stack0_there, counts, keep0, to_partner(send0), keep_p, theirs_p), []
    )
    ring0 = lax.all_to_all(local0, "dp", 0, 0, axis_index_groups=FIRST_RINGS, tiled=True)
    *parts0, bias0 = highway_backward(
        0, meta, grad_t0, grad_g0, transform_weight, gate_weight, [local0], [encoded_parts]
    )
    received0 = bank_pieces(parts0)
    (ring1,) = gate(meta, [ring1], [bias0])
    own1 = lax.psum_scatter(ring1, "dp", axis_index_groups=SECOND_RINGS, tiled=True)
    coef, encoded = run(
        bank_sum_kernel,
        "bank_sum",
        [shape(FB, TOK), shape(TOK, 128)],
        meta,
        (counts, *received0, res0, summed, proj_bias[None]),
        after=[ring1],
        specs=[SMEM()] + [VMEM()] * 7,
    )
    pieces0 = run(
        middle_kernel,
        "middle",
        [shape(152, FB)] * RING,
        meta,
        (ring0,),
        [pltpu.VMEM((PART, FB), F32)],
        [coef],
    )
    second0 = ring_pieces(pieces0, along_second)
    (own1,) = gate(meta, [own1], [pieces0[0]])
    gathered1 = lax.all_gather(own1, "dp")
    keep_s, send_s, table = conv_backward(
        meta,
        (coef, lifted, emb_high, emb_low),
        conv_weight,
        chars,
        (bias0, bias1, bias_p),
        [own1],
    )
    own0, factor, *crossing = run(
        collect_ring_kernel,
        "collect_ring",
        [shape(128, FB), shape(8, FB)] + [shape(64, 128)] * BANKS,
        meta,
        (*second0, table),
    )

    (own0,) = run(
        collect_kernel,
        "collect",
        [shape(224, FB)],
        meta,
        (
            own0,
            keep_s,
            to_partner(send_s),
            crossing[0],
            *[along_bank(crossing[k], k) for k in range(1, BANKS)],
            factor,
        ),
    )
    low, high = run(
        merge_kernel,
        "merge",
        [shape(288, FB), shape(368, FB)],
        meta,
        ring_gather(own0, along_second),
    )
    near = [along_first(low, 1), along_first(high, 1)]
    back = [along_first(low, 3), along_first(high, 3)]
    mine = [low, high]
    theirs = [to_partner(v) for v in mine]
    sources = tuple((j, half) for j in (0, 1, 3, 2) for half in ((0, 1), (2, 3)))
    outs = list(place(sources[0:2], meta, mine[0:2], theirs[0:2], [], []))
    mine += gate(meta, [*near, *back], [outs[2]])
    far = [along_first(mine[2], 1), along_first(mine[5], 3)]
    theirs += [to_partner(v) for v in mine[2:]]
    outs[:2] = place_last(meta, gathered1, factor, outs[:2], [])
    outs = place(sources[2:6], meta, mine[2:6], theirs[2:6], outs, [])
    far = gate(meta, far, [outs[2]])
    mine += far
    theirs += [to_partner(v) for v in far]
    sum_wt, sum_wg, sum_pw = place(sources[6:8], meta, mine[6:8], theirs[6:8], outs, [])
    spots = (1, 3, 5, 7)
    sum_kernel, sum_cbias, sum_bt, sum_bg, sum_pb, sum_table = finish(
        meta, [mine[i] for i in spots], [theirs[i] for i in spots]
    )
    return (
        encoded,
        sum_table.T,
        sum_kernel,
        sum_cbias[0],
        sum_wt,
        sum_bt,
        sum_wg,
        sum_bg,
        sum_pw,
        sum_pb[0],
    )


def solution(mesh):
    return jax.shard_map(
        on_device,
        mesh=mesh,
        in_specs=(
            P("dp", None),
            P("dp"),
            P(),
            P(None, "bank"),
            P("bank"),
            P(None, None, "bank"),
            P(None, "bank"),
            P(None, None, "bank"),
            P(None, "bank"),
            P(None, "bank"),
            P("bank"),
            P("dp", "bank"),
        ),
        out_specs=(
            P("dp", "bank"),
            P(),
            P(None, "bank"),
            P("bank"),
            P(None, None, "bank"),
            P(None, "bank"),
            P(None, None, "bank"),
            P(None, "bank"),
            P(None, "bank"),
            P("bank"),
        ),
        check_vma=False,
    )
```

```python
import functools

import jax
import jax.numpy as jnp
from jax import lax
from jax.experimental import pallas as pl
from jax.experimental.pallas import tpu as pltpu
from jax.sharding import PartitionSpec as P

F32 = jnp.float32
BF16 = jnp.bfloat16
LOG2E = 1.4426950408889634
MIB = 2**20

TOK = 128
CH = 50
CHP = 56
FB = 512
TAPS = 7
EMB = 16
ROWS = TAPS * EMB
BANKS = 4
RING = 4
STEP = 10

VMEM_LIMIT = 62 * MIB

VMEM = functools.partial(pl.BlockSpec, memory_space=pltpu.VMEM)
ANY = functools.partial(pl.BlockSpec, memory_space=pl.ANY)
SMEM = functools.partial(pl.BlockSpec, memory_space=pltpu.SMEM)


PARAMS = pltpu.CompilerParams(vmem_limit_bytes=VMEM_LIMIT)


def shape(*dims, dtype=F32):
    return jax.ShapeDtypeStruct(dims, dtype)


def run(kernel, name, outs, meta, inputs, scratch=(), after=(), specs=None, out_specs=None, aliases=None):
    inputs, after = list(inputs), list(after)
    count = 1 + len(inputs)

    def body(*refs):
        kernel(*refs[:count], *refs[count + len(after) :])

    return pl.pallas_call(
        body,
        out_shape=outs,
        in_specs=[SMEM()] + list(specs or [VMEM()] * len(inputs)) + [ANY()] * len(after),
        out_specs=list(out_specs or [VMEM()] * len(outs)),
        scratch_shapes=list(scratch),
        input_output_aliases=aliases or {},
        compiler_params=PARAMS,
        name=name,
    )(meta, *inputs, *after)


def gate_kernel(meta, *refs):
    pass


def gate(meta, values, after):
    values = list(values)
    return run(
        gate_kernel,
        "gate",
        [jax.ShapeDtypeStruct(v.shape, v.dtype) for v in values],
        meta,
        values,
        after=after,
        specs=[ANY()] * len(values),
        out_specs=[ANY()] * len(values),
        aliases={1 + i: i for i in range(len(values))},
    )


def along_bank(value, shift):
    return lax.ppermute(value, "bank", [(i, (i + shift) % BANKS) for i in range(BANKS)])


def place_of(z, y, core):
    return (z * RING + y) * 2 + core


def to_partner(value):
    return lax.ppermute(value, "dp", [(i, i ^ 1) for i in range(2 * RING * RING)])


def ring_perm(shift, z_core):
    perm = []
    for z in range(RING):
        for y in range(RING):
            for core in range(2):
                if core == z_core:
                    to = place_of((z + shift) % RING, y, core)
                else:
                    to = place_of(z, (y + shift) % RING, core)
                perm.append((place_of(z, y, core), to))
    return perm


FIRST_RINGS = [[place_of(z, y, 0) for z in range(RING)] for y in range(RING)] + [
    [place_of(z, y, 1) for y in range(RING)] for z in range(RING)
]
SECOND_RINGS = [[place_of(z, y, 0) for y in range(RING)] for z in range(RING)] + [
    [place_of(z, y, 1) for z in range(RING)] for y in range(RING)
]


def along_first(value, shift):
    return lax.ppermute(value, "dp", ring_perm(shift, 0))


def along_second(value, shift):
    return lax.ppermute(value, "dp", ring_perm(shift, 1))


def split(value):
    high = value.astype(BF16)
    low = (value - high.astype(F32)).astype(BF16)
    return high, low


def dot(left, right, dims=((1,), (0,))):
    return lax.dot_general(left, right, (dims, ((), ())), preferred_element_type=F32)


def dot3(left, right, dims=((1,), (0,))):
    lh, ll = split(left)
    rh, rl = split(right)
    return dot(lh, rh, dims) + dot(ll, rh, dims) + dot(lh, rl, dims)


def widths_of(column):
    width = jnp.ones_like(column)
    for power in range(6):
        width = width + (column >= 32 * 2**power).astype(jnp.int32)
    return width


def conv_forward_kernel(
    meta, chars, table, weight, bias, pooled, summed, lifted_out, emb_high, emb_low, wide, wide_table, lifted, sems
):
    start = meta[0] * FB
    column = start + lax.broadcasted_iota(jnp.int32, (ROWS, FB), 1)
    tap = lax.broadcasted_iota(jnp.int32, (ROWS, FB), 0) // EMB
    kernel = jnp.where(tap < widths_of(column), weight[...], 0.0) * LOG2E
    high = kernel.astype(BF16).astype(F32)
    shift = bias[...] * LOG2E
    shift_high = shift.astype(BF16).astype(F32)
    row = lax.broadcasted_iota(jnp.int32, (EMB, FB), 0)
    shifts = jnp.where(row == 0, shift_high, jnp.where(row == 1, shift - shift_high, 0.0))
    rows = [high, kernel - high, shifts, jnp.zeros((EMB, FB), F32)]
    wide[...] = jnp.concatenate(rows, axis=0).T.astype(BF16)
    wide_table[:, 0 : table.shape[1]] = table[...]
    parts = [wide_table[:, 128 * i : 128 * (i + 1)] for i in range(3)]
    for p in range(CH):
        ids = jnp.broadcast_to(chars[p : p + 1, :], (EMB, TOK))
        lane = ids & 127
        part = ids >> 7
        found = [
            jnp.take_along_axis(t, lane, axis=1, mode="promise_in_bounds") for t in parts
        ]
        value = jnp.where(part == 0, found[0], jnp.where(part == 1, found[1], found[2]))
        high, low = split(value)
        emb_high[p * EMB : (p + 1) * EMB, :] = high
        emb_low[p * EMB : (p + 1) * EMB, :] = low
    zeros = jnp.zeros(((CHP - CH) * EMB, TOK), BF16)
    emb_high[CH * EMB :, :] = zeros
    emb_low[CH * EMB :, :] = zeros
    one_row = lax.broadcasted_iota(jnp.int32, (EMB, 2 * TOK), 0)
    ones = jnp.where(one_row < 2, 1.0, 0.0).astype(BF16)
    width = widths_of(start + lax.broadcasted_iota(jnp.int32, (FB, TOK), 0))

    def window(ref, pair):
        base = pair * 2 * EMB
        return jnp.concatenate(
            [ref[base : base + ROWS, :], ref[base + EMB : base + EMB + ROWS, :]], axis=1
        )

    for pair in range(CH // 2):
        high = window(emb_high, pair)
        low = window(emb_low, pair)
        pre = dot(wide[:, : 2 * ROWS + EMB], jnp.concatenate([high, high, ones], axis=0))
        pre += dot(wide[:, :ROWS], low)
        both = jnp.exp2(pre)
        first, second = both[:, :TOK], both[:, TOK:]
        if 2 * pair + 1 > CH - TAPS:
            first = jnp.where(width <= CH - 2 * pair, first, 0.0)
            second = jnp.where(width <= CH - 2 * pair - 1, second, 0.0)
        lifted[2 * pair] = first
        lifted[2 * pair + 1] = second
        pltpu.make_async_copy(
            lifted.at[pl.ds(2 * pair, 2)], lifted_out.at[pl.ds(2 * pair, 2)], sems.at[pair]
        ).start()
        if pair:
            summed[...] += first + second
        else:
            summed[...] = first + second
    valid = (CH + 1 - width).astype(F32)
    total = summed[...] + valid
    summed[...] = total
    pooled[...] = jnp.log(total / valid).T
    for pair in range(CH // 2):
        pltpu.make_async_copy(
            lifted.at[pl.ds(2 * pair, 2)], lifted_out.at[pl.ds(2 * pair, 2)], sems.at[pair]
        ).wait()


def conv_forward(meta, chars_t, table_t, weight, bias, after):
    return run(
        conv_forward_kernel,
        "conv_forward",
        (
            shape(TOK, FB),
            shape(FB, TOK),
            shape(CH, FB, TOK),
            shape(CHP * EMB, TOK, dtype=BF16),
            shape(CHP * EMB, TOK, dtype=BF16),
        ),
        meta,
        (chars_t, table_t, weight, bias),
        (
            pltpu.VMEM((FB, 2 * ROWS + 2 * EMB), BF16),
            pltpu.VMEM((EMB, 384), F32),
            pltpu.VMEM((CH, FB, TOK), F32),
            pltpu.SemaphoreType.DMA((CH // 2,)),
        ),
        after,
        out_specs=[VMEM(), VMEM(), ANY(), VMEM(), VMEM()],
    )


def bank_sum_kernel(meta, count, r0, r1, r2, r3, residual, summed, proj_bias, coef, encoded):
    total = r0[...] + r1[...] + r2[...] + r3[...]
    coef[...] = (total[0:TOK] + residual[...]).T / summed[...]
    value = jnp.concatenate([total[TOK:, q * 128 : (q + 1) * 128] for q in range(4)], axis=0)
    live = live_rows(count[0], 128)
    encoded[...] = jnp.where(live, value + proj_bias[...], 0.0)


def conv_backward_kernel(
    meta, coef, lifted, emb_high, emb_low, weight, chars, bias0, bias1, bias_p, keep, send, table,
    kernel, grads, windows, acc, grad_emb, buffer, sems,
):
    start = meta[0] * FB
    copies = [
        pltpu.make_async_copy(
            lifted.at[pl.ds(i * 2, 2)], buffer.at[pl.ds(i * 2, 2)], sems.at[i]
        )
        for i in range(CH // 2)
    ]
    for copy in copies:
        copy.start()
    column = start + lax.broadcasted_iota(jnp.int32, (ROWS, FB), 1)
    tap = lax.broadcasted_iota(jnp.int32, (ROWS, FB), 0) // EMB
    high, low = split(jnp.where(tap < widths_of(column), weight[...], 0.0))
    kernel[0:ROWS] = high
    kernel[ROWS:] = low
    grad_emb[...] = jnp.zeros_like(grad_emb)
    row = lax.broadcasted_iota(jnp.int32, (EMB, STEP * TOK), 0)
    ones = jnp.where(row < 1, 1.0, 0.0).astype(BF16)
    for slot in range(2):
        windows[slot, 2 * ROWS :, :] = ones

    for step in range(CH // STEP):
        slot = step % 2
        for j in range(STEP):
            p = step * STEP + j
            if p % 2 == 0:
                copies[p // 2].wait()
            high, low = split(coef[...] * buffer[p])
            lanes = slice(j * TOK, (j + 1) * TOK)
            grads[slot, 0:FB, lanes] = high
            grads[slot, FB:, lanes] = low
            windows[slot, 0:ROWS, lanes] = emb_high[p * EMB : p * EMB + ROWS, :]
            windows[slot, ROWS : 2 * ROWS, lanes] = emb_low[p * EMB : p * EMB + ROWS, :]
        part = dot(grads[slot], windows[slot], ((1,), (1,)))
        if step:
            acc[...] += part
        else:
            acc[...] = part
        from_high = dot(kernel[...], grads[slot, 0:FB, :])
        from_low = dot(kernel[0:ROWS, :], grads[slot, FB:, :])
        grad_windows = from_high[0:ROWS] + from_high[ROWS:] + from_low
        for j in range(STEP):
            base = (step * STEP + j) * EMB
            grad_emb[base : base + ROWS, :] += grad_windows[:, j * TOK : (j + 1) * TOK]

    total = acc[...]
    grad_kernel = total[0:FB, 0:ROWS] + total[0:FB, ROWS : 2 * ROWS] + total[FB:, 0:ROWS]
    grad_bias = total[0:FB, 2 * ROWS :] + total[FB:, 2 * ROWS :]
    full = jnp.concatenate([grad_kernel, grad_bias], axis=1).T
    column = start + lax.broadcasted_iota(jnp.int32, (ROWS + EMB, FB), 1)
    row = lax.broadcasted_iota(jnp.int32, (ROWS + EMB, FB), 0)
    full = jnp.where((row > ROWS) | (row // EMB >= widths_of(column)) & (row < ROWS), 0.0, full)
    more = jnp.concatenate(
        [
            bias0[0:2],
            bias1[0:2],
            jnp.concatenate([bias_p[0:1], jnp.zeros((1, FB - 128), F32)], axis=1),
            jnp.zeros((10, FB), F32),
        ],
        axis=0,
    )
    full = jnp.concatenate([full[: ROWS + 1], more], axis=0)
    first_core = meta[1] == 0
    keep[...] = jnp.where(first_core, full[:64], full[64:])
    send[...] = jnp.where(first_core, full[64:], full[:64])
    found = jnp.zeros((2 * EMB, 384), F32)
    vocab = lax.broadcasted_iota(jnp.int32, (TOK, 384), 1)
    for begin in range(0, CH, STEP):
        left, right = [], []
        for q in range(begin, begin + STEP):
            high, low = split(grad_emb[q * EMB : (q + 1) * EMB, :])
            left.append(jnp.concatenate([high, low], axis=0))
            right.append(jnp.where(chars[:, q : q + 1] == vocab, 1.0, 0.0).astype(BF16))
        found += dot(jnp.concatenate(left, axis=1), jnp.concatenate(right, axis=0))
    found = found[0:EMB] + found[EMB:]
    for i in range(3):
        table[i * EMB : (i + 1) * EMB] = found[:, i * 128 : (i + 1) * 128]


def conv_backward(meta, inputs, weight, chars, biases, after):
    return run(
        conv_backward_kernel,
        "conv_backward",
        [shape(64, FB), shape(64, FB), shape(48, 128)],
        meta,
        (*inputs, weight, chars, *biases),
        (
            pltpu.VMEM((2 * ROWS, FB), BF16),
            pltpu.VMEM((2, 2 * FB, STEP * TOK), BF16),
            pltpu.VMEM((2, 2 * ROWS + EMB, STEP * TOK), BF16),
            pltpu.VMEM((2 * FB, 2 * ROWS + EMB), F32),
            pltpu.VMEM((CHP * EMB, TOK), F32),
            pltpu.VMEM((CH, FB, TOK), F32),
            pltpu.SemaphoreType.DMA((CH // 2,)),
        ),
        after,
        [VMEM(), ANY()] + [VMEM()] * 7,
    )


def live_rows(count, columns):
    return lax.broadcasted_iota(jnp.int32, (TOK, columns), 0) < count


def early_rows_kernel(meta, received, out, grads):
    for j in range(1, BANKS):
        source = (meta[0] + BANKS - j) % BANKS
        out[j - 1] = received[source, TOK:]
        grads[j - 1] = received[source, 0:TOK]


def bank_rows(meta, mine, others):
    found = []
    first = meta[1] == 0
    for i in range(BANKS - 1):
        low = jnp.where(first, mine[i], others[i])
        high = jnp.where(first, others[i], mine[i])
        found.append(jnp.concatenate([low, high], axis=0))
    return found


def grad_hidden_kernel(meta, count, cot, grads, mine, others, proj, token, out):
    live = live_rows(count[0], 128)
    total = dot3(jnp.where(live, cot[...], 0.0), proj[...], ((1,), (1,)))
    for i, rows in enumerate(bank_rows(meta, mine, others)):
        total += dot3(jnp.where(live, grads[i], 0.0), rows, ((1,), (1,)))
    out[...] = total


def with_bank_rows(kernel, name, outs, meta, count, inputs, proj, after):
    return pl.pallas_call(
        kernel,
        out_shape=outs,
        grid_spec=pltpu.PrefetchScalarGridSpec(
            num_scalar_prefetch=2,
            grid=(1,),
            in_specs=[VMEM()] * len(inputs)
            + [pl.BlockSpec((FB, 128), lambda i, meta, count: (meta[0], 0)), ANY()],
            out_specs=[VMEM()] * len(outs),
        ),
        compiler_params=PARAMS,
        name=name,
    )(meta, count, *inputs, proj, after)


def projection_kernel(meta, count, hidden, cot, cots, mine, others, proj, token, keep, send, encoded, bias):
    live = live_rows(count[0], 128)
    grads = [jnp.where(live, value, 0.0) for value in (cot[...], cots[0], cots[1], cots[2])]
    rows = [proj[...]] + bank_rows(meta, mine, others)
    value = hidden[...]
    both = jnp.concatenate(split(value), axis=0)
    turned = jnp.concatenate(split(value.T), axis=0)
    first = meta[1] == 0
    for j in range(BANKS):
        high, low = split(rows[j])
        part = dot(both, high)
        part = part[0:TOK] + part[TOK:] + dot(both[0:TOK], low)
        for q in range(4):
            encoded[j * 32 : (j + 1) * 32, q * 128 : (q + 1) * 128] = part[q * 32 : (q + 1) * 32]
        high, low = split(grads[j])
        part = dot(turned, high)
        part = part[0:FB] + part[FB:] + dot(turned[0:FB], low)
        lanes = slice(j * 128, (j + 1) * 128)
        keep[:, lanes] = jnp.where(first, part[0:256], part[256:])
        send[:, lanes] = jnp.where(first, part[256:], part[0:256])
    bias[...] = jnp.broadcast_to(jnp.sum(grads[0], axis=0, keepdims=True), (8, 128))


def early_pack_kernel(meta, cot, p1, p2, p3, out):
    for j, ref in enumerate((p1, p2, p3)):
        to = (meta[0] + 1 + j) % BANKS
        out[to, 0:TOK] = cot[...]
        out[to, TOK:] = ref[...]


def early_pack(meta, cot, proj):
    def rows(j):
        return pl.BlockSpec((256, 128), lambda i, meta: ((meta[0] + j) % BANKS * 2 + meta[1], 0))

    return pl.pallas_call(
        early_pack_kernel,
        out_shape=shape(BANKS, TOK + 256, 128),
        grid_spec=pltpu.PrefetchScalarGridSpec(
            num_scalar_prefetch=1,
            grid=(1,),
            in_specs=[VMEM()] + [rows(j) for j in range(1, BANKS)],
            out_specs=VMEM(),
        ),
        compiler_params=PARAMS,
        name="early_pack",
    )(meta, cot, proj, proj, proj)


def sigmoid(value):
    return 1.0 / (1.0 + jnp.exp(-value))


def weight_copies(layer, shift, meta, weights, buffer, sems):
    found = []
    for i in range(BANKS):
        for m, ref in enumerate(weights):
            base = pl.multiple_of((meta[0] + shift + i) % BANKS * FB, FB)
            for half in range(2):
                rows = pl.ds(base + half * 256, 256)
                found.append(
                    pltpu.make_async_copy(
                        ref.at[layer, rows],
                        buffer.at[m, i, pl.ds(half * 256, 256)],
                        sems.at[m, i, half],
                    )
                )
    return found


WEIGHT_SCRATCH = (
    pltpu.VMEM((2, BANKS, FB, FB), F32),
    pltpu.SemaphoreType.DMA((2, BANKS, 2)),
)


def forward_kernel(layer, meta, x0, x1, x2, x3, weight_t, weight_g, bias_t, bias_g, *rest):
    last = layer == 1
    *rest, buffer, sems = rest
    if last:
        grad, hidden, out_t, out_g, out_r, keep, stack = rest
    else:
        hidden, out_t, out_g, out_r, stack = rest
    copies = weight_copies(layer, 0, meta, (weight_t, weight_g), buffer, sems)
    for copy in copies:
        copy.start()
    acc = [jnp.zeros((TOK, FB), F32), jnp.zeros((TOK, FB), F32)]
    for i, ref in enumerate((x0, x1, x2, x3)):
        value = ref[...]
        stack[i * TOK : (i + 1) * TOK] = value
        both = jnp.concatenate(split(value), axis=0)
        for m in range(2):
            for copy in copies[i * 4 + m * 2 : i * 4 + m * 2 + 2]:
                copy.wait()
            high, low = split(buffer[m, i])
            found = dot(both, high)
            acc[m] += found[0:TOK] + found[TOK:] + dot(both[0:TOK], low)
    pre_t = acc[0] + bias_t[layer : layer + 1]
    gate = sigmoid(acc[1] + bias_g[layer : layer + 1])
    sigma = sigmoid(pre_t)
    own = x0[...]
    silu = pre_t * sigma
    hidden[...] = gate * silu + (1.0 - gate) * own
    slope_t = gate * sigma * (1.0 + pre_t * (1.0 - sigma))
    slope_g = (silu - own) * gate * (1.0 - gate)
    if last:
        grad_t = grad[...] * slope_t
        grad_g = grad[...] * slope_g
        out_t[...] = grad_t
        out_g[...] = grad_g
        out_r[...] = grad[...] * (1.0 - gate)
        first = meta[1] == 0
        keep[...] = jnp.where(first, grad_t, grad_g)
        stack[BANKS * TOK :] = jnp.where(first, grad_g, grad_t)
    else:
        out_t[...] = slope_t
        out_g[...] = slope_g
        out_r[...] = 1.0 - gate


def highway_forward(layer, meta, blocks, weight_t, weight_g, bias_t, bias_g, after, grad=()):
    last = layer == 1
    outs = [shape(TOK, FB)] * (4 + last) + [shape((BANKS + last) * TOK, FB)]
    return run(
        functools.partial(forward_kernel, layer),
        "highway_forward",
        outs,
        meta,
        (*blocks, weight_t, weight_g, bias_t, bias_g, *grad),
        WEIGHT_SCRATCH,
        after,
        [VMEM()] * 4 + [ANY()] * 2 + [VMEM()] * (2 + last),
    )


def slopes_kernel(
    meta, count, r0, r1, r2, r3, residual, slope_t, slope_g, slope_r, out_t, out_g, out_r, keep, send
):
    grad = r0[...] + r1[...] + r2[...] + r3[...] + residual[...]
    grad_t = grad * slope_t[...]
    grad_g = grad * slope_g[...]
    first = meta[1] == 0
    out_t[...] = grad_t
    out_g[...] = grad_g
    out_r[...] = grad * slope_r[...]
    keep[...] = jnp.where(first, grad_t, grad_g)
    send[0:TOK] = jnp.where(first, grad_g, grad_t)
    send[TOK:] = jnp.full((8, FB), count[0].astype(F32))


def backward_kernel(layer, meta, grad_t, grad_g, *rest):
    *rest, bias, buffer, sems = rest
    encoded = rest.pop(0) if layer == 0 else None
    weight_t, weight_g, *outs = rest
    copies = weight_copies(layer, 1, meta, (weight_t, weight_g), buffer, sems)
    for copy in copies:
        copy.start()
    left = [jnp.concatenate(split(ref[...]), axis=0) for ref in (grad_t, grad_g)]
    sums = [jnp.sum(ref[...], axis=0, keepdims=True) for ref in (grad_t, grad_g)]
    row = lax.broadcasted_iota(jnp.int32, (8, FB), 0)
    bias[...] = jnp.where(row == 0, sums[0], jnp.where(row == 1, sums[1], 0.0))
    for i in range(BANKS):
        total = jnp.zeros((TOK, FB), F32)
        for m in range(2):
            for copy in copies[i * 4 + m * 2 : i * 4 + m * 2 + 2]:
                copy.wait()
            high, low = split(buffer[m, i])
            both = dot(left[m], high, ((1,), (1,)))
            total += both[0:TOK] + both[TOK:] + dot(left[m][0:TOK], low, ((1,), (1,)))
        outs[i][0:TOK] = total
        if layer == 0:
            j = BANKS - 1 - i
            outs[i][TOK:] = encoded[j * 32 : (j + 1) * 32]


def highway_backward(layer, meta, grad_t, grad_g, weight_t, weight_g, after, encoded=()):
    parts = [shape(TOK + 32 * len(encoded), FB)] * BANKS
    return run(
        functools.partial(backward_kernel, layer),
        "highway_backward",
        parts + [shape(8, FB)],
        meta,
        (grad_t, grad_g, *encoded, weight_t, weight_g),
        WEIGHT_SCRATCH,
        after,
        [VMEM()] * (2 + len(encoded)) + [ANY()] * 2,
    )


def pack_kernel(meta, mine, theirs, out, stage, sems_in, sems_out):
    copies, done = [], []
    for k in range(RING):
        spot = (k + BANKS - meta[0]) % BANKS
        rows = pl.ds(pl.multiple_of(spot * TOK, TOK), TOK)
        for c, ref in enumerate((mine, theirs)):
            copies.append(
                pltpu.make_async_copy(
                    ref.at[rows], stage.at[k, pl.ds(c * TOK, TOK)], sems_in.at[k, c]
                )
            )
            copies[-1].start()
    for k in range(RING):
        copies[2 * k].wait()
        copies[2 * k + 1].wait()
        done.append(pltpu.make_async_copy(stage.at[k], out.at[k], sems_out.at[k]))
        done[-1].start()
    for copy in done:
        copy.wait()


def pack(meta, mine, theirs, after):
    return run(
        pack_kernel,
        "pack",
        [shape(RING, 2 * TOK, FB)],
        meta,
        (mine, theirs),
        (
            pltpu.VMEM((RING, 2 * TOK, FB), F32),
            pltpu.SemaphoreType.DMA((RING, 2)),
            pltpu.SemaphoreType.DMA((RING,)),
        ),
        after,
        specs=[ANY()] * 2,
        out_specs=[ANY()],
    )


def local_grad_kernel(meta, mine, theirs, keep, out, stage, sems):
    high, low = split(jnp.concatenate([keep[...], theirs[BANKS * TOK :]], axis=0))
    copies = []
    for i in range(BANKS):
        rows = slice(i * TOK, (i + 1) * TOK)
        hidden = jnp.concatenate([mine[rows], theirs[rows]], axis=0).T
        left_high, left_low = split(hidden)
        stage[i] = dot(left_high, high) + dot(left_low, high) + dot(left_high, low)
        position = (meta[0] + i) % BANKS
        copies.append(pltpu.make_async_copy(stage.at[i], out.at[position], sems.at[i]))
        copies[-1].start()
    for copy in copies:
        copy.wait()


def turn_hidden_kernel(meta, hidden, high, low):
    for k in range(RING):
        block = hidden[(meta[2] + RING - k) % RING].T
        lanes = slice(k * 2 * TOK, (k + 1) * 2 * TOK)
        high[:, lanes], low[:, lanes] = split(block)


CHIP = 2 * TOK + 64 + 8


def pack_grads_kernel(meta, count, keep, theirs, keep_p, theirs_p, *outs):
    for k, out in enumerate(outs):
        out[0:TOK] = keep[...]
        out[TOK : 2 * TOK] = theirs[0:TOK]
        rows = pl.ds(pl.multiple_of((meta[2] + k) % RING * 64, 64), 64)
        out[2 * TOK : 2 * TOK + 64] = keep_p[rows, :] + theirs_p[rows, :]
        out[2 * TOK + 64 :] = theirs[TOK:] + count[0].astype(F32)


def ring_grad_kernel(meta, high, low, *refs):
    full, total = refs[-2:]
    outs = refs[-2 - RING : -2]
    ins = refs[:RING]
    right = [split(ref[0 : 2 * TOK]) for ref in ins]
    right_high = jnp.concatenate([r[0] for r in right], axis=0)
    right_low = jnp.concatenate([r[1] for r in right], axis=0)
    full[...] = dot(high[...], right_high) + dot(low[...], right_high) + dot(high[...], right_low)
    total[...] = sum(ref[2 * TOK :] for ref in ins)
    for k, out in enumerate(outs):
        spot = (meta[3] + k) % RING
        out[0:128] = full[pl.ds(pl.multiple_of(spot * 128, 128), 128), :]
        out[128:144] = total[pl.ds(pl.multiple_of(spot * 16, 16), 16), :]
        out[144:] = total[64:]


def collect_ring_kernel(meta, r0, r1, r2, r3, table, out, factor, *crossing):
    total = r0[...] + r1[...] + r2[...] + r3[...]
    scale = lax.rsqrt(total[144:145, :])
    out[...] = total[0:128] * scale
    for k, ref in enumerate(crossing):
        j = (BANKS - k) % BANKS
        ref[0:EMB] = total[128:144, j * 128 : (j + 1) * 128] * scale[:, 0:128]
        ref[EMB:] = table[...] * scale[:, 0:128]
    factor[...] = jnp.broadcast_to(scale, (8, FB))


def collect_kernel(meta, keep, theirs, x0, x1, x2, x3, factor, out):
    scale = factor[0:1, :]
    for j, ref in enumerate((x0, x1, x2, x3)):
        out[0:16, j * 128 : (j + 1) * 128] = ref[0:EMB]
    out[16:80] = (keep[...] + theirs[...]) * scale
    table = x0[EMB:] + x1[EMB:] + x2[EMB:] + x3[EMB:]
    blocks = [table[i * EMB : (i + 1) * EMB] for i in range(3)] + [jnp.zeros((EMB, 128), F32)]
    out[80:] = jnp.concatenate(blocks, axis=1)


def merge_kernel(meta, *refs):
    *parts, low, high = refs
    small = parts[RING:]
    for i in range(RING):
        out, spot = (low, i) if i < 2 else (high, i - 2)
        out[spot * 144 : spot * 144 + 128] = parts[i][...]
        out[spot * 144 + 128 : (spot + 1) * 144] = small[i][0:16]
    high[288:] = sum(ref[16:] for ref in small)


def place_last_kernel(given, meta, gathered, factor, *refs):
    out_t, out_g, stage, loads, puts = refs[given:]
    copies = [
        pltpu.make_async_copy(
            gathered.at[pl.ds(i * 2, 2)], stage.at[pl.ds(i * 2, 2)], loads.at[i]
        )
        for i in range(RING * RING)
    ]
    for copy in copies:
        copy.start()
    scale = factor[0:1, :]
    done = []
    for i, copy in enumerate(copies):
        copy.wait()
        for core, out in enumerate((out_t, out_g)):
            stage[i * 2 + core] = stage[i * 2 + core] * scale
            row = i if core == 0 else i % RING * RING + i // RING
            done.append(
                pltpu.make_async_copy(
                    stage.at[i * 2 + core], out.at[1, pl.ds(row * 128, 128)], puts.at[i * 2 + core]
                )
            )
            done[-1].start()
    for copy in done:
        copy.wait()


def place_last(meta, gathered, factor, outs, after):
    return run(
        functools.partial(place_last_kernel, len(outs)),
        "place",
        [shape(2, 2048, FB)] * 2,
        meta,
        (gathered, factor, *outs),
        (
            pltpu.VMEM((32, 128, FB), F32),
            pltpu.SemaphoreType.DMA((16,)),
            pltpu.SemaphoreType.DMA((32,)),
        ),
        after,
        [ANY(), VMEM()] + [ANY()] * len(outs),
        [ANY()] * 2,
        {3 + i: i for i in range(len(outs))},
    )


ROWS0 = 144


def place_kernel(sources, given, ending, meta, *refs):
    count = len(sources)
    mine, theirs = refs[:count], refs[count : 2 * count]
    ends = refs[2 * count : 2 * count + 2 * RING * ending]
    refs = refs[2 * count + 2 * RING * ending + given :]
    outs, small, refs = refs[:3], refs[3 : 3 + 6 * ending], refs[3 + 6 * ending :]
    stages, loads, sems = refs[:count], refs[count], refs[count + 1]
    if ending:
        end_stage, end_sems = refs[count + 2 :]
        copies = [
            pltpu.make_async_copy(ref.at[pl.ds(288, 80)], end_stage.at[i], end_sems.at[i])
            for i, ref in enumerate(ends)
        ]
        for copy in copies:
            copy.start()

    def load(i, core):
        ref = (mine, theirs)[core][i]
        many = len(sources[i][1]) * ROWS0
        return pltpu.make_async_copy(ref.at[pl.ds(0, many)], stages[i].at[core], loads.at[i, core])

    for i in range(count):
        for core in range(2):
            load(i, core).start()
    puts = []
    for i, (j, blocks) in enumerate(sources):
        for core in range(2):
            load(i, core).wait()
        for stream in range(2):
            holder = jnp.where(meta[1] == stream, 0, 1)
            major, minor = (meta[4], meta[5]) if stream == 0 else (meta[5], meta[4])
            first = (major + RING - j) % RING
            for spot, k in enumerate(blocks):
                second = (minor + RING - k) % RING
                base = pl.multiple_of((first * RING + second) * 128, 128)
                found = [
                    (
                        stages[i].at[holder, pl.ds(spot * ROWS0, 128)],
                        outs[stream].at[0, pl.ds(base, 128)],
                    )
                ]
                for q in range(BANKS):
                    bank = (meta[0] + BANKS - q) % BANKS
                    base = pl.multiple_of(bank * FB + stream * 256 + first * 64 + second * 16, 16)
                    found.append(
                        (
                            stages[i].at[holder, pl.ds(spot * ROWS0 + 128, 16), pl.ds(q * 128, 128)],
                            outs[2].at[pl.ds(base, 16)],
                        )
                    )
                for a, b in found:
                    puts.append(pltpu.make_async_copy(a, b, sems.at[len(puts)]))
                    puts[-1].start()
    if ending:
        for copy in copies:
            copy.wait()
        finish(meta, end_stage, small)
    for copy in puts:
        copy.wait()


def finish(meta, stage, outs):
    kernel, cbias, bt, bg, pb, table = outs
    own = sum(stage[i] for i in range(RING))
    other = sum(stage[i] for i in range(RING, 2 * RING))
    first = meta[1] == 0
    low = jnp.where(first, own, other)
    high = jnp.where(first, other, own)
    flat = jnp.concatenate([low[0:64], high[0:64]], axis=0)
    kernel[...] = flat[:ROWS]
    cbias[...] = flat[ROWS : ROWS + 1]
    row = ROWS + 1
    bt[...] = jnp.concatenate([flat[row : row + 1], flat[row + 2 : row + 3]], axis=0)
    bg[...] = jnp.concatenate([flat[row + 1 : row + 2], flat[row + 3 : row + 4]], axis=0)
    pb[...] = flat[row + 4 : row + 5, 0:128]
    table[...] = (own[64:] + other[64:])[:, 0:262]


def place(sources, meta, mine, theirs, outs, after, ends=None):
    total = sum(len(blocks) for _, blocks in sources) * 2 * 5
    ending = ends is not None
    inputs = [*mine, *theirs] + ([*ends[0], *ends[1]] if ending else [])
    start = 1 + len(inputs)
    shapes = [shape(2, 2048, FB)] * 2 + [shape(2048, 128)]
    if ending:
        shapes += [
            shape(ROWS, FB), shape(1, FB), shape(2, FB), shape(2, FB), shape(1, 128), shape(EMB, 262),
        ]
    return run(
        functools.partial(place_kernel, sources, len(outs), ending),
        "place",
        shapes,
        meta,
        [*inputs, *outs],
        [pltpu.VMEM((2, len(blocks) * ROWS0, FB), F32) for _, blocks in sources]
        + [
            pltpu.SemaphoreType.DMA((len(sources), 2)),
            pltpu.SemaphoreType.DMA((total,)),
        ]
        + (
            [pltpu.VMEM((2 * RING, 80, FB), F32), pltpu.SemaphoreType.DMA((2 * RING,))]
            if ending
            else []
        ),
        after,
        specs=[ANY()] * (len(inputs) + len(outs)),
        out_specs=[ANY()] * 3 + [VMEM()] * (6 * ending),
        aliases={start + i: i for i in range(len(outs))},
    )


def on_device(
    chars,
    counts,
    char_table,
    conv_weight,
    conv_bias,
    transform_weight,
    transform_bias,
    gate_weight,
    gate_bias,
    proj_weight,
    proj_bias,
    cotangent,
):
    here = lax.axis_index("dp")
    bank = lax.axis_index("bank")
    z, y, core = here // (2 * RING), here // 2 % RING, here % 2
    first = jnp.where(core == 0, z, y)
    second = jnp.where(core == 0, y, z)
    meta = jnp.stack([bank, core, first, second, z, y]).astype(jnp.int32)

    early = early_pack(meta, cotangent, proj_weight)
    early_received = lax.all_to_all(early, "bank", 0, 0, tiled=True)
    pooled, summed, lifted, emb_high, emb_low = conv_forward(
        meta, chars.T, char_table.T, conv_weight, conv_bias[None], [early]
    )

    def gather(block):
        others = {i: along_bank(block, -i) for i in (2, 1, 3)}
        return [block, others[1], others[2], others[3]]

    def bank_pieces(parts):
        return [parts[3]] + [along_bank(parts[i - 1], i) for i in (2, 1, 3)]

    def ring_gather(value, mover):
        moved = {k: mover(value, k) for k in (2, 1, 3)}
        return [value, moved[1], moved[2], moved[3]]

    def ring_pieces(pieces, mover):
        moved = {k: mover(pieces[k], k) for k in (2, 1, 3)}
        return [pieces[0], moved[1], moved[2], moved[3]]

    weights = (transform_weight, gate_weight, transform_bias, gate_bias)
    blocks0 = gather(pooled)
    rows, cots = run(
        early_rows_kernel,
        "early_rows",
        [shape(3, 256, 128), shape(3, TOK, 128)],
        meta,
        (early_received,),
        after=[pooled],
    )
    banks = (cotangent, cots, rows, to_partner(rows))
    hidden1, slope_t, slope_g, slope_r, stack0 = highway_forward(
        0, meta, blocks0, *weights, [rows]
    )
    blocks1 = gather(hidden1)
    (grad_last,) = with_bank_rows(
        grad_hidden_kernel, "grad_hidden", [shape(TOK, FB)], meta, counts, banks, proj_weight, hidden1
    )
    (packed0,) = pack(meta, stack0, to_partner(stack0), [grad_last])
    hidden_0 = lax.all_to_all(packed0, "dp", 0, 0, axis_index_groups=FIRST_RINGS, tiled=True)
    hidden2, grad_t1, grad_g1, res1, keep1, stack1 = highway_forward(
        1, meta, blocks1, *weights, [packed0], [grad_last]
    )

    *parts1, bias1 = highway_backward(
        1, meta, grad_t1, grad_g1, transform_weight, gate_weight, []
    )
    received1 = bank_pieces(parts1)
    (hidden_0,) = gate(meta, [hidden_0], [bias1])
    (local1,) = run(
        local_grad_kernel,
        "local_grad",
        [shape(RING, FB, FB)],
        meta,
        (stack1, to_partner(stack1), keep1),
        (pltpu.VMEM((BANKS, FB, FB), F32), pltpu.SemaphoreType.DMA((BANKS,))),
        [hidden_0],
        out_specs=[ANY()],
    )
    ring1 = lax.psum_scatter(local1, "dp", axis_index_groups=FIRST_RINGS)
    keep_p, send_p, encoded_parts, bias_p = with_bank_rows(
        projection_kernel,
        "projection",
        [shape(256, FB), shape(256, FB), shape(128, FB), shape(8, 128)],
        meta,
        counts,
        (hidden2, *banks),
        proj_weight,
        local1,
    )
    theirs_p = to_partner(send_p)
    turned = run(
        turn_hidden_kernel,
        "turn_hidden",
        [shape(FB, 8 * TOK, dtype=BF16)] * 2,
        meta,
        (hidden_0,),
        after=[keep_p],
    )
    grad_t0, grad_g0, res0, keep0, send0 = run(
        slopes_kernel,
        "slopes",
        [shape(TOK, FB)] * 4 + [shape(TOK + 8, FB)],
        meta,
        (counts, *received1, res1, slope_t, slope_g, slope_r),
        after=[turned[0]],
        specs=[SMEM()] + [VMEM()] * 8,
    )
    packed_g = run(
        pack_grads_kernel,
        "pack_grads",
        [shape(CHIP, FB)] * RING,
        meta,
        (counts, keep0, to_partner(send0), keep_p, theirs_p),
        specs=[SMEM()] + [VMEM()] * 4,
    )
    grads_0 = ring_pieces(packed_g, along_first)
    *parts0, bias0 = highway_backward(
        0, meta, grad_t0, grad_g0, transform_weight, gate_weight, [packed_g[0]], [encoded_parts]
    )
    received0 = bank_pieces(parts0)
    (ring1,) = gate(meta, [ring1], [bias0, grads_0[1], grads_0[3]])
    own1 = lax.psum_scatter(ring1, "dp", axis_index_groups=SECOND_RINGS, tiled=True)
    pieces0 = run(
        ring_grad_kernel,
        "ring_grad",
        [shape(152, FB)] * RING,
        meta,
        (*turned, *grads_0),
        [pltpu.VMEM((FB, FB), F32), pltpu.VMEM((72, FB), F32)],
        [ring1],
    )
    second0 = ring_pieces(pieces0, along_second)
    coef, encoded = run(
        bank_sum_kernel,
        "bank_sum",
        [shape(FB, TOK), shape(TOK, 128)],
        meta,
        (counts, *received0, res0, summed, proj_bias[None]),
        after=[pieces0[0]],
        specs=[SMEM()] + [VMEM()] * 7,
    )
    (own1,) = gate(meta, [own1], [coef])
    gathered1 = lax.all_gather(own1, "dp")
    keep_s, send_s, table = conv_backward(
        meta,
        (coef, lifted, emb_high, emb_low),
        conv_weight,
        chars,
        (bias0, bias1, bias_p),
        [own1],
    )
    own0, factor, *crossing = run(
        collect_ring_kernel,
        "collect_ring",
        [shape(128, FB), shape(8, FB)] + [shape(64, 128)] * BANKS,
        meta,
        (*second0, table),
    )

    own_parts = ring_gather(own0, along_second)
    (small,) = run(
        collect_kernel,
        "collect",
        [shape(96, FB)],
        meta,
        (
            keep_s,
            to_partner(send_s),
            crossing[0],
            *[along_bank(crossing[k], k) for k in range(1, BANKS)],
            factor,
        ),
        after=[own_parts[1], own_parts[3]],
    )
    low, high = run(
        merge_kernel,
        "merge",
        [shape(288, FB), shape(368, FB)],
        meta,
        (*own_parts, *ring_gather(small, along_second)),
    )
    near = [along_first(low, 1), along_first(high, 1)]
    back = [along_first(low, 3), along_first(high, 3)]
    mine = [low, high]
    theirs = [to_partner(v) for v in mine]
    sources = tuple((j, half) for j in (0, 1, 3, 2) for half in ((0, 1), (2, 3)))
    outs = place_last(meta, gathered1, factor, [], [low])
    outs = list(place(sources[0:2], meta, mine[0:2], theirs[0:2], outs, []))
    mine += gate(meta, [*near, *back], [outs[2]])
    far = [along_first(mine[2], 1), along_first(mine[5], 3)]
    theirs += [to_partner(v) for v in mine[2:]]
    outs = place(sources[2:6], meta, mine[2:6], theirs[2:6], outs, [])
    far = gate(meta, far, [outs[2]])
    mine += far
    theirs += [to_partner(v) for v in far]
    spots = (1, 3, 5, 7)
    sum_wt, sum_wg, sum_pw, sum_kernel, sum_cbias, sum_bt, sum_bg, sum_pb, sum_table = place(
        sources[6:8],
        meta,
        mine[6:8],
        theirs[6:8],
        outs,
        [],
        ([mine[i] for i in spots], [theirs[i] for i in spots]),
    )
    return (
        encoded,
        sum_table.T,
        sum_kernel,
        sum_cbias[0],
        sum_wt,
        sum_bt,
        sum_wg,
        sum_bg,
        sum_pw,
        sum_pb[0],
    )


def solution(mesh):
    return jax.shard_map(
        on_device,
        mesh=mesh,
        in_specs=(
            P("dp", None),
            P("dp"),
            P(),
            P(None, "bank"),
            P("bank"),
            P(None, None, "bank"),
            P(None, "bank"),
            P(None, None, "bank"),
            P(None, "bank"),
            P(None, "bank"),
            P("bank"),
            P("dp", "bank"),
        ),
        out_specs=(
            P("dp", "bank"),
            P(),
            P(None, "bank"),
            P("bank"),
            P(None, None, "bank"),
            P(None, "bank"),
            P(None, None, "bank"),
            P(None, "bank"),
            P(None, "bank"),
            P("bank"),
        ),
        check_vma=False,
    )
```

```python
import functools

import jax
import jax.numpy as jnp
from jax import lax
from jax.experimental import pallas as pl
from jax.experimental.pallas import tpu as pltpu
from jax.sharding import PartitionSpec as P

F32 = jnp.float32
BF16 = jnp.bfloat16
LOG2E = 1.4426950408889634
MIB = 2**20

TOK = 128
CH = 50
CHP = 56
FB = 512
TAPS = 7
EMB = 16
ROWS = TAPS * EMB
BANKS = 4
RING = 4
STEP = 10

VMEM_LIMIT = 64 * MIB - 64 * 1024

VMEM = functools.partial(pl.BlockSpec, memory_space=pltpu.VMEM)
ANY = functools.partial(pl.BlockSpec, memory_space=pl.ANY)
SMEM = functools.partial(pl.BlockSpec, memory_space=pltpu.SMEM)


PARAMS = pltpu.CompilerParams(vmem_limit_bytes=VMEM_LIMIT)


def shape(*dims, dtype=F32):
    return jax.ShapeDtypeStruct(dims, dtype)


def run(kernel, name, outs, meta, inputs, scratch=(), after=(), specs=None, out_specs=None, aliases=None):
    inputs, after = list(inputs), list(after)
    count = 1 + len(inputs)

    def body(*refs):
        kernel(*refs[:count], *refs[count + len(after) :])

    return pl.pallas_call(
        body,
        out_shape=outs,
        in_specs=[SMEM()] + list(specs or [VMEM()] * len(inputs)) + [ANY()] * len(after),
        out_specs=list(out_specs or [VMEM()] * len(outs)),
        scratch_shapes=list(scratch),
        input_output_aliases=aliases or {},
        compiler_params=PARAMS,
        name=name,
    )(meta, *inputs, *after)


def gate_kernel(meta, *refs):
    pass


def gate(meta, values, after):
    values = list(values)
    return run(
        gate_kernel,
        "gate",
        [jax.ShapeDtypeStruct(v.shape, v.dtype) for v in values],
        meta,
        values,
        after=after,
        specs=[ANY()] * len(values),
        out_specs=[ANY()] * len(values),
        aliases={1 + i: i for i in range(len(values))},
    )


def along_bank(value, shift):
    return lax.ppermute(value, "bank", [(i, (i + shift) % BANKS) for i in range(BANKS)])


def place_of(z, y, core):
    return (z * RING + y) * 2 + core


def to_partner(value):
    return lax.ppermute(value, "dp", [(i, i ^ 1) for i in range(2 * RING * RING)])


def ring_perm(shift, z_core):
    perm = []
    for z in range(RING):
        for y in range(RING):
            for core in range(2):
                if core == z_core:
                    to = place_of((z + shift) % RING, y, core)
                else:
                    to = place_of(z, (y + shift) % RING, core)
                perm.append((place_of(z, y, core), to))
    return perm


FIRST_RINGS = [[place_of(z, y, 0) for z in range(RING)] for y in range(RING)] + [
    [place_of(z, y, 1) for y in range(RING)] for z in range(RING)
]
SECOND_RINGS = [[place_of(z, y, 0) for y in range(RING)] for z in range(RING)] + [
    [place_of(z, y, 1) for z in range(RING)] for y in range(RING)
]


def along_first(value, shift):
    return lax.ppermute(value, "dp", ring_perm(shift, 0))


def along_second(value, shift):
    return lax.ppermute(value, "dp", ring_perm(shift, 1))


def split(value):
    high = value.astype(BF16)
    low = (value - high.astype(F32)).astype(BF16)
    return high, low


def dot(left, right, dims=((1,), (0,))):
    return lax.dot_general(left, right, (dims, ((), ())), preferred_element_type=F32)


def dot3(left, right, dims=((1,), (0,))):
    lh, ll = split(left)
    rh, rl = split(right)
    return dot(lh, rh, dims) + dot(ll, rh, dims) + dot(lh, rl, dims)


def widths_of(column):
    width = jnp.ones_like(column)
    for power in range(6):
        width = width + (column >= 32 * 2**power).astype(jnp.int32)
    return width


def conv_forward_kernel(
    meta, chars, table, weight, bias, pooled, summed, lifted_out, emb_high, emb_low, wide, wide_table, lifted, sems
):
    start = meta[0] * FB
    column = start + lax.broadcasted_iota(jnp.int32, (ROWS, FB), 1)
    tap = lax.broadcasted_iota(jnp.int32, (ROWS, FB), 0) // EMB
    kernel = jnp.where(tap < widths_of(column), weight[...], 0.0) * LOG2E
    high = kernel.astype(BF16).astype(F32)
    shift = bias[...] * LOG2E
    shift_high = shift.astype(BF16).astype(F32)
    row = lax.broadcasted_iota(jnp.int32, (EMB, FB), 0)
    shifts = jnp.where(row == 0, shift_high, jnp.where(row == 1, shift - shift_high, 0.0))
    rows = [high, kernel - high, shifts, jnp.zeros((EMB, FB), F32)]
    wide[...] = jnp.concatenate(rows, axis=0).T.astype(BF16)
    wide_table[:, 0 : table.shape[1]] = table[...]
    parts = [wide_table[:, 128 * i : 128 * (i + 1)] for i in range(3)]
    for p in range(CH):
        ids = jnp.broadcast_to(chars[p : p + 1, :], (EMB, TOK))
        lane = ids & 127
        part = ids >> 7
        found = [
            jnp.take_along_axis(t, lane, axis=1, mode="promise_in_bounds") for t in parts
        ]
        value = jnp.where(part == 0, found[0], jnp.where(part == 1, found[1], found[2]))
        high, low = split(value)
        emb_high[p * EMB : (p + 1) * EMB, :] = high
        emb_low[p * EMB : (p + 1) * EMB, :] = low
    zeros = jnp.zeros(((CHP - CH) * EMB, TOK), BF16)
    emb_high[CH * EMB :, :] = zeros
    emb_low[CH * EMB :, :] = zeros
    one_row = lax.broadcasted_iota(jnp.int32, (EMB, 2 * TOK), 0)
    ones = jnp.where(one_row < 2, 1.0, 0.0).astype(BF16)
    width = widths_of(start + lax.broadcasted_iota(jnp.int32, (FB, TOK), 0))

    def window(ref, pair):
        base = pair * 2 * EMB
        return jnp.concatenate(
            [ref[base : base + ROWS, :], ref[base + EMB : base + EMB + ROWS, :]], axis=1
        )

    for pair in range(CH // 2):
        high = window(emb_high, pair)
        low = window(emb_low, pair)
        pre = dot(wide[:, : 2 * ROWS + EMB], jnp.concatenate([high, high, ones], axis=0))
        pre += dot(wide[:, :ROWS], low)
        both = jnp.exp2(pre)
        first, second = both[:, :TOK], both[:, TOK:]
        if 2 * pair + 1 > CH - TAPS:
            first = jnp.where(width <= CH - 2 * pair, first, 0.0)
            second = jnp.where(width <= CH - 2 * pair - 1, second, 0.0)
        lifted[2 * pair] = first
        lifted[2 * pair + 1] = second
        pltpu.make_async_copy(
            lifted.at[pl.ds(2 * pair, 2)], lifted_out.at[pl.ds(2 * pair, 2)], sems.at[pair]
        ).start()
        if pair:
            summed[...] += first + second
        else:
            summed[...] = first + second
    valid = (CH + 1 - width).astype(F32)
    total = summed[...] + valid
    summed[...] = total
    pooled[...] = jnp.log(total / valid).T
    for pair in range(CH // 2):
        pltpu.make_async_copy(
            lifted.at[pl.ds(2 * pair, 2)], lifted_out.at[pl.ds(2 * pair, 2)], sems.at[pair]
        ).wait()


def conv_forward(meta, chars_t, table_t, weight, bias, after):
    return run(
        conv_forward_kernel,
        "conv_forward",
        (
            shape(TOK, FB),
            shape(FB, TOK),
            shape(CH, FB, TOK),
            shape(CHP * EMB, TOK, dtype=BF16),
            shape(CHP * EMB, TOK, dtype=BF16),
        ),
        meta,
        (chars_t, table_t, weight, bias),
        (
            pltpu.VMEM((FB, 2 * ROWS + 2 * EMB), BF16),
            pltpu.VMEM((EMB, 384), F32),
            pltpu.VMEM((CH, FB, TOK), F32),
            pltpu.SemaphoreType.DMA((CH // 2,)),
        ),
        after,
        out_specs=[VMEM(), VMEM(), ANY(), VMEM(), VMEM()],
    )


def bank_sum_kernel(meta, count, r0, r1, r2, r3, residual, summed, proj_bias, passed, coef, encoded, same):
    total = r0[...] + r1[...] + r2[...] + r3[...]
    coef[...] = (total[0:TOK] + residual[...]).T / summed[...]
    value = jnp.concatenate([total[TOK:, q * 128 : (q + 1) * 128] for q in range(4)], axis=0)
    live = live_rows(count[0], 128)
    encoded[...] = jnp.where(live, value + proj_bias[...], 0.0)


def conv_backward_kernel(
    meta, coef, lifted, emb_high, emb_low, weight, chars, bias0, bias1, bias_p, keep, send, table,
    kernel, grads, windows, acc, grad_emb, buffer, sems,
):
    start = meta[0] * FB
    copies = [
        pltpu.make_async_copy(
            lifted.at[pl.ds(i * 2, 2)], buffer.at[pl.ds(i * 2, 2)], sems.at[i]
        )
        for i in range(CH // 2)
    ]
    for copy in copies:
        copy.start()
    column = start + lax.broadcasted_iota(jnp.int32, (ROWS, FB), 1)
    tap = lax.broadcasted_iota(jnp.int32, (ROWS, FB), 0) // EMB
    high, low = split(jnp.where(tap < widths_of(column), weight[...], 0.0))
    kernel[0:ROWS] = high
    kernel[ROWS:] = low
    grad_emb[...] = jnp.zeros_like(grad_emb)
    row = lax.broadcasted_iota(jnp.int32, (EMB, STEP * TOK), 0)
    ones = jnp.where(row < 1, 1.0, 0.0).astype(BF16)
    for slot in range(2):
        windows[slot, 2 * ROWS :, :] = ones

    for step in range(CH // STEP):
        slot = step % 2
        for j in range(STEP):
            p = step * STEP + j
            if p % 2 == 0:
                copies[p // 2].wait()
            high, low = split(coef[...] * buffer[p])
            lanes = slice(j * TOK, (j + 1) * TOK)
            grads[slot, 0:FB, lanes] = high
            grads[slot, FB:, lanes] = low
            windows[slot, 0:ROWS, lanes] = emb_high[p * EMB : p * EMB + ROWS, :]
            windows[slot, ROWS : 2 * ROWS, lanes] = emb_low[p * EMB : p * EMB + ROWS, :]
        part = dot(grads[slot], windows[slot], ((1,), (1,)))
        if step:
            acc[...] += part
        else:
            acc[...] = part
        from_high = dot(kernel[...], grads[slot, 0:FB, :])
        from_low = dot(kernel[0:ROWS, :], grads[slot, FB:, :])
        grad_windows = from_high[0:ROWS] + from_high[ROWS:] + from_low
        for j in range(STEP):
            base = (step * STEP + j) * EMB
            grad_emb[base : base + ROWS, :] += grad_windows[:, j * TOK : (j + 1) * TOK]

    total = acc[...]
    grad_kernel = total[0:FB, 0:ROWS] + total[0:FB, ROWS : 2 * ROWS] + total[FB:, 0:ROWS]
    grad_bias = total[0:FB, 2 * ROWS :] + total[FB:, 2 * ROWS :]
    full = jnp.concatenate([grad_kernel, grad_bias], axis=1).T
    column = start + lax.broadcasted_iota(jnp.int32, (ROWS + EMB, FB), 1)
    row = lax.broadcasted_iota(jnp.int32, (ROWS + EMB, FB), 0)
    full = jnp.where((row > ROWS) | (row // EMB >= widths_of(column)) & (row < ROWS), 0.0, full)
    more = jnp.concatenate(
        [
            bias0[0:2],
            bias1[0:2],
            jnp.concatenate([bias_p[0:1], jnp.zeros((1, FB - 128), F32)], axis=1),
            jnp.zeros((10, FB), F32),
        ],
        axis=0,
    )
    full = jnp.concatenate([full[: ROWS + 1], more], axis=0)
    first_core = meta[1] == 0
    keep[...] = jnp.where(first_core, full[:64], full[64:])
    send[...] = jnp.where(first_core, full[64:], full[:64])
    found = jnp.zeros((2 * EMB, 384), F32)
    vocab = lax.broadcasted_iota(jnp.int32, (TOK, 384), 1).astype(F32)
    ids = jnp.concatenate([chars[...].astype(F32), jnp.zeros((CHP - CH, TOK), F32)], axis=0).T
    for begin in range(0, CH, STEP):
        left, right = [], []
        for q in range(begin, begin + STEP):
            high, low = split(grad_emb[q * EMB : (q + 1) * EMB, :])
            left.append(jnp.concatenate([high, low], axis=0))
            right.append(jnp.where(ids[:, q : q + 1] == vocab, 1.0, 0.0).astype(BF16))
        found += dot(jnp.concatenate(left, axis=1), jnp.concatenate(right, axis=0))
    found = found[0:EMB] + found[EMB:]
    for i in range(3):
        table[i * EMB : (i + 1) * EMB] = found[:, i * 128 : (i + 1) * 128]


def conv_backward(meta, inputs, weight, chars, biases, after):
    return run(
        conv_backward_kernel,
        "conv_backward",
        [shape(64, FB), shape(64, FB), shape(48, 128)],
        meta,
        (*inputs, weight, chars, *biases),
        (
            pltpu.VMEM((2 * ROWS, FB), BF16),
            pltpu.VMEM((2, 2 * FB, STEP * TOK), BF16),
            pltpu.VMEM((2, 2 * ROWS + EMB, STEP * TOK), BF16),
            pltpu.VMEM((2 * FB, 2 * ROWS + EMB), F32),
            pltpu.VMEM((CHP * EMB, TOK), F32),
            pltpu.VMEM((CH, FB, TOK), F32),
            pltpu.SemaphoreType.DMA((CH // 2,)),
        ),
        after,
        [VMEM(), ANY()] + [VMEM()] * 7,
    )


def live_rows(count, columns):
    return lax.broadcasted_iota(jnp.int32, (TOK, columns), 0) < count


def early_rows_kernel(meta, received, out, grads):
    for j in range(1, BANKS):
        source = (meta[0] + BANKS - j) % BANKS
        out[j - 1] = received[source, TOK:]
        grads[j - 1] = received[source, 0:TOK]


def bank_rows(meta, mine, others):
    found = []
    first = meta[1] == 0
    for i in range(BANKS - 1):
        low = jnp.where(first, mine[i], others[i])
        high = jnp.where(first, others[i], mine[i])
        found.append(jnp.concatenate([low, high], axis=0))
    return found


def grad_hidden_kernel(meta, count, cot, grads, mine, others, proj, token, out):
    live = live_rows(count[0], 128)
    total = dot3(jnp.where(live, cot[...], 0.0), proj[...], ((1,), (1,)))
    for i, rows in enumerate(bank_rows(meta, mine, others)):
        total += dot3(jnp.where(live, grads[i], 0.0), rows, ((1,), (1,)))
    out[...] = total


def with_bank_rows(kernel, name, outs, meta, count, inputs, proj, after):
    return pl.pallas_call(
        kernel,
        out_shape=outs,
        grid_spec=pltpu.PrefetchScalarGridSpec(
            num_scalar_prefetch=2,
            grid=(1,),
            in_specs=[VMEM()] * len(inputs)
            + [pl.BlockSpec((FB, 128), lambda i, meta, count: (meta[0], 0)), ANY()],
            out_specs=[VMEM()] * len(outs),
        ),
        compiler_params=PARAMS,
        name=name,
    )(meta, count, *inputs, proj, after)


def projection_kernel(meta, count, hidden, cot, cots, mine, others, proj, token, keep, send, encoded, bias):
    live = live_rows(count[0], 128)
    grads = [jnp.where(live, value, 0.0) for value in (cot[...], cots[0], cots[1], cots[2])]
    rows = [proj[...]] + bank_rows(meta, mine, others)
    value = hidden[...]
    both = jnp.concatenate(split(value), axis=0)
    turned = jnp.concatenate(split(value.T), axis=0)
    first = meta[1] == 0
    for j in range(BANKS):
        high, low = split(rows[j])
        part = dot(both, high)
        part = part[0:TOK] + part[TOK:] + dot(both[0:TOK], low)
        for q in range(4):
            encoded[j * 32 : (j + 1) * 32, q * 128 : (q + 1) * 128] = part[q * 32 : (q + 1) * 32]
        high, low = split(grads[j])
        part = dot(turned, high)
        part = part[0:FB] + part[FB:] + dot(turned[0:FB], low)
        lanes = slice(j * 128, (j + 1) * 128)
        keep[:, lanes] = jnp.where(first, part[0:256], part[256:])
        send[:, lanes] = jnp.where(first, part[256:], part[0:256])
    bias[...] = jnp.broadcast_to(jnp.sum(grads[0], axis=0, keepdims=True), (8, 128))


def early_pack_kernel(meta, cot, p1, p2, p3, out):
    for j, ref in enumerate((p1, p2, p3)):
        to = (meta[0] + 1 + j) % BANKS
        out[to, 0:TOK] = cot[...]
        out[to, TOK:] = ref[...]


def early_pack(meta, cot, proj):
    def rows(j):
        return pl.BlockSpec((256, 128), lambda i, meta: ((meta[0] + j) % BANKS * 2 + meta[1], 0))

    return pl.pallas_call(
        early_pack_kernel,
        out_shape=shape(BANKS, TOK + 256, 128),
        grid_spec=pltpu.PrefetchScalarGridSpec(
            num_scalar_prefetch=1,
            grid=(1,),
            in_specs=[VMEM()] + [rows(j) for j in range(1, BANKS)],
            out_specs=VMEM(),
        ),
        compiler_params=PARAMS,
        name="early_pack",
    )(meta, cot, proj, proj, proj)


def sigmoid(value):
    return 1.0 / (1.0 + jnp.exp(-value))


def weight_copies(layer, shift, meta, weights, buffer, sems):
    found = []
    for i in range(BANKS):
        for m, ref in enumerate(weights):
            base = pl.multiple_of((meta[0] + shift + i) % BANKS * FB, FB)
            for half in range(2):
                rows = pl.ds(base + half * 256, 256)
                found.append(
                    pltpu.make_async_copy(
                        ref.at[layer, rows],
                        buffer.at[m, i, pl.ds(half * 256, 256)],
                        sems.at[m, i, half],
                    )
                )
    return found


WEIGHT_SCRATCH = (
    pltpu.VMEM((2, BANKS, FB, FB), F32),
    pltpu.SemaphoreType.DMA((2, BANKS, 2)),
)


def forward_kernel(layer, meta, x0, x1, x2, x3, weight_t, weight_g, bias_t, bias_g, *rest):
    last = layer == 1
    *rest, buffer, sems = rest
    if last:
        grad, hidden, out_t, out_g, out_r, keep, stack = rest
    else:
        hidden, out_t, out_g, out_r, stack = rest
    copies = weight_copies(layer, 0, meta, (weight_t, weight_g), buffer, sems)
    for copy in copies:
        copy.start()
    acc = [jnp.zeros((TOK, FB), F32), jnp.zeros((TOK, FB), F32)]
    for i, ref in enumerate((x0, x1, x2, x3)):
        value = ref[...]
        stack[i * TOK : (i + 1) * TOK] = value
        both = jnp.concatenate(split(value), axis=0)
        for m in range(2):
            for copy in copies[i * 4 + m * 2 : i * 4 + m * 2 + 2]:
                copy.wait()
            high, low = split(buffer[m, i])
            found = dot(both, high)
            acc[m] += found[0:TOK] + found[TOK:] + dot(both[0:TOK], low)
    pre_t = acc[0] + bias_t[layer : layer + 1]
    gate = sigmoid(acc[1] + bias_g[layer : layer + 1])
    sigma = sigmoid(pre_t)
    own = x0[...]
    silu = pre_t * sigma
    hidden[...] = gate * silu + (1.0 - gate) * own
    slope_t = gate * sigma * (1.0 + pre_t * (1.0 - sigma))
    slope_g = (silu - own) * gate * (1.0 - gate)
    if last:
        grad_t = grad[...] * slope_t
        grad_g = grad[...] * slope_g
        out_t[...] = grad_t
        out_g[...] = grad_g
        out_r[...] = grad[...] * (1.0 - gate)
        first = meta[1] == 0
        keep[...] = jnp.where(first, grad_t, grad_g)
        stack[BANKS * TOK :] = jnp.where(first, grad_g, grad_t)
    else:
        out_t[...] = slope_t
        out_g[...] = slope_g
        out_r[...] = 1.0 - gate


def highway_forward(layer, meta, blocks, weight_t, weight_g, bias_t, bias_g, after, grad=()):
    last = layer == 1
    outs = [shape(TOK, FB)] * (4 + last) + [shape((BANKS + last) * TOK, FB)]
    return run(
        functools.partial(forward_kernel, layer),
        "highway_forward",
        outs,
        meta,
        (*blocks, weight_t, weight_g, bias_t, bias_g, *grad),
        WEIGHT_SCRATCH,
        after,
        [VMEM()] * 4 + [ANY()] * 2 + [VMEM()] * (2 + last),
    )


def slopes_kernel(
    meta, count, r0, r1, r2, r3, residual, slope_t, slope_g, slope_r, out_t, out_g, out_r, keep, send
):
    grad = r0[...] + r1[...] + r2[...] + r3[...] + residual[...]
    grad_t = grad * slope_t[...]
    grad_g = grad * slope_g[...]
    first = meta[1] == 0
    out_t[...] = grad_t
    out_g[...] = grad_g
    out_r[...] = grad * slope_r[...]
    keep[...] = jnp.where(first, grad_t, grad_g)
    send[0:TOK] = jnp.where(first, grad_g, grad_t)
    send[TOK:] = jnp.full((8, FB), count[0].astype(F32))


def backward_kernel(layer, meta, grad_t, grad_g, *rest):
    *rest, bias, buffer, sems = rest
    encoded = rest.pop(0) if layer == 0 else None
    weight_t, weight_g, *outs = rest
    copies = weight_copies(layer, 1, meta, (weight_t, weight_g), buffer, sems)
    for copy in copies:
        copy.start()
    left = [jnp.concatenate(split(ref[...]), axis=0) for ref in (grad_t, grad_g)]
    sums = [jnp.sum(ref[...], axis=0, keepdims=True) for ref in (grad_t, grad_g)]
    row = lax.broadcasted_iota(jnp.int32, (8, FB), 0)
    bias[...] = jnp.where(row == 0, sums[0], jnp.where(row == 1, sums[1], 0.0))
    for i in range(BANKS):
        total = jnp.zeros((TOK, FB), F32)
        for m in range(2):
            for copy in copies[i * 4 + m * 2 : i * 4 + m * 2 + 2]:
                copy.wait()
            high, low = split(buffer[m, i])
            both = dot(left[m], high, ((1,), (1,)))
            total += both[0:TOK] + both[TOK:] + dot(left[m][0:TOK], low, ((1,), (1,)))
        outs[i][0:TOK] = total
        if layer == 0:
            j = BANKS - 1 - i
            outs[i][TOK:] = encoded[j * 32 : (j + 1) * 32]


def highway_backward(layer, meta, grad_t, grad_g, weight_t, weight_g, after, encoded=()):
    parts = [shape(TOK + 32 * len(encoded), FB)] * BANKS
    return run(
        functools.partial(backward_kernel, layer),
        "highway_backward",
        parts + [shape(8, FB)],
        meta,
        (grad_t, grad_g, *encoded, weight_t, weight_g),
        WEIGHT_SCRATCH,
        after,
        [VMEM()] * (2 + len(encoded)) + [ANY()] * 2,
    )


def pack_kernel(meta, mine, theirs, out, stage, sems_in, sems_out):
    copies, done = [], []
    for k in range(RING):
        spot = (k + BANKS - meta[0]) % BANKS
        rows = pl.ds(pl.multiple_of(spot * TOK, TOK), TOK)
        for c, ref in enumerate((mine, theirs)):
            copies.append(
                pltpu.make_async_copy(
                    ref.at[rows], stage.at[k, pl.ds(c * TOK, TOK)], sems_in.at[k, c]
                )
            )
            copies[-1].start()
    for k in range(RING):
        copies[2 * k].wait()
        copies[2 * k + 1].wait()
        done.append(pltpu.make_async_copy(stage.at[k], out.at[k], sems_out.at[k]))
        done[-1].start()
    for copy in done:
        copy.wait()


def pack(meta, mine, theirs, after):
    return run(
        pack_kernel,
        "pack",
        [shape(RING, 2 * TOK, FB)],
        meta,
        (mine, theirs),
        (
            pltpu.VMEM((RING, 2 * TOK, FB), F32),
            pltpu.SemaphoreType.DMA((RING, 2)),
            pltpu.SemaphoreType.DMA((RING,)),
        ),
        after,
        specs=[ANY()] * 2,
        out_specs=[ANY()],
    )


def local_grad_kernel(meta, mine, theirs, keep, out, stage, sems):
    high, low = split(jnp.concatenate([keep[...], theirs[BANKS * TOK :]], axis=0))
    copies = []
    for i in range(BANKS):
        rows = slice(i * TOK, (i + 1) * TOK)
        hidden = jnp.concatenate([mine[rows], theirs[rows]], axis=0).T
        left_high, left_low = split(hidden)
        stage[i] = dot(left_high, high) + dot(left_low, high) + dot(left_high, low)
        position = (meta[0] + i) % BANKS
        copies.append(pltpu.make_async_copy(stage.at[i], out.at[position], sems.at[i]))
        copies[-1].start()
    for copy in copies:
        copy.wait()


def turn_hidden_kernel(meta, hidden, high, low):
    for k in range(RING):
        block = hidden[(meta[2] + RING - k) % RING].T
        lanes = slice(k * 2 * TOK, (k + 1) * 2 * TOK)
        high[:, lanes], low[:, lanes] = split(block)


CHIP = 2 * TOK + 64 + 8


def pack_grads_kernel(meta, count, keep, theirs, keep_p, theirs_p, *outs):
    for k, out in enumerate(outs):
        out[0:TOK] = keep[...]
        out[TOK : 2 * TOK] = theirs[0:TOK]
        rows = pl.ds(pl.multiple_of((meta[2] + k) % RING * 64, 64), 64)
        out[2 * TOK : 2 * TOK + 64] = keep_p[rows, :] + theirs_p[rows, :]
        out[2 * TOK + 64 :] = theirs[TOK:] + count[0].astype(F32)


def ring_grad_kernel(meta, high, low, *refs):
    full, total = refs[-2:]
    outs = refs[-2 - RING : -2]
    ins = refs[:RING]
    right = [split(ref[0 : 2 * TOK]) for ref in ins]
    right_high = jnp.concatenate([r[0] for r in right], axis=0)
    right_low = jnp.concatenate([r[1] for r in right], axis=0)
    full[...] = dot(high[...], right_high) + dot(low[...], right_high) + dot(high[...], right_low)
    total[...] = sum(ref[2 * TOK :] for ref in ins)
    for k, out in enumerate(outs):
        spot = (meta[3] + k) % RING
        out[0:128] = full[pl.ds(pl.multiple_of(spot * 128, 128), 128), :]
        out[128:144] = total[pl.ds(pl.multiple_of(spot * 16, 16), 16), :]
        out[144:] = total[64:]


def collect_ring_kernel(meta, r0, r1, r2, r3, table, out, factor, *crossing):
    total = r0[...] + r1[...] + r2[...] + r3[...]
    scale = lax.rsqrt(total[144:145, :])
    out[...] = total[0:128] * scale
    for k, ref in enumerate(crossing):
        j = (BANKS - k) % BANKS
        ref[0:EMB] = total[128:144, j * 128 : (j + 1) * 128] * scale[:, 0:128]
        ref[EMB:] = table[...] * scale[:, 0:128]
    factor[...] = jnp.broadcast_to(scale, (8, FB))


def collect_kernel(meta, keep, theirs, x0, x1, x2, x3, factor, own, out, both):
    scale = factor[0:1, :]
    for j, ref in enumerate((x0, x1, x2, x3)):
        out[0:16, j * 128 : (j + 1) * 128] = ref[0:EMB]
    out[16:80] = (keep[...] + theirs[...]) * scale
    table = x0[EMB:] + x1[EMB:] + x2[EMB:] + x3[EMB:]
    blocks = [table[i * EMB : (i + 1) * EMB] for i in range(3)] + [jnp.zeros((EMB, 128), F32)]
    out[80:] = jnp.concatenate(blocks, axis=1)
    both[0:128] = own[...]
    both[128:] = out[...]


def merge_kernel(meta, *refs):
    own, near, back, own_s, near_s, back_s, far, low, high = refs
    parts = (
        (own[...], own_s[...]),
        (near[...], near_s[...]),
        (far[0:128], far[128:]),
        (back[...], back_s[...]),
    )
    for i, (value, small) in enumerate(parts):
        out, spot = (low, i) if i < 2 else (high, i - 2)
        out[spot * 144 : spot * 144 + 128] = value
        out[spot * 144 + 128 : (spot + 1) * 144] = small[0:16]
    high[288:] = sum(small[16:] for _, small in parts)


def place_last_kernel(given, meta, gathered, factor, *refs):
    out_t, out_g, stage, loads, puts = refs[given:]
    copies = [
        pltpu.make_async_copy(
            gathered.at[pl.ds(i * 2, 2)], stage.at[pl.ds(i * 2, 2)], loads.at[i]
        )
        for i in range(RING * RING)
    ]
    for copy in copies:
        copy.start()
    scale = factor[0:1, :]
    done = []
    for i, copy in enumerate(copies):
        copy.wait()
        for core, out in enumerate((out_t, out_g)):
            stage[i * 2 + core] = stage[i * 2 + core] * scale
            row = i if core == 0 else i % RING * RING + i // RING
            done.append(
                pltpu.make_async_copy(
                    stage.at[i * 2 + core], out.at[1, pl.ds(row * 128, 128)], puts.at[i * 2 + core]
                )
            )
            done[-1].start()
    for copy in done:
        copy.wait()


def place_last(meta, gathered, factor, outs, after):
    return run(
        functools.partial(place_last_kernel, len(outs)),
        "place",
        [shape(2, 2048, FB)] * 2,
        meta,
        (gathered, factor, *outs),
        (
            pltpu.VMEM((32, 128, FB), F32),
            pltpu.SemaphoreType.DMA((16,)),
            pltpu.SemaphoreType.DMA((32,)),
        ),
        after,
        [ANY(), VMEM()] + [ANY()] * len(outs),
        [ANY()] * 2,
        {3 + i: i for i in range(len(outs))},
    )


ROWS0 = 144


def place_kernel(sources, given, ending, meta, *refs):
    count = len(sources)
    mine, theirs = refs[:count], refs[count : 2 * count]
    ends = refs[2 * count : 2 * count + 2 * RING * ending]
    refs = refs[2 * count + 2 * RING * ending + given :]
    outs, small, refs = refs[:3], refs[3 : 3 + 6 * ending], refs[3 + 6 * ending :]
    stages, loads, sems = refs[:count], refs[count], refs[count + 1]
    if ending:
        end_stage, end_sems = refs[count + 2 :]
        copies = [
            pltpu.make_async_copy(ref.at[pl.ds(288, 80)], end_stage.at[i], end_sems.at[i])
            for i, ref in enumerate(ends)
        ]
        for copy in copies:
            copy.start()

    def load(i, core):
        ref = (mine, theirs)[core][i]
        many = len(sources[i][1]) * ROWS0
        return pltpu.make_async_copy(ref.at[pl.ds(0, many)], stages[i].at[core], loads.at[i, core])

    for i in range(count):
        for core in range(2):
            load(i, core).start()
    puts = []
    for i, (j, blocks) in enumerate(sources):
        for core in range(2):
            load(i, core).wait()
        for stream in range(2):
            holder = jnp.where(meta[1] == stream, 0, 1)
            major, minor = (meta[4], meta[5]) if stream == 0 else (meta[5], meta[4])
            first = (major + RING - j) % RING
            for spot, k in enumerate(blocks):
                second = (minor + RING - k) % RING
                base = pl.multiple_of((first * RING + second) * 128, 128)
                found = [
                    (
                        stages[i].at[holder, pl.ds(spot * ROWS0, 128)],
                        outs[stream].at[0, pl.ds(base, 128)],
                    )
                ]
                for q in range(BANKS):
                    bank = (meta[0] + BANKS - q) % BANKS
                    base = pl.multiple_of(bank * FB + stream * 256 + first * 64 + second * 16, 16)
                    found.append(
                        (
                            stages[i].at[holder, pl.ds(spot * ROWS0 + 128, 16), pl.ds(q * 128, 128)],
                            outs[2].at[pl.ds(base, 16)],
                        )
                    )
                for a, b in found:
                    puts.append(pltpu.make_async_copy(a, b, sems.at[len(puts)]))
                    puts[-1].start()
    if ending:
        for copy in copies:
            copy.wait()
        finish(meta, end_stage, small)
    for copy in puts:
        copy.wait()


def finish(meta, stage, outs):
    kernel, cbias, bt, bg, pb, table = outs
    own = sum(stage[i] for i in range(RING))
    other = sum(stage[i] for i in range(RING, 2 * RING))
    first = meta[1] == 0
    low = jnp.where(first, own, other)
    high = jnp.where(first, other, own)
    flat = jnp.concatenate([low[0:64], high[0:64]], axis=0)
    kernel[...] = flat[:ROWS]
    cbias[...] = flat[ROWS : ROWS + 1]
    row = ROWS + 1
    bt[...] = jnp.concatenate([flat[row : row + 1], flat[row + 2 : row + 3]], axis=0)
    bg[...] = jnp.concatenate([flat[row + 1 : row + 2], flat[row + 3 : row + 4]], axis=0)
    pb[...] = flat[row + 4 : row + 5, 0:128]
    table[...] = (own[64:] + other[64:])[:, 0:262]


def place(sources, meta, mine, theirs, outs, after, ends=None):
    total = sum(len(blocks) for _, blocks in sources) * 2 * 5
    ending = ends is not None
    inputs = [*mine, *theirs] + ([*ends[0], *ends[1]] if ending else [])
    start = 1 + len(inputs)
    shapes = [shape(2, 2048, FB)] * 2 + [shape(2048, 128)]
    if ending:
        shapes += [
            shape(ROWS, FB), shape(1, FB), shape(2, FB), shape(2, FB), shape(1, 128), shape(EMB, 262),
        ]
    return run(
        functools.partial(place_kernel, sources, len(outs), ending),
        "place",
        shapes,
        meta,
        [*inputs, *outs],
        [pltpu.VMEM((2, len(blocks) * ROWS0, FB), F32) for _, blocks in sources]
        + [
            pltpu.SemaphoreType.DMA((len(sources), 2)),
            pltpu.SemaphoreType.DMA((total,)),
        ]
        + (
            [pltpu.VMEM((2 * RING, 80, FB), F32), pltpu.SemaphoreType.DMA((2 * RING,))]
            if ending
            else []
        ),
        after,
        specs=[ANY()] * (len(inputs) + len(outs)),
        out_specs=[ANY()] * 3 + [VMEM()] * (6 * ending),
        aliases={start + i: i for i in range(len(outs))},
    )


def on_device(
    chars,
    counts,
    char_table,
    conv_weight,
    conv_bias,
    transform_weight,
    transform_bias,
    gate_weight,
    gate_bias,
    proj_weight,
    proj_bias,
    cotangent,
):
    here = lax.axis_index("dp")
    bank = lax.axis_index("bank")
    z, y, core = here // (2 * RING), here // 2 % RING, here % 2
    first = jnp.where(core == 0, z, y)
    second = jnp.where(core == 0, y, z)
    meta = jnp.stack([bank, core, first, second, z, y]).astype(jnp.int32)

    early = early_pack(meta, cotangent, proj_weight)
    early_received = lax.all_to_all(early, "bank", 0, 0, tiled=True)
    pooled, summed, lifted, emb_high, emb_low = conv_forward(
        meta, chars.T, char_table.T, conv_weight, conv_bias[None], [early]
    )

    def gather(block):
        others = {i: along_bank(block, -i) for i in (2, 1, 3)}
        return [block, others[1], others[2], others[3]]

    def bank_pieces(parts):
        return [parts[3]] + [along_bank(parts[i - 1], i) for i in (2, 1, 3)]

    def ring_gather(value, mover):
        moved = {k: mover(value, k) for k in (2, 1, 3)}
        return [value, moved[1], moved[2], moved[3]]

    def ring_pieces(pieces, mover):
        moved = {k: mover(pieces[k], k) for k in (2, 1, 3)}
        return [pieces[0], moved[1], moved[2], moved[3]]

    weights = (transform_weight, gate_weight, transform_bias, gate_bias)
    blocks0 = gather(pooled)
    rows, cots = run(
        early_rows_kernel,
        "early_rows",
        [shape(3, 256, 128), shape(3, TOK, 128)],
        meta,
        (early_received,),
        after=[pooled],
    )
    banks = (cotangent, cots, rows, to_partner(rows))
    hidden1, slope_t, slope_g, slope_r, stack0 = highway_forward(
        0, meta, blocks0, *weights, [rows]
    )
    blocks1 = gather(hidden1)
    (packed0,) = pack(meta, stack0, to_partner(stack0), [hidden1])
    (grad_last,) = with_bank_rows(
        grad_hidden_kernel, "grad_hidden", [shape(TOK, FB)], meta, counts, banks, proj_weight, packed0
    )
    hidden_0 = lax.all_to_all(packed0, "dp", 0, 0, axis_index_groups=FIRST_RINGS, tiled=True)
    hidden2, grad_t1, grad_g1, res1, keep1, stack1 = highway_forward(
        1, meta, blocks1, *weights, [], [grad_last]
    )

    *parts1, bias1 = highway_backward(
        1, meta, grad_t1, grad_g1, transform_weight, gate_weight, []
    )
    received1 = bank_pieces(parts1)
    (local1,) = run(
        local_grad_kernel,
        "local_grad",
        [shape(RING, FB, FB)],
        meta,
        (stack1, to_partner(stack1), keep1),
        (pltpu.VMEM((BANKS, FB, FB), F32), pltpu.SemaphoreType.DMA((BANKS,))),
        [bias1, hidden_0],
        out_specs=[ANY()],
    )
    ring1 = lax.psum_scatter(local1, "dp", axis_index_groups=FIRST_RINGS)
    keep_p, send_p, encoded_parts, bias_p = with_bank_rows(
        projection_kernel,
        "projection",
        [shape(256, FB), shape(256, FB), shape(128, FB), shape(8, 128)],
        meta,
        counts,
        (hidden2, *banks),
        proj_weight,
        local1,
    )
    theirs_p = to_partner(send_p)
    turned = run(
        turn_hidden_kernel,
        "turn_hidden",
        [shape(FB, 8 * TOK, dtype=BF16)] * 2,
        meta,
        (hidden_0,),
        after=[keep_p],
    )
    grad_t0, grad_g0, res0, keep0, send0 = run(
        slopes_kernel,
        "slopes",
        [shape(TOK, FB)] * 4 + [shape(TOK + 8, FB)],
        meta,
        (counts, *received1, res1, slope_t, slope_g, slope_r),
        after=[turned[0]],
        specs=[SMEM()] + [VMEM()] * 8,
    )
    packed_g = run(
        pack_grads_kernel,
        "pack_grads",
        [shape(CHIP, FB)] * RING,
        meta,
        (counts, keep0, to_partner(send0), keep_p, theirs_p),
        specs=[SMEM()] + [VMEM()] * 4,
    )
    grads_0 = ring_pieces(packed_g, along_first)
    *parts0, bias0 = highway_backward(
        0, meta, grad_t0, grad_g0, transform_weight, gate_weight, [packed_g[0]], [encoded_parts]
    )
    received0 = bank_pieces(parts0)
    (ring1,) = gate(meta, [ring1], [bias0, grads_0[1], grads_0[3]])
    own1 = lax.psum_scatter(ring1, "dp", axis_index_groups=SECOND_RINGS, tiled=True)
    pieces0 = run(
        ring_grad_kernel,
        "ring_grad",
        [shape(152, FB)] * RING,
        meta,
        (*turned, *grads_0),
        [pltpu.VMEM((FB, FB), F32), pltpu.VMEM((72, FB), F32)],
        [ring1],
    )
    second0 = ring_pieces(pieces0, along_second)
    coef, encoded, own1 = run(
        bank_sum_kernel,
        "bank_sum",
        [shape(FB, TOK), shape(TOK, 128), shape(128, FB)],
        meta,
        (counts, *received0, res0, summed, proj_bias[None], own1),
        after=[pieces0[0]],
        specs=[SMEM()] + [VMEM()] * 7 + [ANY()],
        out_specs=[VMEM(), VMEM(), ANY()],
        aliases={9: 2},
    )
    gathered1 = lax.all_gather(own1, "dp")
    keep_s, send_s, table = conv_backward(
        meta,
        (coef, lifted, emb_high, emb_low),
        conv_weight,
        chars.T,
        (bias0, bias1, bias_p),
        [coef],
    )
    theirs_s = to_partner(send_s)
    own0, factor, *crossing = run(
        collect_ring_kernel,
        "collect_ring",
        [shape(128, FB), shape(8, FB)] + [shape(64, 128)] * BANKS,
        meta,
        (*second0, table),
        after=[theirs_s],
    )

    near0, back0 = along_second(own0, 1), along_second(own0, 3)
    small, both = run(
        collect_kernel,
        "collect",
        [shape(96, FB), shape(224, FB)],
        meta,
        (
            keep_s,
            theirs_s,
            crossing[0],
            *[along_bank(crossing[k], k) for k in range(1, BANKS)],
            factor,
            own0,
        ),
        after=[near0, back0],
    )
    low, high = run(
        merge_kernel,
        "merge",
        [shape(288, FB), shape(368, FB)],
        meta,
        (
            own0,
            near0,
            back0,
            small,
            along_second(small, 1),
            along_second(small, 3),
            along_second(both, 2),
        ),
    )
    near = [along_first(low, 1), along_first(high, 1)]
    back = [along_first(low, 3), along_first(high, 3)]
    mine = [low, high]
    theirs = [to_partner(v) for v in mine]
    sources = tuple((j, half) for j in (0, 1, 3, 2) for half in ((0, 1), (2, 3)))
    outs = place_last(meta, gathered1, factor, [], [low])
    outs = list(place(sources[0:2], meta, mine[0:2], theirs[0:2], outs, []))
    mine += gate(meta, [*near, *back], [outs[2]])
    far = [along_first(mine[2], 1), along_first(mine[5], 3)]
    theirs += [to_partner(v) for v in mine[2:]]
    outs = place(sources[2:6], meta, mine[2:6], theirs[2:6], outs, [])
    far = gate(meta, far, [outs[2]])
    mine += far
    theirs += [to_partner(v) for v in far]
    spots = (1, 3, 5, 7)
    sum_wt, sum_wg, sum_pw, sum_kernel, sum_cbias, sum_bt, sum_bg, sum_pb, sum_table = place(
        sources[6:8],
        meta,
        mine[6:8],
        theirs[6:8],
        outs,
        [],
        ([mine[i] for i in spots], [theirs[i] for i in spots]),
    )
    return (
        encoded,
        sum_table.T,
        sum_kernel,
        sum_cbias[0],
        sum_wt,
        sum_bt,
        sum_wg,
        sum_bg,
        sum_pw,
        sum_pb[0],
    )


def solution(mesh):
    return jax.shard_map(
        on_device,
        mesh=mesh,
        in_specs=(
            P("dp", None),
            P("dp"),
            P(),
            P(None, "bank"),
            P("bank"),
            P(None, None, "bank"),
            P(None, "bank"),
            P(None, None, "bank"),
            P(None, "bank"),
            P(None, "bank"),
            P("bank"),
            P("dp", "bank"),
        ),
        out_specs=(
            P("dp", "bank"),
            P(),
            P(None, "bank"),
            P("bank"),
            P(None, None, "bank"),
            P(None, "bank"),
            P(None, None, "bank"),
            P(None, "bank"),
            P(None, "bank"),
            P("bank"),
        ),
        check_vma=False,
    )
```

```python
import functools

import jax
import jax.numpy as jnp
from jax import lax
from jax.experimental import pallas as pl
from jax.experimental.pallas import tpu as pltpu
from jax.sharding import PartitionSpec as P

F32 = jnp.float32
BF16 = jnp.bfloat16
LOG2E = 1.4426950408889634
MIB = 2**20

TOK = 128
CH = 50
CHP = 56
FB = 512
TAPS = 7
EMB = 16
ROWS = TAPS * EMB
BANKS = 4
RING = 4
STEP = 10

VMEM_LIMIT = 64 * MIB - 64 * 1024

VMEM = functools.partial(pl.BlockSpec, memory_space=pltpu.VMEM)
ANY = functools.partial(pl.BlockSpec, memory_space=pl.ANY)
SMEM = functools.partial(pl.BlockSpec, memory_space=pltpu.SMEM)


PARAMS = pltpu.CompilerParams(vmem_limit_bytes=VMEM_LIMIT)


def shape(*dims, dtype=F32):
    return jax.ShapeDtypeStruct(dims, dtype)


def run(kernel, name, outs, meta, inputs, scratch=(), after=(), specs=None, out_specs=None, aliases=None):
    inputs, after = list(inputs), list(after)
    count = 1 + len(inputs)

    def body(*refs):
        kernel(*refs[:count], *refs[count + len(after) :])

    return pl.pallas_call(
        body,
        out_shape=outs,
        in_specs=[SMEM()] + list(specs or [VMEM()] * len(inputs)) + [ANY()] * len(after),
        out_specs=list(out_specs or [VMEM()] * len(outs)),
        scratch_shapes=list(scratch),
        input_output_aliases=aliases or {},
        compiler_params=PARAMS,
        name=name,
    )(meta, *inputs, *after)


def gate_kernel(meta, *refs):
    pass


def gate(meta, values, after):
    values = list(values)
    return run(
        gate_kernel,
        "gate",
        [jax.ShapeDtypeStruct(v.shape, v.dtype) for v in values],
        meta,
        values,
        after=after,
        specs=[ANY()] * len(values),
        out_specs=[ANY()] * len(values),
        aliases={1 + i: i for i in range(len(values))},
    )


def along_bank(value, shift):
    return lax.ppermute(value, "bank", [(i, (i + shift) % BANKS) for i in range(BANKS)])


def place_of(z, y, core):
    return (z * RING + y) * 2 + core


def to_partner(value):
    return lax.ppermute(value, "dp", [(i, i ^ 1) for i in range(2 * RING * RING)])


def ring_perm(shift, z_core):
    perm = []
    for z in range(RING):
        for y in range(RING):
            for core in range(2):
                if core == z_core:
                    to = place_of((z + shift) % RING, y, core)
                else:
                    to = place_of(z, (y + shift) % RING, core)
                perm.append((place_of(z, y, core), to))
    return perm


FIRST_RINGS = [[place_of(z, y, 0) for z in range(RING)] for y in range(RING)] + [
    [place_of(z, y, 1) for y in range(RING)] for z in range(RING)
]
SECOND_RINGS = [[place_of(z, y, 0) for y in range(RING)] for z in range(RING)] + [
    [place_of(z, y, 1) for z in range(RING)] for y in range(RING)
]


def along_first(value, shift):
    return lax.ppermute(value, "dp", ring_perm(shift, 0))


def along_second(value, shift):
    return lax.ppermute(value, "dp", ring_perm(shift, 1))


def split(value):
    high = value.astype(BF16)
    low = (value - high.astype(F32)).astype(BF16)
    return high, low


def dot(left, right, dims=((1,), (0,))):
    return lax.dot_general(left, right, (dims, ((), ())), preferred_element_type=F32)


def dot3(left, right, dims=((1,), (0,))):
    lh, ll = split(left)
    rh, rl = split(right)
    return dot(lh, rh, dims) + dot(ll, rh, dims) + dot(lh, rl, dims)


def widths_of(column):
    width = jnp.ones_like(column)
    for power in range(6):
        width = width + (column >= 32 * 2**power).astype(jnp.int32)
    return width


def conv_forward_kernel(
    meta, chars, table, weight, bias, pooled, summed, lifted_out, emb_high, emb_low, wide, wide_table, lifted, sems
):
    start = meta[0] * FB
    column = start + lax.broadcasted_iota(jnp.int32, (ROWS, FB), 1)
    tap = lax.broadcasted_iota(jnp.int32, (ROWS, FB), 0) // EMB
    kernel = jnp.where(tap < widths_of(column), weight[...], 0.0) * LOG2E
    high = kernel.astype(BF16).astype(F32)
    shift = bias[...] * LOG2E
    shift_high = shift.astype(BF16).astype(F32)
    row = lax.broadcasted_iota(jnp.int32, (EMB, FB), 0)
    shifts = jnp.where(row == 0, shift_high, jnp.where(row == 1, shift - shift_high, 0.0))
    rows = [high, kernel - high, shifts, jnp.zeros((EMB, FB), F32)]
    wide[...] = jnp.concatenate(rows, axis=0).T.astype(BF16)
    wide_table[:, 0 : table.shape[1]] = table[...]
    parts = [wide_table[:, 128 * i : 128 * (i + 1)] for i in range(3)]
    for p in range(CH):
        ids = jnp.broadcast_to(chars[p : p + 1, :], (EMB, TOK))
        lane = ids & 127
        part = ids >> 7
        found = [
            jnp.take_along_axis(t, lane, axis=1, mode="promise_in_bounds") for t in parts
        ]
        value = jnp.where(part == 0, found[0], jnp.where(part == 1, found[1], found[2]))
        high, low = split(value)
        emb_high[p * EMB : (p + 1) * EMB, :] = high
        emb_low[p * EMB : (p + 1) * EMB, :] = low
    zeros = jnp.zeros(((CHP - CH) * EMB, TOK), BF16)
    emb_high[CH * EMB :, :] = zeros
    emb_low[CH * EMB :, :] = zeros
    one_row = lax.broadcasted_iota(jnp.int32, (EMB, 2 * TOK), 0)
    ones = jnp.where(one_row < 2, 1.0, 0.0).astype(BF16)
    width = widths_of(start + lax.broadcasted_iota(jnp.int32, (FB, TOK), 0))

    def window(ref, pair):
        base = pair * 2 * EMB
        return jnp.concatenate(
            [ref[base : base + ROWS, :], ref[base + EMB : base + EMB + ROWS, :]], axis=1
        )

    for pair in range(CH // 2):
        high = window(emb_high, pair)
        low = window(emb_low, pair)
        pre = dot(wide[:, : 2 * ROWS + EMB], jnp.concatenate([high, high, ones], axis=0))
        pre += dot(wide[:, :ROWS], low)
        both = jnp.exp2(pre)
        first, second = both[:, :TOK], both[:, TOK:]
        if 2 * pair + 1 > CH - TAPS:
            first = jnp.where(width <= CH - 2 * pair, first, 0.0)
            second = jnp.where(width <= CH - 2 * pair - 1, second, 0.0)
        lifted[2 * pair] = first
        lifted[2 * pair + 1] = second
        pltpu.make_async_copy(
            lifted.at[pl.ds(2 * pair, 2)], lifted_out.at[pl.ds(2 * pair, 2)], sems.at[pair]
        ).start()
        if pair:
            summed[...] += first + second
        else:
            summed[...] = first + second
    valid = (CH + 1 - width).astype(F32)
    total = summed[...] + valid
    summed[...] = total
    pooled[...] = jnp.log(total / valid).T
    for pair in range(CH // 2):
        pltpu.make_async_copy(
            lifted.at[pl.ds(2 * pair, 2)], lifted_out.at[pl.ds(2 * pair, 2)], sems.at[pair]
        ).wait()


def conv_forward(meta, chars_t, table_t, weight, bias, after):
    return run(
        conv_forward_kernel,
        "conv_forward",
        (
            shape(TOK, FB),
            shape(FB, TOK),
            shape(CH, FB, TOK),
            shape(CHP * EMB, TOK, dtype=BF16),
            shape(CHP * EMB, TOK, dtype=BF16),
        ),
        meta,
        (chars_t, table_t, weight, bias),
        (
            pltpu.VMEM((FB, 2 * ROWS + 2 * EMB), BF16),
            pltpu.VMEM((EMB, 384), F32),
            pltpu.VMEM((CH, FB, TOK), F32),
            pltpu.SemaphoreType.DMA((CH // 2,)),
        ),
        after,
        out_specs=[VMEM(), VMEM(), ANY(), VMEM(), VMEM()],
    )


def bank_sum_kernel(meta, count, r0, r1, r2, r3, residual, summed, proj_bias, passed, coef, encoded, same):
    total = r0[...] + r1[...] + r2[...] + r3[...]
    coef[...] = (total[0:TOK] + residual[...]).T / summed[...]
    value = jnp.concatenate([total[TOK:, q * 128 : (q + 1) * 128] for q in range(4)], axis=0)
    live = live_rows(count[0], 128)
    encoded[...] = jnp.where(live, value + proj_bias[...], 0.0)


def conv_backward_kernel(
    meta, coef, lifted, emb_high, emb_low, weight, chars, bias0, bias1, bias_p, keep, send, table,
    kernel, grads, windows, acc, grad_emb, buffer, sems,
):
    start = meta[0] * FB
    copies = [
        pltpu.make_async_copy(
            lifted.at[pl.ds(i * 2, 2)], buffer.at[pl.ds(i * 2, 2)], sems.at[i]
        )
        for i in range(CH // 2)
    ]
    for copy in copies:
        copy.start()
    column = start + lax.broadcasted_iota(jnp.int32, (ROWS, FB), 1)
    tap = lax.broadcasted_iota(jnp.int32, (ROWS, FB), 0) // EMB
    high, low = split(jnp.where(tap < widths_of(column), weight[...], 0.0))
    kernel[0:ROWS] = high
    kernel[ROWS:] = low
    grad_emb[...] = jnp.zeros_like(grad_emb)
    row = lax.broadcasted_iota(jnp.int32, (EMB, STEP * TOK), 0)
    ones = jnp.where(row < 1, 1.0, 0.0).astype(BF16)
    for slot in range(2):
        windows[slot, 2 * ROWS :, :] = ones

    for step in range(CH // STEP):
        slot = step % 2
        for j in range(STEP):
            p = step * STEP + j
            if p % 2 == 0:
                copies[p // 2].wait()
            high, low = split(coef[...] * buffer[p])
            lanes = slice(j * TOK, (j + 1) * TOK)
            grads[slot, 0:FB, lanes] = high
            grads[slot, FB:, lanes] = low
            windows[slot, 0:ROWS, lanes] = emb_high[p * EMB : p * EMB + ROWS, :]
            windows[slot, ROWS : 2 * ROWS, lanes] = emb_low[p * EMB : p * EMB + ROWS, :]
        part = dot(grads[slot], windows[slot], ((1,), (1,)))
        if step:
            acc[...] += part
        else:
            acc[...] = part
        from_high = dot(kernel[...], grads[slot, 0:FB, :])
        from_low = dot(kernel[0:ROWS, :], grads[slot, FB:, :])
        grad_windows = from_high[0:ROWS] + from_high[ROWS:] + from_low
        for j in range(STEP):
            base = (step * STEP + j) * EMB
            grad_emb[base : base + ROWS, :] += grad_windows[:, j * TOK : (j + 1) * TOK]

    total = acc[...]
    grad_kernel = total[0:FB, 0:ROWS] + total[0:FB, ROWS : 2 * ROWS] + total[FB:, 0:ROWS]
    grad_bias = total[0:FB, 2 * ROWS :] + total[FB:, 2 * ROWS :]
    full = jnp.concatenate([grad_kernel, grad_bias], axis=1).T
    column = start + lax.broadcasted_iota(jnp.int32, (ROWS + EMB, FB), 1)
    row = lax.broadcasted_iota(jnp.int32, (ROWS + EMB, FB), 0)
    full = jnp.where((row > ROWS) | (row // EMB >= widths_of(column)) & (row < ROWS), 0.0, full)
    more = jnp.concatenate(
        [
            bias0[0:2],
            bias1[0:2],
            jnp.concatenate([bias_p[0:1], jnp.zeros((1, FB - 128), F32)], axis=1),
            jnp.zeros((10, FB), F32),
        ],
        axis=0,
    )
    full = jnp.concatenate([full[: ROWS + 1], more], axis=0)
    first_core = meta[1] == 0
    keep[...] = jnp.where(first_core, full[:64], full[64:])
    send[...] = jnp.where(first_core, full[64:], full[:64])
    found = jnp.zeros((2 * EMB, 384), F32)
    vocab = lax.broadcasted_iota(jnp.int32, (TOK, 384), 1).astype(F32)
    ids = jnp.concatenate([chars[...].astype(F32), jnp.zeros((CHP - CH, TOK), F32)], axis=0).T
    for begin in range(0, CH, STEP):
        left, right = [], []
        for q in range(begin, begin + STEP):
            high, low = split(grad_emb[q * EMB : (q + 1) * EMB, :])
            left.append(jnp.concatenate([high, low], axis=0))
            right.append(jnp.where(ids[:, q : q + 1] == vocab, 1.0, 0.0).astype(BF16))
        found += dot(jnp.concatenate(left, axis=1), jnp.concatenate(right, axis=0))
    found = found[0:EMB] + found[EMB:]
    for i in range(3):
        table[i * EMB : (i + 1) * EMB] = found[:, i * 128 : (i + 1) * 128]


def conv_backward(meta, inputs, weight, chars, biases, after):
    return run(
        conv_backward_kernel,
        "conv_backward",
        [shape(64, FB), shape(64, FB), shape(48, 128)],
        meta,
        (*inputs, weight, chars, *biases),
        (
            pltpu.VMEM((2 * ROWS, FB), BF16),
            pltpu.VMEM((2, 2 * FB, STEP * TOK), BF16),
            pltpu.VMEM((2, 2 * ROWS + EMB, STEP * TOK), BF16),
            pltpu.VMEM((2 * FB, 2 * ROWS + EMB), F32),
            pltpu.VMEM((CHP * EMB, TOK), F32),
            pltpu.VMEM((CH, FB, TOK), F32),
            pltpu.SemaphoreType.DMA((CH // 2,)),
        ),
        after,
        [VMEM(), ANY()] + [VMEM()] * 7,
    )


def live_rows(count, columns):
    return lax.broadcasted_iota(jnp.int32, (TOK, columns), 0) < count


def early_rows_kernel(meta, received, out, grads):
    for j in range(1, BANKS):
        source = (meta[0] + BANKS - j) % BANKS
        out[j - 1] = received[source, TOK:]
        grads[j - 1] = received[source, 0:TOK]


def bank_rows(meta, mine, others):
    found = []
    first = meta[1] == 0
    for i in range(BANKS - 1):
        low = jnp.where(first, mine[i], others[i])
        high = jnp.where(first, others[i], mine[i])
        found.append(jnp.concatenate([low, high], axis=0))
    return found


def grad_hidden_kernel(meta, count, cot, grads, mine, others, proj, token, out):
    live = live_rows(count[0], 128)
    total = dot3(jnp.where(live, cot[...], 0.0), proj[...], ((1,), (1,)))
    for i, rows in enumerate(bank_rows(meta, mine, others)):
        total += dot3(jnp.where(live, grads[i], 0.0), rows, ((1,), (1,)))
    out[...] = total


def with_bank_rows(kernel, name, outs, meta, count, inputs, proj, after):
    return pl.pallas_call(
        kernel,
        out_shape=outs,
        grid_spec=pltpu.PrefetchScalarGridSpec(
            num_scalar_prefetch=2,
            grid=(1,),
            in_specs=[VMEM()] * len(inputs)
            + [pl.BlockSpec((FB, 128), lambda i, meta, count: (meta[0], 0)), ANY()],
            out_specs=[VMEM()] * len(outs),
        ),
        compiler_params=PARAMS,
        name=name,
    )(meta, count, *inputs, proj, after)


def projection_kernel(meta, count, hidden, cot, cots, mine, others, proj, token, keep, send, encoded, bias):
    live = live_rows(count[0], 128)
    grads = [jnp.where(live, value, 0.0) for value in (cot[...], cots[0], cots[1], cots[2])]
    rows = [proj[...]] + bank_rows(meta, mine, others)
    value = hidden[...]
    both = jnp.concatenate(split(value), axis=0)
    turned = jnp.concatenate(split(value.T), axis=0)
    first = meta[1] == 0
    for j in range(BANKS):
        high, low = split(rows[j])
        part = dot(both, high)
        part = part[0:TOK] + part[TOK:] + dot(both[0:TOK], low)
        for q in range(4):
            encoded[j * 32 : (j + 1) * 32, q * 128 : (q + 1) * 128] = part[q * 32 : (q + 1) * 32]
        high, low = split(grads[j])
        part = dot(turned, high)
        part = part[0:FB] + part[FB:] + dot(turned[0:FB], low)
        lanes = slice(j * 128, (j + 1) * 128)
        keep[:, lanes] = jnp.where(first, part[0:256], part[256:])
        send[:, lanes] = jnp.where(first, part[256:], part[0:256])
    bias[...] = jnp.broadcast_to(jnp.sum(grads[0], axis=0, keepdims=True), (8, 128))


def early_pack_kernel(meta, cot, p1, p2, p3, out):
    for j, ref in enumerate((p1, p2, p3)):
        to = (meta[0] + 1 + j) % BANKS
        out[to, 0:TOK] = cot[...]
        out[to, TOK:] = ref[...]


def early_pack(meta, cot, proj):
    def rows(j):
        return pl.BlockSpec((256, 128), lambda i, meta: ((meta[0] + j) % BANKS * 2 + meta[1], 0))

    return pl.pallas_call(
        early_pack_kernel,
        out_shape=shape(BANKS, TOK + 256, 128),
        grid_spec=pltpu.PrefetchScalarGridSpec(
            num_scalar_prefetch=1,
            grid=(1,),
            in_specs=[VMEM()] + [rows(j) for j in range(1, BANKS)],
            out_specs=VMEM(),
        ),
        compiler_params=PARAMS,
        name="early_pack",
    )(meta, cot, proj, proj, proj)


def sigmoid(value):
    return 1.0 / (1.0 + jnp.exp(-value))


def weight_copies(layer, shift, meta, weights, buffer, sems):
    found = []
    for i in range(BANKS):
        for m, ref in enumerate(weights):
            base = pl.multiple_of((meta[0] + shift + i) % BANKS * FB, FB)
            for half in range(2):
                rows = pl.ds(base + half * 256, 256)
                found.append(
                    pltpu.make_async_copy(
                        ref.at[layer, rows],
                        buffer.at[m, i, pl.ds(half * 256, 256)],
                        sems.at[m, i, half],
                    )
                )
    return found


WEIGHT_SCRATCH = (
    pltpu.VMEM((2, BANKS, FB, FB), F32),
    pltpu.SemaphoreType.DMA((2, BANKS, 2)),
)


def forward_kernel(layer, meta, x0, x1, x2, x3, weight_t, weight_g, bias_t, bias_g, *rest):
    last = layer == 1
    *rest, buffer, sems = rest
    if last:
        grad, hidden, out_t, out_g, out_r, keep, stack = rest
    else:
        hidden, out_t, out_g, out_r, stack = rest
    copies = weight_copies(layer, 0, meta, (weight_t, weight_g), buffer, sems)
    for copy in copies:
        copy.start()
    acc = [jnp.zeros((TOK, FB), F32), jnp.zeros((TOK, FB), F32)]
    for i, ref in enumerate((x0, x1, x2, x3)):
        value = ref[...]
        stack[i * TOK : (i + 1) * TOK] = value
        both = jnp.concatenate(split(value), axis=0)
        for m in range(2):
            for copy in copies[i * 4 + m * 2 : i * 4 + m * 2 + 2]:
                copy.wait()
            high, low = split(buffer[m, i])
            found = dot(both, high)
            acc[m] += found[0:TOK] + found[TOK:] + dot(both[0:TOK], low)
    pre_t = acc[0] + bias_t[layer : layer + 1]
    gate = sigmoid(acc[1] + bias_g[layer : layer + 1])
    sigma = sigmoid(pre_t)
    own = x0[...]
    silu = pre_t * sigma
    hidden[...] = gate * silu + (1.0 - gate) * own
    slope_t = gate * sigma * (1.0 + pre_t * (1.0 - sigma))
    slope_g = (silu - own) * gate * (1.0 - gate)
    if last:
        grad_t = grad[...] * slope_t
        grad_g = grad[...] * slope_g
        out_t[...] = grad_t
        out_g[...] = grad_g
        out_r[...] = grad[...] * (1.0 - gate)
        first = meta[1] == 0
        keep[...] = jnp.where(first, grad_t, grad_g)
        stack[BANKS * TOK :] = jnp.where(first, grad_g, grad_t)
    else:
        out_t[...] = slope_t
        out_g[...] = slope_g
        out_r[...] = 1.0 - gate


def highway_forward(layer, meta, blocks, weight_t, weight_g, bias_t, bias_g, after, grad=()):
    last = layer == 1
    outs = [shape(TOK, FB)] * (4 + last) + [shape((BANKS + last) * TOK, FB)]
    return run(
        functools.partial(forward_kernel, layer),
        "highway_forward",
        outs,
        meta,
        (*blocks, weight_t, weight_g, bias_t, bias_g, *grad),
        WEIGHT_SCRATCH,
        after,
        [VMEM()] * 4 + [ANY()] * 2 + [VMEM()] * (2 + last),
    )


def slopes_kernel(
    meta, count, r0, r1, r2, r3, residual, slope_t, slope_g, slope_r, out_t, out_g, out_r, keep, send
):
    grad = r0[...] + r1[...] + r2[...] + r3[...] + residual[...]
    grad_t = grad * slope_t[...]
    grad_g = grad * slope_g[...]
    first = meta[1] == 0
    out_t[...] = grad_t
    out_g[...] = grad_g
    out_r[...] = grad * slope_r[...]
    keep[...] = jnp.where(first, grad_t, grad_g)
    send[0:TOK] = jnp.where(first, grad_g, grad_t)
    send[TOK:] = jnp.full((8, FB), count[0].astype(F32))


def backward_kernel(layer, meta, grad_t, grad_g, *rest):
    *rest, bias, buffer, sems = rest
    encoded = rest.pop(0) if layer == 0 else None
    weight_t, weight_g, *outs = rest
    copies = weight_copies(layer, 1, meta, (weight_t, weight_g), buffer, sems)
    for copy in copies:
        copy.start()
    left = [jnp.concatenate(split(ref[...]), axis=0) for ref in (grad_t, grad_g)]
    sums = [jnp.sum(ref[...], axis=0, keepdims=True) for ref in (grad_t, grad_g)]
    row = lax.broadcasted_iota(jnp.int32, (8, FB), 0)
    bias[...] = jnp.where(row == 0, sums[0], jnp.where(row == 1, sums[1], 0.0))
    for i in range(BANKS):
        total = jnp.zeros((TOK, FB), F32)
        for m in range(2):
            for copy in copies[i * 4 + m * 2 : i * 4 + m * 2 + 2]:
                copy.wait()
            high, low = split(buffer[m, i])
            both = dot(left[m], high, ((1,), (1,)))
            total += both[0:TOK] + both[TOK:] + dot(left[m][0:TOK], low, ((1,), (1,)))
        outs[i][0:TOK] = total
        if layer == 0:
            j = BANKS - 1 - i
            outs[i][TOK:] = encoded[j * 32 : (j + 1) * 32]


def highway_backward(layer, meta, grad_t, grad_g, weight_t, weight_g, after, encoded=()):
    parts = [shape(TOK + 32 * len(encoded), FB)] * BANKS
    return run(
        functools.partial(backward_kernel, layer),
        "highway_backward",
        parts + [shape(8, FB)],
        meta,
        (grad_t, grad_g, *encoded, weight_t, weight_g),
        WEIGHT_SCRATCH,
        after,
        [VMEM()] * (2 + len(encoded)) + [ANY()] * 2,
    )


def pack_kernel(meta, mine, theirs, out, stage, sems_in, sems_out):
    copies, done = [], []
    for k in range(RING):
        spot = (k + BANKS - meta[0]) % BANKS
        rows = pl.ds(pl.multiple_of(spot * TOK, TOK), TOK)
        for c, ref in enumerate((mine, theirs)):
            copies.append(
                pltpu.make_async_copy(
                    ref.at[rows], stage.at[k, pl.ds(c * TOK, TOK)], sems_in.at[k, c]
                )
            )
            copies[-1].start()
    for k in range(RING):
        copies[2 * k].wait()
        copies[2 * k + 1].wait()
        done.append(pltpu.make_async_copy(stage.at[k], out.at[k], sems_out.at[k]))
        done[-1].start()
    for copy in done:
        copy.wait()


def pack(meta, mine, theirs, after):
    return run(
        pack_kernel,
        "pack",
        [shape(RING, 2 * TOK, FB)],
        meta,
        (mine, theirs),
        (
            pltpu.VMEM((RING, 2 * TOK, FB), F32),
            pltpu.SemaphoreType.DMA((RING, 2)),
            pltpu.SemaphoreType.DMA((RING,)),
        ),
        after,
        specs=[ANY()] * 2,
        out_specs=[ANY()],
    )


def local_grad_kernel(meta, mine, theirs, keep, out, stage, sems):
    high, low = split(jnp.concatenate([keep[...], theirs[BANKS * TOK :]], axis=0))
    copies = []
    for i in range(BANKS):
        rows = slice(i * TOK, (i + 1) * TOK)
        hidden = jnp.concatenate([mine[rows], theirs[rows]], axis=0).T
        left_high, left_low = split(hidden)
        stage[i] = dot(left_high, high) + dot(left_low, high) + dot(left_high, low)
        position = (meta[0] + i) % BANKS
        copies.append(pltpu.make_async_copy(stage.at[i], out.at[position], sems.at[i]))
        copies[-1].start()
    for copy in copies:
        copy.wait()


def turn_hidden_kernel(meta, hidden, high, low):
    for k in range(RING):
        block = hidden[(meta[2] + RING - k) % RING].T
        lanes = slice(k * 2 * TOK, (k + 1) * 2 * TOK)
        high[:, lanes], low[:, lanes] = split(block)


CHIP = 2 * TOK + 64 + 8


def pack_grads_kernel(meta, count, keep, theirs, keep_p, theirs_p, *outs):
    for k, out in enumerate(outs):
        out[0:TOK] = keep[...]
        out[TOK : 2 * TOK] = theirs[0:TOK]
        rows = pl.ds(pl.multiple_of((meta[2] + k) % RING * 64, 64), 64)
        out[2 * TOK : 2 * TOK + 64] = keep_p[rows, :] + theirs_p[rows, :]
        out[2 * TOK + 64 :] = theirs[TOK:] + count[0].astype(F32)


def ring_grad_kernel(meta, high, low, *refs):
    full, total = refs[-2:]
    outs = refs[-2 - RING : -2]
    ins = refs[:RING]
    right = [split(ref[0 : 2 * TOK]) for ref in ins]
    right_high = jnp.concatenate([r[0] for r in right], axis=0)
    right_low = jnp.concatenate([r[1] for r in right], axis=0)
    full[...] = dot(high[...], right_high) + dot(low[...], right_high) + dot(high[...], right_low)
    total[...] = sum(ref[2 * TOK :] for ref in ins)
    for k, out in enumerate(outs):
        spot = (meta[3] + k) % RING
        out[0:128] = full[pl.ds(pl.multiple_of(spot * 128, 128), 128), :]
        out[128:144] = total[pl.ds(pl.multiple_of(spot * 16, 16), 16), :]
        out[144:] = total[64:]


def collect_ring_kernel(meta, r0, r1, r2, r3, table, out, factor, *crossing):
    total = r0[...] + r1[...] + r2[...] + r3[...]
    scale = lax.rsqrt(total[144:145, :])
    out[...] = total[0:128] * scale
    for k, ref in enumerate(crossing):
        j = (BANKS - k) % BANKS
        ref[0:EMB] = total[128:144, j * 128 : (j + 1) * 128] * scale[:, 0:128]
        ref[EMB:] = table[...] * scale[:, 0:128]
    factor[...] = jnp.broadcast_to(scale, (8, FB))


def collect_kernel(meta, keep, theirs, x0, x1, x2, x3, factor, out):
    scale = factor[0:1, :]
    for j, ref in enumerate((x0, x1, x2, x3)):
        out[0:16, j * 128 : (j + 1) * 128] = ref[0:EMB]
    out[16:80] = (keep[...] + theirs[...]) * scale
    table = x0[EMB:] + x1[EMB:] + x2[EMB:] + x3[EMB:]
    blocks = [table[i * EMB : (i + 1) * EMB] for i in range(3)] + [jnp.zeros((EMB, 128), F32)]
    out[80:] = jnp.concatenate(blocks, axis=1)


def merge_kernel(meta, *refs):
    *parts, low, high = refs
    small = parts[RING:]
    for i in range(RING):
        out, spot = (low, i) if i < 2 else (high, i - 2)
        out[spot * 144 : spot * 144 + 128] = parts[i][...]
        out[spot * 144 + 128 : (spot + 1) * 144] = small[i][0:16]
    high[288:] = sum(ref[16:] for ref in small)


def place_last_kernel(given, meta, gathered, factor, *refs):
    out_t, out_g, stage, loads, puts = refs[given:]
    copies = [
        pltpu.make_async_copy(
            gathered.at[pl.ds(i * 2, 2)], stage.at[pl.ds(i * 2, 2)], loads.at[i]
        )
        for i in range(RING * RING)
    ]
    for copy in copies:
        copy.start()
    scale = factor[0:1, :]
    done = []
    for i, copy in enumerate(copies):
        copy.wait()
        for core, out in enumerate((out_t, out_g)):
            stage[i * 2 + core] = stage[i * 2 + core] * scale
            row = i if core == 0 else i % RING * RING + i // RING
            done.append(
                pltpu.make_async_copy(
                    stage.at[i * 2 + core], out.at[1, pl.ds(row * 128, 128)], puts.at[i * 2 + core]
                )
            )
            done[-1].start()
    for copy in done:
        copy.wait()


def place_last(meta, gathered, factor, outs, after):
    return run(
        functools.partial(place_last_kernel, len(outs)),
        "place",
        [shape(2, 2048, FB)] * 2,
        meta,
        (gathered, factor, *outs),
        (
            pltpu.VMEM((32, 128, FB), F32),
            pltpu.SemaphoreType.DMA((16,)),
            pltpu.SemaphoreType.DMA((32,)),
        ),
        after,
        [ANY(), VMEM()] + [ANY()] * len(outs),
        [ANY()] * 2,
        {3 + i: i for i in range(len(outs))},
    )


ROWS0 = 144


def place_kernel(sources, given, ending, meta, *refs):
    count = len(sources)
    mine, theirs = refs[:count], refs[count : 2 * count]
    ends = refs[2 * count : 2 * count + 2 * RING * ending]
    refs = refs[2 * count + 2 * RING * ending + given :]
    outs, small, refs = refs[:3], refs[3 : 3 + 6 * ending], refs[3 + 6 * ending :]
    stages, loads, sems = refs[:count], refs[count], refs[count + 1]
    if ending:
        end_stage, end_sems = refs[count + 2 :]
        copies = [
            pltpu.make_async_copy(ref.at[pl.ds(288, 80)], end_stage.at[i], end_sems.at[i])
            for i, ref in enumerate(ends)
        ]
        for copy in copies:
            copy.start()

    def load(i, core):
        ref = (mine, theirs)[core][i]
        many = len(sources[i][1]) * ROWS0
        return pltpu.make_async_copy(ref.at[pl.ds(0, many)], stages[i].at[core], loads.at[i, core])

    for i in range(count):
        for core in range(2):
            load(i, core).start()
    puts = []
    for i, (j, blocks) in enumerate(sources):
        for core in range(2):
            load(i, core).wait()
        for stream in range(2):
            holder = jnp.where(meta[1] == stream, 0, 1)
            major, minor = (meta[4], meta[5]) if stream == 0 else (meta[5], meta[4])
            first = (major + RING - j) % RING
            for spot, k in enumerate(blocks):
                second = (minor + RING - k) % RING
                base = pl.multiple_of((first * RING + second) * 128, 128)
                found = [
                    (
                        stages[i].at[holder, pl.ds(spot * ROWS0, 128)],
                        outs[stream].at[0, pl.ds(base, 128)],
                    )
                ]
                for q in range(BANKS):
                    bank = (meta[0] + BANKS - q) % BANKS
                    base = pl.multiple_of(bank * FB + stream * 256 + first * 64 + second * 16, 16)
                    found.append(
                        (
                            stages[i].at[holder, pl.ds(spot * ROWS0 + 128, 16), pl.ds(q * 128, 128)],
                            outs[2].at[pl.ds(base, 16)],
                        )
                    )
                for a, b in found:
                    puts.append(pltpu.make_async_copy(a, b, sems.at[len(puts)]))
                    puts[-1].start()
    if ending:
        for copy in copies:
            copy.wait()
        finish(meta, end_stage, small)
    for copy in puts:
        copy.wait()


def finish(meta, stage, outs):
    kernel, cbias, bt, bg, pb, table = outs
    own = sum(stage[i] for i in range(RING))
    other = sum(stage[i] for i in range(RING, 2 * RING))
    first = meta[1] == 0
    low = jnp.where(first, own, other)
    high = jnp.where(first, other, own)
    flat = jnp.concatenate([low[0:64], high[0:64]], axis=0)
    kernel[...] = flat[:ROWS]
    cbias[...] = flat[ROWS : ROWS + 1]
    row = ROWS + 1
    bt[...] = jnp.concatenate([flat[row : row + 1], flat[row + 2 : row + 3]], axis=0)
    bg[...] = jnp.concatenate([flat[row + 1 : row + 2], flat[row + 3 : row + 4]], axis=0)
    pb[...] = flat[row + 4 : row + 5, 0:128]
    table[...] = (own[64:] + other[64:])[:, 0:262]


def place(sources, meta, mine, theirs, outs, after, ends=None):
    total = sum(len(blocks) for _, blocks in sources) * 2 * 5
    ending = ends is not None
    inputs = [*mine, *theirs] + ([*ends[0], *ends[1]] if ending else [])
    start = 1 + len(inputs)
    shapes = [shape(2, 2048, FB)] * 2 + [shape(2048, 128)]
    if ending:
        shapes += [
            shape(ROWS, FB), shape(1, FB), shape(2, FB), shape(2, FB), shape(1, 128), shape(EMB, 262),
        ]
    return run(
        functools.partial(place_kernel, sources, len(outs), ending),
        "place",
        shapes,
        meta,
        [*inputs, *outs],
        [pltpu.VMEM((2, len(blocks) * ROWS0, FB), F32) for _, blocks in sources]
        + [
            pltpu.SemaphoreType.DMA((len(sources), 2)),
            pltpu.SemaphoreType.DMA((total,)),
        ]
        + (
            [pltpu.VMEM((2 * RING, 80, FB), F32), pltpu.SemaphoreType.DMA((2 * RING,))]
            if ending
            else []
        ),
        after,
        specs=[ANY()] * (len(inputs) + len(outs)),
        out_specs=[ANY()] * 3 + [VMEM()] * (6 * ending),
        aliases={start + i: i for i in range(len(outs))},
    )


def on_device(
    chars,
    counts,
    char_table,
    conv_weight,
    conv_bias,
    transform_weight,
    transform_bias,
    gate_weight,
    gate_bias,
    proj_weight,
    proj_bias,
    cotangent,
):
    here = lax.axis_index("dp")
    bank = lax.axis_index("bank")
    z, y, core = here // (2 * RING), here // 2 % RING, here % 2
    first = jnp.where(core == 0, z, y)
    second = jnp.where(core == 0, y, z)
    meta = jnp.stack([bank, core, first, second, z, y]).astype(jnp.int32)

    early = early_pack(meta, cotangent, proj_weight)
    early_received = lax.all_to_all(early, "bank", 0, 0, tiled=True)
    pooled, summed, lifted, emb_high, emb_low = conv_forward(
        meta, chars.T, char_table.T, conv_weight, conv_bias[None], [early]
    )

    def gather(block):
        others = {i: along_bank(block, -i) for i in (2, 1, 3)}
        return [block, others[1], others[2], others[3]]

    def bank_pieces(parts):
        return [parts[3]] + [along_bank(parts[i - 1], i) for i in (2, 1, 3)]

    def ring_gather(value, mover):
        moved = {k: mover(value, k) for k in (2, 1, 3)}
        return [value, moved[1], moved[2], moved[3]]

    def ring_pieces(pieces, mover):
        moved = {k: mover(pieces[k], k) for k in (2, 1, 3)}
        return [pieces[0], moved[1], moved[2], moved[3]]

    weights = (transform_weight, gate_weight, transform_bias, gate_bias)
    blocks0 = gather(pooled)
    rows, cots = run(
        early_rows_kernel,
        "early_rows",
        [shape(3, 256, 128), shape(3, TOK, 128)],
        meta,
        (early_received,),
        after=[pooled],
    )
    banks = (cotangent, cots, rows, to_partner(rows))
    hidden1, slope_t, slope_g, slope_r, stack0 = highway_forward(
        0, meta, blocks0, *weights, [rows]
    )
    blocks1 = gather(hidden1)
    (packed0,) = pack(meta, stack0, to_partner(stack0), [hidden1])
    (grad_last,) = with_bank_rows(
        grad_hidden_kernel, "grad_hidden", [shape(TOK, FB)], meta, counts, banks, proj_weight, packed0
    )
    hidden_0 = lax.all_to_all(packed0, "dp", 0, 0, axis_index_groups=FIRST_RINGS, tiled=True)
    hidden2, grad_t1, grad_g1, res1, keep1, stack1 = highway_forward(
        1, meta, blocks1, *weights, [], [grad_last]
    )

    *parts1, bias1 = highway_backward(
        1, meta, grad_t1, grad_g1, transform_weight, gate_weight, []
    )
    received1 = bank_pieces(parts1)
    (local1,) = run(
        local_grad_kernel,
        "local_grad",
        [shape(RING, FB, FB)],
        meta,
        (stack1, to_partner(stack1), keep1),
        (pltpu.VMEM((BANKS, FB, FB), F32), pltpu.SemaphoreType.DMA((BANKS,))),
        [bias1, hidden_0],
        out_specs=[ANY()],
    )
    ring1 = lax.psum_scatter(local1, "dp", axis_index_groups=FIRST_RINGS)
    keep_p, send_p, encoded_parts, bias_p = with_bank_rows(
        projection_kernel,
        "projection",
        [shape(256, FB), shape(256, FB), shape(128, FB), shape(8, 128)],
        meta,
        counts,
        (hidden2, *banks),
        proj_weight,
        local1,
    )
    theirs_p = to_partner(send_p)
    turned = run(
        turn_hidden_kernel,
        "turn_hidden",
        [shape(FB, 8 * TOK, dtype=BF16)] * 2,
        meta,
        (hidden_0,),
        after=[keep_p],
    )
    grad_t0, grad_g0, res0, keep0, send0 = run(
        slopes_kernel,
        "slopes",
        [shape(TOK, FB)] * 4 + [shape(TOK + 8, FB)],
        meta,
        (counts, *received1, res1, slope_t, slope_g, slope_r),
        after=[turned[0]],
        specs=[SMEM()] + [VMEM()] * 8,
    )
    packed_g = run(
        pack_grads_kernel,
        "pack_grads",
        [shape(CHIP, FB)] * RING,
        meta,
        (counts, keep0, to_partner(send0), keep_p, theirs_p),
        specs=[SMEM()] + [VMEM()] * 4,
    )
    grads_0 = ring_pieces(packed_g, along_first)
    *parts0, bias0 = highway_backward(
        0, meta, grad_t0, grad_g0, transform_weight, gate_weight, [packed_g[0]], [encoded_parts]
    )
    received0 = bank_pieces(parts0)
    (ring1,) = gate(meta, [ring1], [bias0, grads_0[1], grads_0[3]])
    own1 = lax.psum_scatter(ring1, "dp", axis_index_groups=SECOND_RINGS, tiled=True)
    pieces0 = run(
        ring_grad_kernel,
        "ring_grad",
        [shape(152, FB)] * RING,
        meta,
        (*turned, *grads_0),
        [pltpu.VMEM((FB, FB), F32), pltpu.VMEM((72, FB), F32)],
        [ring1],
    )
    second0 = ring_pieces(pieces0, along_second)
    coef, encoded, own1 = run(
        bank_sum_kernel,
        "bank_sum",
        [shape(FB, TOK), shape(TOK, 128), shape(128, FB)],
        meta,
        (counts, *received0, res0, summed, proj_bias[None], own1),
        after=[pieces0[0]],
        specs=[SMEM()] + [VMEM()] * 7 + [ANY()],
        out_specs=[VMEM(), VMEM(), ANY()],
        aliases={9: 2},
    )
    gathered1 = lax.all_gather(own1, "dp")
    keep_s, send_s, table = conv_backward(
        meta,
        (coef, lifted, emb_high, emb_low),
        conv_weight,
        chars.T,
        (bias0, bias1, bias_p),
        [coef],
    )
    own0, factor, *crossing = run(
        collect_ring_kernel,
        "collect_ring",
        [shape(128, FB), shape(8, FB)] + [shape(64, 128)] * BANKS,
        meta,
        (*second0, table),
    )

    own_parts = ring_gather(own0, along_second)
    (small,) = run(
        collect_kernel,
        "collect",
        [shape(96, FB)],
        meta,
        (
            keep_s,
            to_partner(send_s),
            crossing[0],
            *[along_bank(crossing[k], k) for k in range(1, BANKS)],
            factor,
        ),
        after=[own_parts[1], own_parts[3]],
    )
    low, high = run(
        merge_kernel,
        "merge",
        [shape(288, FB), shape(368, FB)],
        meta,
        (*own_parts, *ring_gather(small, along_second)),
    )
    near = [along_first(low, 1), along_first(high, 1)]
    back = [along_first(low, 3), along_first(high, 3)]
    mine = [low, high]
    theirs = [to_partner(v) for v in mine]
    sources = tuple((j, half) for j in (0, 1, 3, 2) for half in ((0, 1), (2, 3)))
    outs = place_last(meta, gathered1, factor, [], [low])
    outs = list(place(sources[0:2], meta, mine[0:2], theirs[0:2], outs, []))
    mine += gate(meta, [*near, *back], [outs[2]])
    far = [along_first(mine[2], 1), along_first(mine[5], 3)]
    theirs += [to_partner(v) for v in mine[2:]]
    outs = place(sources[2:6], meta, mine[2:6], theirs[2:6], outs, [])
    far = gate(meta, far, [outs[2]])
    mine += far
    theirs += [to_partner(v) for v in far]
    spots = (1, 3, 5, 7)
    sum_wt, sum_wg, sum_pw, sum_kernel, sum_cbias, sum_bt, sum_bg, sum_pb, sum_table = place(
        sources[6:8],
        meta,
        mine[6:8],
        theirs[6:8],
        outs,
        [],
        ([mine[i] for i in spots], [theirs[i] for i in spots]),
    )
    return (
        encoded,
        sum_table.T,
        sum_kernel,
        sum_cbias[0],
        sum_wt,
        sum_bt,
        sum_wg,
        sum_bg,
        sum_pw,
        sum_pb[0],
    )


def solution(mesh):
    return jax.shard_map(
        on_device,
        mesh=mesh,
        in_specs=(
            P("dp", None),
            P("dp"),
            P(),
            P(None, "bank"),
            P("bank"),
            P(None, None, "bank"),
            P(None, "bank"),
            P(None, None, "bank"),
            P(None, "bank"),
            P(None, "bank"),
            P("bank"),
            P("dp", "bank"),
        ),
        out_specs=(
            P("dp", "bank"),
            P(),
            P(None, "bank"),
            P("bank"),
            P(None, None, "bank"),
            P(None, "bank"),
            P(None, None, "bank"),
            P(None, "bank"),
            P(None, "bank"),
            P("bank"),
        ),
        check_vma=False,
    )
```

```python
import functools

import jax
import jax.numpy as jnp
from jax import lax
from jax.experimental import pallas as pl
from jax.experimental.pallas import tpu as pltpu
from jax.sharding import PartitionSpec as P

F32 = jnp.float32
BF16 = jnp.bfloat16
LOG2E = 1.4426950408889634
MIB = 2**20

TOK = 128
CH = 50
CHP = 56
FB = 512
TAPS = 7
EMB = 16
ROWS = TAPS * EMB
BANKS = 4
RING = 4
STEP = 10

VMEM_LIMIT = 64 * MIB - 64 * 1024

VMEM = functools.partial(pl.BlockSpec, memory_space=pltpu.VMEM)
ANY = functools.partial(pl.BlockSpec, memory_space=pl.ANY)
SMEM = functools.partial(pl.BlockSpec, memory_space=pltpu.SMEM)


PARAMS = pltpu.CompilerParams(vmem_limit_bytes=VMEM_LIMIT)


def shape(*dims, dtype=F32):
    return jax.ShapeDtypeStruct(dims, dtype)


def run(kernel, name, outs, meta, inputs, scratch=(), after=(), specs=None, out_specs=None, aliases=None):
    inputs, after = list(inputs), list(after)
    count = 1 + len(inputs)

    def body(*refs):
        kernel(*refs[:count], *refs[count + len(after) :])

    return pl.pallas_call(
        body,
        out_shape=outs,
        in_specs=[SMEM()] + list(specs or [VMEM()] * len(inputs)) + [ANY()] * len(after),
        out_specs=list(out_specs or [VMEM()] * len(outs)),
        scratch_shapes=list(scratch),
        input_output_aliases=aliases or {},
        compiler_params=PARAMS,
        name=name,
    )(meta, *inputs, *after)


def gate_kernel(meta, *refs):
    pass


def gate(meta, values, after):
    values = list(values)
    return run(
        gate_kernel,
        "gate",
        [jax.ShapeDtypeStruct(v.shape, v.dtype) for v in values],
        meta,
        values,
        after=after,
        specs=[ANY()] * len(values),
        out_specs=[ANY()] * len(values),
        aliases={1 + i: i for i in range(len(values))},
    )


def along_bank(value, shift):
    return lax.ppermute(value, "bank", [(i, (i + shift) % BANKS) for i in range(BANKS)])


def place_of(z, y, core):
    return (z * RING + y) * 2 + core


def to_partner(value):
    return lax.ppermute(value, "dp", [(i, i ^ 1) for i in range(2 * RING * RING)])


def ring_perm(shift, z_core):
    perm = []
    for z in range(RING):
        for y in range(RING):
            for core in range(2):
                if core == z_core:
                    to = place_of((z + shift) % RING, y, core)
                else:
                    to = place_of(z, (y + shift) % RING, core)
                perm.append((place_of(z, y, core), to))
    return perm


FIRST_RINGS = [[place_of(z, y, 0) for z in range(RING)] for y in range(RING)] + [
    [place_of(z, y, 1) for y in range(RING)] for z in range(RING)
]
SECOND_RINGS = [[place_of(z, y, 0) for y in range(RING)] for z in range(RING)] + [
    [place_of(z, y, 1) for z in range(RING)] for y in range(RING)
]


def along_first(value, shift):
    return lax.ppermute(value, "dp", ring_perm(shift, 0))


def along_second(value, shift):
    return lax.ppermute(value, "dp", ring_perm(shift, 1))


def split(value):
    high = value.astype(BF16)
    low = (value - high.astype(F32)).astype(BF16)
    return high, low


def dot(left, right, dims=((1,), (0,))):
    return lax.dot_general(left, right, (dims, ((), ())), preferred_element_type=F32)


def dot3(left, right, dims=((1,), (0,))):
    lh, ll = split(left)
    rh, rl = split(right)
    return dot(lh, rh, dims) + dot(ll, rh, dims) + dot(lh, rl, dims)


def widths_of(column):
    width = jnp.ones_like(column)
    for power in range(6):
        width = width + (column >= 32 * 2**power).astype(jnp.int32)
    return width


def conv_forward_kernel(
    meta, chars, table, weight, bias, pooled, summed, lifted_out, emb_high, emb_low, wide, wide_table, lifted, sems
):
    start = meta[0] * FB
    column = start + lax.broadcasted_iota(jnp.int32, (ROWS, FB), 1)
    tap = lax.broadcasted_iota(jnp.int32, (ROWS, FB), 0) // EMB
    kernel = jnp.where(tap < widths_of(column), weight[...], 0.0) * LOG2E
    high = kernel.astype(BF16).astype(F32)
    shift = bias[...] * LOG2E
    shift_high = shift.astype(BF16).astype(F32)
    row = lax.broadcasted_iota(jnp.int32, (EMB, FB), 0)
    shifts = jnp.where(row == 0, shift_high, jnp.where(row == 1, shift - shift_high, 0.0))
    rows = [high, kernel - high, shifts, jnp.zeros((EMB, FB), F32)]
    wide[...] = jnp.concatenate(rows, axis=0).T.astype(BF16)
    wide_table[:, 0 : table.shape[1]] = table[...]
    parts = [wide_table[:, 128 * i : 128 * (i + 1)] for i in range(3)]
    for p in range(CH):
        ids = jnp.broadcast_to(chars[p : p + 1, :], (EMB, TOK))
        lane = ids & 127
        part = ids >> 7
        found = [
            jnp.take_along_axis(t, lane, axis=1, mode="promise_in_bounds") for t in parts
        ]
        value = jnp.where(part == 0, found[0], jnp.where(part == 1, found[1], found[2]))
        high, low = split(value)
        emb_high[p * EMB : (p + 1) * EMB, :] = high
        emb_low[p * EMB : (p + 1) * EMB, :] = low
    zeros = jnp.zeros(((CHP - CH) * EMB, TOK), BF16)
    emb_high[CH * EMB :, :] = zeros
    emb_low[CH * EMB :, :] = zeros
    one_row = lax.broadcasted_iota(jnp.int32, (EMB, 2 * TOK), 0)
    ones = jnp.where(one_row < 2, 1.0, 0.0).astype(BF16)
    width = widths_of(start + lax.broadcasted_iota(jnp.int32, (FB, TOK), 0))

    def window(ref, pair):
        base = pair * 2 * EMB
        return jnp.concatenate(
            [ref[base : base + ROWS, :], ref[base + EMB : base + EMB + ROWS, :]], axis=1
        )

    for pair in range(CH // 2):
        high = window(emb_high, pair)
        low = window(emb_low, pair)
        pre = dot(wide[:, : 2 * ROWS + EMB], jnp.concatenate([high, high, ones], axis=0))
        pre += dot(wide[:, :ROWS], low)
        both = jnp.exp2(pre)
        first, second = both[:, :TOK], both[:, TOK:]
        if 2 * pair + 1 > CH - TAPS:
            first = jnp.where(width <= CH - 2 * pair, first, 0.0)
            second = jnp.where(width <= CH - 2 * pair - 1, second, 0.0)
        lifted[2 * pair] = first
        lifted[2 * pair + 1] = second
        pltpu.make_async_copy(
            lifted.at[pl.ds(2 * pair, 2)], lifted_out.at[pl.ds(2 * pair, 2)], sems.at[pair]
        ).start()
        if pair:
            summed[...] += first + second
        else:
            summed[...] = first + second
    valid = (CH + 1 - width).astype(F32)
    total = summed[...] + valid
    summed[...] = total
    pooled[...] = jnp.log(total / valid).T
    for pair in range(CH // 2):
        pltpu.make_async_copy(
            lifted.at[pl.ds(2 * pair, 2)], lifted_out.at[pl.ds(2 * pair, 2)], sems.at[pair]
        ).wait()


def conv_forward(meta, chars_t, table_t, weight, bias, after):
    return run(
        conv_forward_kernel,
        "conv_forward",
        (
            shape(TOK, FB),
            shape(FB, TOK),
            shape(CH, FB, TOK),
            shape(CHP * EMB, TOK, dtype=BF16),
            shape(CHP * EMB, TOK, dtype=BF16),
        ),
        meta,
        (chars_t, table_t, weight, bias),
        (
            pltpu.VMEM((FB, 2 * ROWS + 2 * EMB), BF16),
            pltpu.VMEM((EMB, 384), F32),
            pltpu.VMEM((CH, FB, TOK), F32),
            pltpu.SemaphoreType.DMA((CH // 2,)),
        ),
        after,
        out_specs=[VMEM(), VMEM(), ANY(), VMEM(), VMEM()],
    )


def bank_sum_kernel(meta, count, r0, r1, r2, r3, residual, summed, proj_bias, passed, coef, encoded, same):
    total = r0[...] + r1[...] + r2[...] + r3[...]
    coef[...] = (total[0:TOK] + residual[...]).T / summed[...]
    value = jnp.concatenate([total[TOK:, q * 128 : (q + 1) * 128] for q in range(4)], axis=0)
    live = live_rows(count[0], 128)
    encoded[...] = jnp.where(live, value + proj_bias[...], 0.0)


def conv_backward_kernel(
    meta, coef, lifted, emb_high, emb_low, weight, chars, bias0, bias1, bias_p, keep, send, table,
    kernel, grads, windows, acc, grad_emb, buffer, sems,
):
    start = meta[0] * FB
    copies = [
        pltpu.make_async_copy(
            lifted.at[pl.ds(i * 2, 2)], buffer.at[pl.ds(i * 2, 2)], sems.at[i]
        )
        for i in range(CH // 2)
    ]
    for copy in copies:
        copy.start()
    column = start + lax.broadcasted_iota(jnp.int32, (ROWS, FB), 1)
    tap = lax.broadcasted_iota(jnp.int32, (ROWS, FB), 0) // EMB
    high, low = split(jnp.where(tap < widths_of(column), weight[...], 0.0))
    kernel[0:ROWS] = high
    kernel[ROWS:] = low
    grad_emb[...] = jnp.zeros_like(grad_emb)
    row = lax.broadcasted_iota(jnp.int32, (EMB, STEP * TOK), 0)
    ones = jnp.where(row < 1, 1.0, 0.0).astype(BF16)
    for slot in range(2):
        windows[slot, 2 * ROWS :, :] = ones

    for step in range(CH // STEP):
        slot = step % 2
        for j in range(STEP):
            p = step * STEP + j
            if p % 2 == 0:
                copies[p // 2].wait()
            high, low = split(coef[...] * buffer[p])
            lanes = slice(j * TOK, (j + 1) * TOK)
            grads[slot, 0:FB, lanes] = high
            grads[slot, FB:, lanes] = low
            windows[slot, 0:ROWS, lanes] = emb_high[p * EMB : p * EMB + ROWS, :]
            windows[slot, ROWS : 2 * ROWS, lanes] = emb_low[p * EMB : p * EMB + ROWS, :]
        part = dot(grads[slot], windows[slot], ((1,), (1,)))
        if step:
            acc[...] += part
        else:
            acc[...] = part
        from_high = dot(kernel[...], grads[slot, 0:FB, :])
        from_low = dot(kernel[0:ROWS, :], grads[slot, FB:, :])
        grad_windows = from_high[0:ROWS] + from_high[ROWS:] + from_low
        for j in range(STEP):
            base = (step * STEP + j) * EMB
            grad_emb[base : base + ROWS, :] += grad_windows[:, j * TOK : (j + 1) * TOK]

    total = acc[...]
    grad_kernel = total[0:FB, 0:ROWS] + total[0:FB, ROWS : 2 * ROWS] + total[FB:, 0:ROWS]
    grad_bias = total[0:FB, 2 * ROWS :] + total[FB:, 2 * ROWS :]
    full = jnp.concatenate([grad_kernel, grad_bias], axis=1).T
    column = start + lax.broadcasted_iota(jnp.int32, (ROWS + EMB, FB), 1)
    row = lax.broadcasted_iota(jnp.int32, (ROWS + EMB, FB), 0)
    full = jnp.where((row > ROWS) | (row // EMB >= widths_of(column)) & (row < ROWS), 0.0, full)
    more = jnp.concatenate(
        [
            bias0[0:2],
            bias1[0:2],
            jnp.concatenate([bias_p[0:1], jnp.zeros((1, FB - 128), F32)], axis=1),
            jnp.zeros((10, FB), F32),
        ],
        axis=0,
    )
    full = jnp.concatenate([full[: ROWS + 1], more], axis=0)
    first_core = meta[1] == 0
    keep[...] = jnp.where(first_core, full[:64], full[64:])
    send[...] = jnp.where(first_core, full[64:], full[:64])
    found = jnp.zeros((2 * EMB, 384), F32)
    vocab = lax.broadcasted_iota(jnp.int32, (TOK, 384), 1).astype(F32)
    ids = jnp.concatenate([chars[...].astype(F32), jnp.zeros((CHP - CH, TOK), F32)], axis=0).T
    for begin in range(0, CH, STEP):
        left, right = [], []
        for q in range(begin, begin + STEP):
            high, low = split(grad_emb[q * EMB : (q + 1) * EMB, :])
            left.append(jnp.concatenate([high, low], axis=0))
            right.append(jnp.where(ids[:, q : q + 1] == vocab, 1.0, 0.0).astype(BF16))
        found += dot(jnp.concatenate(left, axis=1), jnp.concatenate(right, axis=0))
    found = found[0:EMB] + found[EMB:]
    for i in range(3):
        table[i * EMB : (i + 1) * EMB] = found[:, i * 128 : (i + 1) * 128]


def conv_backward(meta, inputs, weight, chars, biases, after):
    return run(
        conv_backward_kernel,
        "conv_backward",
        [shape(64, FB), shape(64, FB), shape(48, 128)],
        meta,
        (*inputs, weight, chars, *biases),
        (
            pltpu.VMEM((2 * ROWS, FB), BF16),
            pltpu.VMEM((2, 2 * FB, STEP * TOK), BF16),
            pltpu.VMEM((2, 2 * ROWS + EMB, STEP * TOK), BF16),
            pltpu.VMEM((2 * FB, 2 * ROWS + EMB), F32),
            pltpu.VMEM((CHP * EMB, TOK), F32),
            pltpu.VMEM((CH, FB, TOK), F32),
            pltpu.SemaphoreType.DMA((CH // 2,)),
        ),
        after,
        [VMEM(), ANY()] + [VMEM()] * 7,
    )


def live_rows(count, columns):
    return lax.broadcasted_iota(jnp.int32, (TOK, columns), 0) < count


def early_rows_kernel(meta, received, out, grads):
    for j in range(1, BANKS):
        source = (meta[0] + BANKS - j) % BANKS
        out[j - 1] = received[source, TOK:]
        grads[j - 1] = received[source, 0:TOK]


def bank_rows(meta, mine, others):
    found = []
    first = meta[1] == 0
    for i in range(BANKS - 1):
        low = jnp.where(first, mine[i], others[i])
        high = jnp.where(first, others[i], mine[i])
        found.append(jnp.concatenate([low, high], axis=0))
    return found


def grad_hidden_kernel(meta, count, cot, grads, mine, others, proj, token, out):
    live = live_rows(count[0], 128)
    total = dot3(jnp.where(live, cot[...], 0.0), proj[...], ((1,), (1,)))
    for i, rows in enumerate(bank_rows(meta, mine, others)):
        total += dot3(jnp.where(live, grads[i], 0.0), rows, ((1,), (1,)))
    out[...] = total


def with_bank_rows(kernel, name, outs, meta, count, inputs, proj, after):
    return pl.pallas_call(
        kernel,
        out_shape=outs,
        grid_spec=pltpu.PrefetchScalarGridSpec(
            num_scalar_prefetch=2,
            grid=(1,),
            in_specs=[VMEM()] * len(inputs)
            + [pl.BlockSpec((FB, 128), lambda i, meta, count: (meta[0], 0)), ANY()],
            out_specs=[VMEM()] * len(outs),
        ),
        compiler_params=PARAMS,
        name=name,
    )(meta, count, *inputs, proj, after)


def projection_kernel(meta, count, hidden, cot, cots, mine, others, proj, token, keep, send, encoded, bias):
    live = live_rows(count[0], 128)
    grads = [jnp.where(live, value, 0.0) for value in (cot[...], cots[0], cots[1], cots[2])]
    rows = [proj[...]] + bank_rows(meta, mine, others)
    value = hidden[...]
    both = jnp.concatenate(split(value), axis=0)
    turned = jnp.concatenate(split(value.T), axis=0)
    first = meta[1] == 0
    for j in range(BANKS):
        high, low = split(rows[j])
        part = dot(both, high)
        part = part[0:TOK] + part[TOK:] + dot(both[0:TOK], low)
        for q in range(4):
            encoded[j * 32 : (j + 1) * 32, q * 128 : (q + 1) * 128] = part[q * 32 : (q + 1) * 32]
        high, low = split(grads[j])
        part = dot(turned, high)
        part = part[0:FB] + part[FB:] + dot(turned[0:FB], low)
        lanes = slice(j * 128, (j + 1) * 128)
        keep[:, lanes] = jnp.where(first, part[0:256], part[256:])
        send[:, lanes] = jnp.where(first, part[256:], part[0:256])
    bias[...] = jnp.broadcast_to(jnp.sum(grads[0], axis=0, keepdims=True), (8, 128))


def early_pack_kernel(meta, cot, p1, p2, p3, out):
    for j, ref in enumerate((p1, p2, p3)):
        to = (meta[0] + 1 + j) % BANKS
        out[to, 0:TOK] = cot[...]
        out[to, TOK:] = ref[...]


def early_pack(meta, cot, proj):
    def rows(j):
        return pl.BlockSpec((256, 128), lambda i, meta: ((meta[0] + j) % BANKS * 2 + meta[1], 0))

    return pl.pallas_call(
        early_pack_kernel,
        out_shape=shape(BANKS, TOK + 256, 128),
        grid_spec=pltpu.PrefetchScalarGridSpec(
            num_scalar_prefetch=1,
            grid=(1,),
            in_specs=[VMEM()] + [rows(j) for j in range(1, BANKS)],
            out_specs=VMEM(),
        ),
        compiler_params=PARAMS,
        name="early_pack",
    )(meta, cot, proj, proj, proj)


def sigmoid(value):
    return 1.0 / (1.0 + jnp.exp(-value))


def weight_copies(layer, shift, meta, weights, buffer, sems):
    found = []
    for i in range(BANKS):
        for m, ref in enumerate(weights):
            base = pl.multiple_of((meta[0] + shift + i) % BANKS * FB, FB)
            for half in range(2):
                rows = pl.ds(base + half * 256, 256)
                found.append(
                    pltpu.make_async_copy(
                        ref.at[layer, rows],
                        buffer.at[m, i, pl.ds(half * 256, 256)],
                        sems.at[m, i, half],
                    )
                )
    return found


WEIGHT_SCRATCH = (
    pltpu.VMEM((2, BANKS, FB, FB), F32),
    pltpu.SemaphoreType.DMA((2, BANKS, 2)),
)


def forward_kernel(layer, meta, x0, x1, x2, x3, weight_t, weight_g, bias_t, bias_g, *rest):
    last = layer == 1
    *rest, buffer, sems = rest
    if last:
        grad, hidden, out_t, out_g, out_r, keep, stack = rest
    else:
        hidden, out_t, out_g, out_r, stack = rest
    copies = weight_copies(layer, 0, meta, (weight_t, weight_g), buffer, sems)
    for copy in copies:
        copy.start()
    acc = [jnp.zeros((TOK, FB), F32), jnp.zeros((TOK, FB), F32)]
    for i, ref in enumerate((x0, x1, x2, x3)):
        value = ref[...]
        stack[i * TOK : (i + 1) * TOK] = value
        both = jnp.concatenate(split(value), axis=0)
        for m in range(2):
            for copy in copies[i * 4 + m * 2 : i * 4 + m * 2 + 2]:
                copy.wait()
            high, low = split(buffer[m, i])
            found = dot(both, high)
            acc[m] += found[0:TOK] + found[TOK:] + dot(both[0:TOK], low)
    pre_t = acc[0] + bias_t[layer : layer + 1]
    gate = sigmoid(acc[1] + bias_g[layer : layer + 1])
    sigma = sigmoid(pre_t)
    own = x0[...]
    silu = pre_t * sigma
    hidden[...] = gate * silu + (1.0 - gate) * own
    slope_t = gate * sigma * (1.0 + pre_t * (1.0 - sigma))
    slope_g = (silu - own) * gate * (1.0 - gate)
    if last:
        grad_t = grad[...] * slope_t
        grad_g = grad[...] * slope_g
        out_t[...] = grad_t
        out_g[...] = grad_g
        out_r[...] = grad[...] * (1.0 - gate)
        first = meta[1] == 0
        keep[...] = jnp.where(first, grad_t, grad_g)
        stack[BANKS * TOK :] = jnp.where(first, grad_g, grad_t)
    else:
        out_t[...] = slope_t
        out_g[...] = slope_g
        out_r[...] = 1.0 - gate


def highway_forward(layer, meta, blocks, weight_t, weight_g, bias_t, bias_g, after, grad=()):
    last = layer == 1
    outs = [shape(TOK, FB)] * (4 + last) + [shape((BANKS + last) * TOK, FB)]
    return run(
        functools.partial(forward_kernel, layer),
        "highway_forward",
        outs,
        meta,
        (*blocks, weight_t, weight_g, bias_t, bias_g, *grad),
        WEIGHT_SCRATCH,
        after,
        [VMEM()] * 4 + [ANY()] * 2 + [VMEM()] * (2 + last),
    )


def slopes_kernel(
    meta, count, r0, r1, r2, r3, residual, slope_t, slope_g, slope_r, out_t, out_g, out_r, keep, send
):
    grad = r0[...] + r1[...] + r2[...] + r3[...] + residual[...]
    grad_t = grad * slope_t[...]
    grad_g = grad * slope_g[...]
    first = meta[1] == 0
    out_t[...] = grad_t
    out_g[...] = grad_g
    out_r[...] = grad * slope_r[...]
    keep[...] = jnp.where(first, grad_t, grad_g)
    send[0:TOK] = jnp.where(first, grad_g, grad_t)
    send[TOK:] = jnp.full((8, FB), count[0].astype(F32))


def backward_kernel(layer, meta, grad_t, grad_g, *rest):
    *rest, bias, buffer, sems = rest
    encoded = rest.pop(0) if layer == 0 else None
    weight_t, weight_g, *outs = rest
    copies = weight_copies(layer, 1, meta, (weight_t, weight_g), buffer, sems)
    for copy in copies:
        copy.start()
    left = [jnp.concatenate(split(ref[...]), axis=0) for ref in (grad_t, grad_g)]
    sums = [jnp.sum(ref[...], axis=0, keepdims=True) for ref in (grad_t, grad_g)]
    row = lax.broadcasted_iota(jnp.int32, (8, FB), 0)
    bias[...] = jnp.where(row == 0, sums[0], jnp.where(row == 1, sums[1], 0.0))
    for i in range(BANKS):
        total = jnp.zeros((TOK, FB), F32)
        for m in range(2):
            for copy in copies[i * 4 + m * 2 : i * 4 + m * 2 + 2]:
                copy.wait()
            high, low = split(buffer[m, i])
            both = dot(left[m], high, ((1,), (1,)))
            total += both[0:TOK] + both[TOK:] + dot(left[m][0:TOK], low, ((1,), (1,)))
        outs[i][0:TOK] = total
        if layer == 0:
            j = BANKS - 1 - i
            outs[i][TOK:] = encoded[j * 32 : (j + 1) * 32]


def highway_backward(layer, meta, grad_t, grad_g, weight_t, weight_g, after, encoded=()):
    parts = [shape(TOK + 32 * len(encoded), FB)] * BANKS
    return run(
        functools.partial(backward_kernel, layer),
        "highway_backward",
        parts + [shape(8, FB)],
        meta,
        (grad_t, grad_g, *encoded, weight_t, weight_g),
        WEIGHT_SCRATCH,
        after,
        [VMEM()] * (2 + len(encoded)) + [ANY()] * 2,
    )


def pack_kernel(meta, mine, theirs, out, stage, sems_in, sems_out):
    copies, done = [], []
    for k in range(RING):
        spot = (k + BANKS - meta[0]) % BANKS
        rows = pl.ds(pl.multiple_of(spot * TOK, TOK), TOK)
        for c, ref in enumerate((mine, theirs)):
            copies.append(
                pltpu.make_async_copy(
                    ref.at[rows], stage.at[k, pl.ds(c * TOK, TOK)], sems_in.at[k, c]
                )
            )
            copies[-1].start()
    for k in range(RING):
        copies[2 * k].wait()
        copies[2 * k + 1].wait()
        done.append(pltpu.make_async_copy(stage.at[k], out.at[k], sems_out.at[k]))
        done[-1].start()
    for copy in done:
        copy.wait()


def pack(meta, mine, theirs, after):
    return run(
        pack_kernel,
        "pack",
        [shape(RING, 2 * TOK, FB)],
        meta,
        (mine, theirs),
        (
            pltpu.VMEM((RING, 2 * TOK, FB), F32),
            pltpu.SemaphoreType.DMA((RING, 2)),
            pltpu.SemaphoreType.DMA((RING,)),
        ),
        after,
        specs=[ANY()] * 2,
        out_specs=[ANY()],
    )


def local_grad_kernel(meta, mine, theirs, keep, out, stage, sems):
    high, low = split(jnp.concatenate([keep[...], theirs[BANKS * TOK :]], axis=0))
    copies = []
    for i in range(BANKS):
        rows = slice(i * TOK, (i + 1) * TOK)
        hidden = jnp.concatenate([mine[rows], theirs[rows]], axis=0).T
        left_high, left_low = split(hidden)
        stage[i] = dot(left_high, high) + dot(left_low, high) + dot(left_high, low)
        position = (meta[0] + i) % BANKS
        copies.append(pltpu.make_async_copy(stage.at[i], out.at[position], sems.at[i]))
        copies[-1].start()
    for copy in copies:
        copy.wait()


def turn_hidden_kernel(meta, hidden, high, low):
    for k in range(RING):
        block = hidden[(meta[2] + RING - k) % RING].T
        lanes = slice(k * 2 * TOK, (k + 1) * 2 * TOK)
        high[:, lanes], low[:, lanes] = split(block)


CHIP = 2 * TOK + 64 + 8


def pack_grads_kernel(meta, count, keep, theirs, keep_p, theirs_p, *outs):
    for k, out in enumerate(outs):
        out[0:TOK] = keep[...]
        out[TOK : 2 * TOK] = theirs[0:TOK]
        rows = pl.ds(pl.multiple_of((meta[2] + k) % RING * 64, 64), 64)
        out[2 * TOK : 2 * TOK + 64] = keep_p[rows, :] + theirs_p[rows, :]
        out[2 * TOK + 64 :] = theirs[TOK:] + count[0].astype(F32)


def ring_grad_kernel(meta, high, low, *refs):
    full, total = refs[-2:]
    outs = refs[-2 - RING : -2]
    ins = refs[:RING]
    right = [split(ref[0 : 2 * TOK]) for ref in ins]
    right_high = jnp.concatenate([r[0] for r in right], axis=0)
    right_low = jnp.concatenate([r[1] for r in right], axis=0)
    full[...] = dot(high[...], right_high) + dot(low[...], right_high) + dot(high[...], right_low)
    total[...] = sum(ref[2 * TOK :] for ref in ins)
    for k, out in enumerate(outs):
        spot = (meta[3] + k) % RING
        out[0:128] = full[pl.ds(pl.multiple_of(spot * 128, 128), 128), :]
        out[128:144] = total[pl.ds(pl.multiple_of(spot * 16, 16), 16), :]
        out[144:] = total[64:]


def collect_ring_kernel(meta, r0, r1, r2, r3, table, out, factor, *crossing):
    total = r0[...] + r1[...] + r2[...] + r3[...]
    scale = lax.rsqrt(total[144:145, :])
    out[...] = total[0:128] * scale
    for k, ref in enumerate(crossing):
        j = (BANKS - k) % BANKS
        ref[0:EMB] = total[128:144, j * 128 : (j + 1) * 128] * scale[:, 0:128]
        ref[EMB:] = table[...] * scale[:, 0:128]
    factor[...] = jnp.broadcast_to(scale, (8, FB))


def collect_kernel(meta, keep, theirs, x0, x1, x2, x3, factor, out):
    scale = factor[0:1, :]
    for j, ref in enumerate((x0, x1, x2, x3)):
        out[0:16, j * 128 : (j + 1) * 128] = ref[0:EMB]
    out[16:80] = (keep[...] + theirs[...]) * scale
    table = x0[EMB:] + x1[EMB:] + x2[EMB:] + x3[EMB:]
    blocks = [table[i * EMB : (i + 1) * EMB] for i in range(3)] + [jnp.zeros((EMB, 128), F32)]
    out[80:] = jnp.concatenate(blocks, axis=1)


def merge_kernel(meta, *refs):
    *parts, out = refs
    small = parts[RING:]
    for i in range(RING):
        out[i * 144 : i * 144 + 128] = parts[i][...]
        out[i * 144 + 128 : (i + 1) * 144] = small[i][0:16]
    out[576:] = sum(ref[16:] for ref in small)


def cut_kernel(meta, near, back, same_near, same_back, near_part, back_part, sems):
    many = near_part.shape[0]
    copies = [
        pltpu.make_async_copy(near.at[pl.ds(0, many)], near_part, sems.at[0]),
        pltpu.make_async_copy(back.at[pl.ds(many, back_part.shape[0])], back_part, sems.at[1]),
    ]
    for copy in copies:
        copy.start()
    for copy in copies:
        copy.wait()


def place_last_kernel(given, meta, gathered, factor, *refs):
    out_t, out_g, stage, loads, puts = refs[given:]
    copies = [
        pltpu.make_async_copy(
            gathered.at[pl.ds(i * 2, 2)], stage.at[pl.ds(i * 2, 2)], loads.at[i]
        )
        for i in range(RING * RING)
    ]
    for copy in copies:
        copy.start()
    scale = factor[0:1, :]
    done = []
    for i, copy in enumerate(copies):
        copy.wait()
        for core, out in enumerate((out_t, out_g)):
            stage[i * 2 + core] = stage[i * 2 + core] * scale
            row = i if core == 0 else i % RING * RING + i // RING
            done.append(
                pltpu.make_async_copy(
                    stage.at[i * 2 + core], out.at[1, pl.ds(row * 128, 128)], puts.at[i * 2 + core]
                )
            )
            done[-1].start()
    for copy in done:
        copy.wait()


def place_last(meta, gathered, factor, outs, after):
    return run(
        functools.partial(place_last_kernel, len(outs)),
        "place",
        [shape(2, 2048, FB)] * 2,
        meta,
        (gathered, factor, *outs),
        (
            pltpu.VMEM((32, 128, FB), F32),
            pltpu.SemaphoreType.DMA((16,)),
            pltpu.SemaphoreType.DMA((32,)),
        ),
        after,
        [ANY(), VMEM()] + [ANY()] * len(outs),
        [ANY()] * 2,
        {3 + i: i for i in range(len(outs))},
    )


ROWS0 = 144


def place_kernel(sources, given, ending, meta, *refs):
    count = len(sources)
    mine, theirs = refs[:count], refs[count : 2 * count]
    ends = refs[2 * count : 2 * count + 2 * RING * ending]
    refs = refs[2 * count + 2 * RING * ending + given :]
    outs, small, refs = refs[:3], refs[3 : 3 + 6 * ending], refs[3 + 6 * ending :]
    stages, loads, sems = refs[:count], refs[count], refs[count + 1]
    if ending:
        end_stage, end_sems = refs[count + 2 :]
        copies = [
            pltpu.make_async_copy(
                ref.at[pl.ds(ref.shape[0] - 80, 80)], end_stage.at[i], end_sems.at[i]
            )
            for i, ref in enumerate(ends)
        ]
        for copy in copies:
            copy.start()

    def load(i, core):
        ref = (mine, theirs)[core][i]
        many = len(sources[i][1]) * ROWS0
        return pltpu.make_async_copy(ref.at[pl.ds(0, many)], stages[i].at[core], loads.at[i, core])

    for i in range(count):
        for core in range(2):
            load(i, core).start()
    puts = []
    for i, (j, blocks) in enumerate(sources):
        for core in range(2):
            load(i, core).wait()
        for stream in range(2):
            holder = jnp.where(meta[1] == stream, 0, 1)
            major, minor = (meta[4], meta[5]) if stream == 0 else (meta[5], meta[4])
            first = (major + RING - j) % RING
            for spot, k in enumerate(blocks):
                second = (minor + RING - k) % RING
                base = pl.multiple_of((first * RING + second) * 128, 128)
                found = [
                    (
                        stages[i].at[holder, pl.ds(spot * ROWS0, 128)],
                        outs[stream].at[0, pl.ds(base, 128)],
                    )
                ]
                for q in range(BANKS):
                    bank = (meta[0] + BANKS - q) % BANKS
                    base = pl.multiple_of(bank * FB + stream * 256 + first * 64 + second * 16, 16)
                    found.append(
                        (
                            stages[i].at[holder, pl.ds(spot * ROWS0 + 128, 16), pl.ds(q * 128, 128)],
                            outs[2].at[pl.ds(base, 16)],
                        )
                    )
                for a, b in found:
                    puts.append(pltpu.make_async_copy(a, b, sems.at[len(puts)]))
                    puts[-1].start()
    if ending:
        for copy in copies:
            copy.wait()
        finish(meta, end_stage, small)
    for copy in puts:
        copy.wait()


def finish(meta, stage, outs):
    kernel, cbias, bt, bg, pb, table = outs
    own = sum(stage[i] for i in range(RING))
    other = sum(stage[i] for i in range(RING, 2 * RING))
    first = meta[1] == 0
    low = jnp.where(first, own, other)
    high = jnp.where(first, other, own)
    flat = jnp.concatenate([low[0:64], high[0:64]], axis=0)
    kernel[...] = flat[:ROWS]
    cbias[...] = flat[ROWS : ROWS + 1]
    row = ROWS + 1
    bt[...] = jnp.concatenate([flat[row : row + 1], flat[row + 2 : row + 3]], axis=0)
    bg[...] = jnp.concatenate([flat[row + 1 : row + 2], flat[row + 3 : row + 4]], axis=0)
    pb[...] = flat[row + 4 : row + 5, 0:128]
    table[...] = (own[64:] + other[64:])[:, 0:262]


def place(sources, meta, mine, theirs, outs, after, ends=None):
    total = sum(len(blocks) for _, blocks in sources) * 2 * 5
    ending = ends is not None
    inputs = [*mine, *theirs] + ([*ends[0], *ends[1]] if ending else [])
    start = 1 + len(inputs)
    shapes = [shape(2, 2048, FB)] * 2 + [shape(2048, 128)]
    if ending:
        shapes += [
            shape(ROWS, FB), shape(1, FB), shape(2, FB), shape(2, FB), shape(1, 128), shape(EMB, 262),
        ]
    return run(
        functools.partial(place_kernel, sources, len(outs), ending),
        "place",
        shapes,
        meta,
        [*inputs, *outs],
        [pltpu.VMEM((2, len(blocks) * ROWS0, FB), F32) for _, blocks in sources]
        + [
            pltpu.SemaphoreType.DMA((len(sources), 2)),
            pltpu.SemaphoreType.DMA((total,)),
        ]
        + (
            [pltpu.VMEM((2 * RING, 80, FB), F32), pltpu.SemaphoreType.DMA((2 * RING,))]
            if ending
            else []
        ),
        after,
        specs=[ANY()] * (len(inputs) + len(outs)),
        out_specs=[ANY()] * 3 + [VMEM()] * (6 * ending),
        aliases={start + i: i for i in range(len(outs))},
    )


def on_device(
    chars,
    counts,
    char_table,
    conv_weight,
    conv_bias,
    transform_weight,
    transform_bias,
    gate_weight,
    gate_bias,
    proj_weight,
    proj_bias,
    cotangent,
):
    here = lax.axis_index("dp")
    bank = lax.axis_index("bank")
    z, y, core = here // (2 * RING), here // 2 % RING, here % 2
    first = jnp.where(core == 0, z, y)
    second = jnp.where(core == 0, y, z)
    meta = jnp.stack([bank, core, first, second, z, y]).astype(jnp.int32)

    early = early_pack(meta, cotangent, proj_weight)
    early_received = lax.all_to_all(early, "bank", 0, 0, tiled=True)
    pooled, summed, lifted, emb_high, emb_low = conv_forward(
        meta, chars.T, char_table.T, conv_weight, conv_bias[None], [early]
    )

    def gather(block):
        others = {i: along_bank(block, -i) for i in (2, 1, 3)}
        return [block, others[1], others[2], others[3]]

    def bank_pieces(parts):
        return [parts[3]] + [along_bank(parts[i - 1], i) for i in (2, 1, 3)]

    def ring_gather(value, mover):
        moved = {k: mover(value, k) for k in (2, 1, 3)}
        return [value, moved[1], moved[2], moved[3]]

    def ring_pieces(pieces, mover):
        moved = {k: mover(pieces[k], k) for k in (2, 1, 3)}
        return [pieces[0], moved[1], moved[2], moved[3]]

    weights = (transform_weight, gate_weight, transform_bias, gate_bias)
    blocks0 = gather(pooled)
    rows, cots = run(
        early_rows_kernel,
        "early_rows",
        [shape(3, 256, 128), shape(3, TOK, 128)],
        meta,
        (early_received,),
        after=[pooled],
    )
    banks = (cotangent, cots, rows, to_partner(rows))
    hidden1, slope_t, slope_g, slope_r, stack0 = highway_forward(
        0, meta, blocks0, *weights, [rows]
    )
    blocks1 = gather(hidden1)
    (packed0,) = pack(meta, stack0, to_partner(stack0), [hidden1])
    (grad_last,) = with_bank_rows(
        grad_hidden_kernel, "grad_hidden", [shape(TOK, FB)], meta, counts, banks, proj_weight, packed0
    )
    hidden_0 = lax.all_to_all(packed0, "dp", 0, 0, axis_index_groups=FIRST_RINGS, tiled=True)
    hidden2, grad_t1, grad_g1, res1, keep1, stack1 = highway_forward(
        1, meta, blocks1, *weights, [], [grad_last]
    )

    *parts1, bias1 = highway_backward(
        1, meta, grad_t1, grad_g1, transform_weight, gate_weight, []
    )
    received1 = bank_pieces(parts1)
    (local1,) = run(
        local_grad_kernel,
        "local_grad",
        [shape(RING, FB, FB)],
        meta,
        (stack1, to_partner(stack1), keep1),
        (pltpu.VMEM((BANKS, FB, FB), F32), pltpu.SemaphoreType.DMA((BANKS,))),
        [bias1, hidden_0],
        out_specs=[ANY()],
    )
    ring1 = lax.psum_scatter(local1, "dp", axis_index_groups=FIRST_RINGS)
    keep_p, send_p, encoded_parts, bias_p = with_bank_rows(
        projection_kernel,
        "projection",
        [shape(256, FB), shape(256, FB), shape(128, FB), shape(8, 128)],
        meta,
        counts,
        (hidden2, *banks),
        proj_weight,
        local1,
    )
    theirs_p = to_partner(send_p)
    turned = run(
        turn_hidden_kernel,
        "turn_hidden",
        [shape(FB, 8 * TOK, dtype=BF16)] * 2,
        meta,
        (hidden_0,),
        after=[keep_p],
    )
    grad_t0, grad_g0, res0, keep0, send0 = run(
        slopes_kernel,
        "slopes",
        [shape(TOK, FB)] * 4 + [shape(TOK + 8, FB)],
        meta,
        (counts, *received1, res1, slope_t, slope_g, slope_r),
        after=[turned[0]],
        specs=[SMEM()] + [VMEM()] * 8,
    )
    packed_g = run(
        pack_grads_kernel,
        "pack_grads",
        [shape(CHIP, FB)] * RING,
        meta,
        (counts, keep0, to_partner(send0), keep_p, theirs_p),
        specs=[SMEM()] + [VMEM()] * 4,
    )
    grads_0 = ring_pieces(packed_g, along_first)
    *parts0, bias0 = highway_backward(
        0, meta, grad_t0, grad_g0, transform_weight, gate_weight, [packed_g[0]], [encoded_parts]
    )
    received0 = bank_pieces(parts0)
    (ring1,) = gate(meta, [ring1], [bias0, grads_0[1], grads_0[3]])
    own1 = lax.psum_scatter(ring1, "dp", axis_index_groups=SECOND_RINGS, tiled=True)
    pieces0 = run(
        ring_grad_kernel,
        "ring_grad",
        [shape(152, FB)] * RING,
        meta,
        (*turned, *grads_0),
        [pltpu.VMEM((FB, FB), F32), pltpu.VMEM((72, FB), F32)],
        [ring1],
    )
    second0 = ring_pieces(pieces0, along_second)
    coef, encoded, own1 = run(
        bank_sum_kernel,
        "bank_sum",
        [shape(FB, TOK), shape(TOK, 128), shape(128, FB)],
        meta,
        (counts, *received0, res0, summed, proj_bias[None], own1),
        after=[pieces0[0]],
        specs=[SMEM()] + [VMEM()] * 7 + [ANY()],
        out_specs=[VMEM(), VMEM(), ANY()],
        aliases={9: 2},
    )
    gathered1 = lax.all_gather(own1, "dp")
    keep_s, send_s, table = conv_backward(
        meta,
        (coef, lifted, emb_high, emb_low),
        conv_weight,
        chars.T,
        (bias0, bias1, bias_p),
        [coef],
    )
    own0, factor, *crossing = run(
        collect_ring_kernel,
        "collect_ring",
        [shape(128, FB), shape(8, FB)] + [shape(64, 128)] * BANKS,
        meta,
        (*second0, table),
    )

    own_parts = ring_gather(own0, along_second)
    (small,) = run(
        collect_kernel,
        "collect",
        [shape(96, FB)],
        meta,
        (
            keep_s,
            to_partner(send_s),
            crossing[0],
            *[along_bank(crossing[k], k) for k in range(1, BANKS)],
            factor,
        ),
        after=[own_parts[1], own_parts[3]],
    )
    (merged,) = run(
        merge_kernel,
        "merge",
        [shape(656, FB)],
        meta,
        (*own_parts, *ring_gather(small, along_second)),
    )
    near, back = along_first(merged, 1), along_first(merged, 3)
    mine = [merged]
    theirs = [to_partner(merged)]
    everything = (0, 1, 2, 3)
    sources = ((0, everything), (1, everything), (3, everything), (2, (0, 1)), (2, (2, 3)))
    outs = place_last(meta, gathered1, factor, [], [merged])
    outs = list(place(sources[0:1], meta, mine, theirs, outs, []))
    near, back, near_part, back_part = run(
        cut_kernel,
        "cut",
        [shape(656, FB), shape(656, FB), shape(288, FB), shape(368, FB)],
        meta,
        (near, back),
        [pltpu.SemaphoreType.DMA((2,))],
        [outs[2]],
        [ANY()] * 2,
        [ANY(), ANY(), VMEM(), VMEM()],
        {1: 0, 2: 1},
    )
    far = [along_first(near_part, 1), along_first(back_part, 3)]
    mine += [near, back]
    theirs += [to_partner(near), to_partner(back)]
    outs = place(sources[1:3], meta, mine[1:3], theirs[1:3], outs, [])
    far = gate(meta, far, [outs[2]])
    mine += far
    theirs += [to_partner(v) for v in far]
    spots = (0, 1, 2, 4)
    sum_wt, sum_wg, sum_pw, sum_kernel, sum_cbias, sum_bt, sum_bg, sum_pb, sum_table = place(
        sources[3:5],
        meta,
        mine[3:5],
        theirs[3:5],
        outs,
        [],
        ([mine[i] for i in spots], [theirs[i] for i in spots]),
    )
    return (
        encoded,
        sum_table.T,
        sum_kernel,
        sum_cbias[0],
        sum_wt,
        sum_bt,
        sum_wg,
        sum_bg,
        sum_pw,
        sum_pb[0],
    )


def solution(mesh):
    return jax.shard_map(
        on_device,
        mesh=mesh,
        in_specs=(
            P("dp", None),
            P("dp"),
            P(),
            P(None, "bank"),
            P("bank"),
            P(None, None, "bank"),
            P(None, "bank"),
            P(None, None, "bank"),
            P(None, "bank"),
            P(None, "bank"),
            P("bank"),
            P("dp", "bank"),
        ),
        out_specs=(
            P("dp", "bank"),
            P(),
            P(None, "bank"),
            P("bank"),
            P(None, None, "bank"),
            P(None, "bank"),
            P(None, None, "bank"),
            P(None, "bank"),
            P(None, "bank"),
            P("bank"),
        ),
        check_vma=False,
    )
```
